256 devices in a mesh: wide: 64 (over x, z, core), narrow: 4 (over y).
Axes of the slice: x: 4, y: 4, z: 8, core: 2. Of those that a mesh axis runs over, the one named last changes fastest.
Arguments:
- features: bfloat16 [262144, 256], P(('wide', 'narrow')), may hold values from -6 to 6
- cotangent: bfloat16 [262144, 256], P(('wide', 'narrow')), may hold values from -0.059814453 to 0.059814453
- self_weight: bfloat16 [256, 256], replicated, may hold values from -0.375 to 0.375
- bases: bfloat16 [32, 256, 256], replicated, may hold values from -0.375 to 0.375
- basis_coef: bfloat16 [128, 32], P('wide'), may hold values from -1 to 1
- block_values: bfloat16 [128, 256, 128, 128], P('wide', 'narrow'), may hold values from -0.125 to 0.125
- block_slots: int32 [128, 256, 2], P('wide', 'narrow'), may hold values from 0 to 63
- fetch_ids: int32 [16384], P(('wide', 'narrow')), may hold values from 0 to 7
Outputs:
- output: bfloat16 [262144, 256], P(('wide', 'narrow'))
- basis_grad: float32 [8192, 256], P(('wide', 'narrow'))
- coef_grad: float32 [128, 32], P('wide')
The draws below stay inside these ranges and needn't reach their ends.
All inputs are finite; a program needn't handle non-finite values.
Results may differ from the reference program's by a relative error of at most 0.0056.
Values may be sent and summed in bfloat16 or wider, within the bound.
A program may use at most 128 MiB of HBM per device.

```python
import jax
import jax.numpy as jnp
from jax import lax

D = 256
NB = 32
BLOCK = 128
EB_DEV = 8
CAP = 1
REL_DEV = 2
BLK_REL = 64
FETCH = 64
ENTITIES = 262144
RELS = 128
N_WIDE = 64
N_NARROW = 4


def touch_ends(array, key, least, top_value):
    longest = array.shape.index(max(array.shape))
    spots = []
    for shift in (0, 1):
        where = [jax.random.randint(jax.random.fold_in(key, axis), (), 0, length) for axis, length in enumerate(array.shape)]
        where[longest] = (where[longest] + shift) % array.shape[longest]
        spots.append(tuple(where))
    return array.at[spots[0]].set(least).at[spots[1]].set(top_value)


def block_scale(own_key, dims, cuts, least, top_value):
    def one(dim, shards_of):
        heights = jax.random.uniform(jax.random.fold_in(jax.random.fold_in(own_key, 6), dim), (shards_of,), jnp.float32, least / len(cuts), top_value / len(cuts))
        return jnp.repeat(jnp.exp(heights), dims[dim] // shards_of).reshape((-1,) + (1,) * (len(dims) - dim - 1))

    factor_of = one(*cuts[0])
    for cut in cuts[1:]:
        factor_of = factor_of * one(*cut)
    return factor_of


def scatter_about(own_key, dims, width, reach, split=(), held_as=jnp.bfloat16):
    level = block_scale(own_key, dims, split, -0.22, 0.18) if split else 1.0
    values = jax.random.normal(own_key, dims, jnp.float32) * width * level
    return jnp.minimum(jnp.maximum(values, -reach), reach).astype(held_as)


def setup_inputs(seed: int = 0) -> dict:
    arg_keys = jax.random.split(jax.random.key(seed), 9)
    return {
        "features": scatter_about(arg_keys[0], (ENTITIES, D), 1.0, 6.0, ((0, 256),)),
        "cotangent": scatter_about(arg_keys[1], (ENTITIES, D), 0.01, 0.059814453, ((0, 256),)),
        "self_weight": scatter_about(arg_keys[2], (D, D), D ** -0.5, 0.375),
        "bases": scatter_about(arg_keys[3], (NB, D, D), D ** -0.5, 0.375),
        "basis_coef": scatter_about(arg_keys[4], (RELS, NB), NB ** -0.5, 1.0, ((0, 64),)),
        "block_values": scatter_about(arg_keys[5], (RELS, N_NARROW * BLK_REL, BLOCK, BLOCK), (BLOCK * 16) ** -0.5, 0.125, ((0, 64), (1, 4))),
        "block_slots": touch_ends(jax.random.randint(arg_keys[6], (RELS, N_NARROW * BLK_REL, 2), 0, FETCH), jax.random.fold_in(arg_keys[6], 1), 0, FETCH - 1).astype(jnp.int32),
        "fetch_ids": touch_ends(jax.random.randint(arg_keys[7], (N_WIDE * N_NARROW * FETCH,), 0, EB_DEV), jax.random.fold_in(arg_keys[7], 1), 0, EB_DEV - 1).astype(jnp.int32),
    }


def reference(features, cotangent, self_weight, bases, basis_coef, block_values, block_slots, fetch_ids):
    group_count = N_WIDE * N_NARROW
    rel_weights = jnp.einsum("rb,bde->rde", basis_coef.astype(jnp.float32), bases.astype(jnp.float32)).astype(jnp.bfloat16)
    grouped_weights = rel_weights.reshape(N_WIDE, REL_DEV, D, D)
    feat_blocks = features.reshape(group_count * EB_DEV, BLOCK, D)
    cot_blocks = cotangent.reshape(group_count * EB_DEV, BLOCK, D)
    fetch_table = fetch_ids.reshape(group_count, FETCH)
    value_table = block_values.reshape(N_WIDE, REL_DEV, N_NARROW, BLK_REL, BLOCK, BLOCK)
    slot_table = block_slots.reshape(N_WIDE, REL_DEV, N_NARROW, BLK_REL, 2)
    slot_pos = jnp.arange(FETCH, dtype=jnp.int32)

    def one_group(carry, group):
        out_sum, rel_grads = carry
        wide_pos = group // N_NARROW
        narrow_pos = group % N_NARROW
        owners = (slot_pos // CAP) * N_NARROW + narrow_pos
        entity = (owners * EB_DEV + fetch_table[group]).astype(jnp.int32)
        fetched_feat = jnp.take(feat_blocks, entity, axis=0)
        fetched_cot = jnp.take(cot_blocks, entity, axis=0)
        group_vals = jnp.take(value_table[wide_pos], narrow_pos, axis=1)
        group_slots = jnp.take(slot_table[wide_pos], narrow_pos, axis=1)
        weights = grouped_weights[wide_pos]
        row_slot = group_slots[:, :, 0]
        col_slot = group_slots[:, :, 1]
        col_feat = jnp.take(fetched_feat, col_slot, axis=0)
        gathered = jnp.einsum("rkij,rkjd->rkid", group_vals.astype(jnp.float32), col_feat.astype(jnp.float32)).astype(jnp.bfloat16)
        slot_pick = (row_slot[:, :, None] == slot_pos[None, None, :]).astype(jnp.float32)
        slot_gathered = jnp.einsum("rks,rkid->rsid", slot_pick, gathered.astype(jnp.float32)).astype(jnp.bfloat16)
        slot_gathered = lax.optimization_barrier(slot_gathered)
        slot_sums = jnp.einsum("rsid,rde->sie", slot_gathered.astype(jnp.float32), weights.astype(jnp.float32)).astype(jnp.bfloat16)
        out_sum = out_sum.at[entity].add(slot_sums.astype(jnp.float32))
        row_cot = jnp.take(fetched_cot, row_slot, axis=0)
        grads = jnp.einsum("rkid,rkie->rde", gathered.astype(jnp.float32), row_cot.astype(jnp.float32))
        rel_grads = rel_grads.at[wide_pos].add(grads)
        return (out_sum, rel_grads), None

    start = (jnp.zeros((group_count * EB_DEV, BLOCK, D), jnp.float32), jnp.zeros((N_WIDE, REL_DEV, D, D), jnp.float32))
    (out_sum, rel_grads), unused = lax.scan(one_group, start, jnp.arange(group_count, dtype=jnp.int32))
    output = (jnp.dot(features, self_weight, preferred_element_type=jnp.float32) + out_sum.reshape(-1, D)).astype(jnp.bfloat16)
    rel_grads = rel_grads.reshape(RELS, D, D)
    basis_grad = jnp.einsum("rb,rde->bde", basis_coef.astype(jnp.float32), rel_grads, precision=lax.Precision.HIGHEST).reshape(NB * D, D)
    coef_grad = jnp.einsum("rde,bde->rb", rel_grads, bases.astype(jnp.float32), precision=lax.Precision.HIGHEST)
    return output, basis_grad, coef_grad
```

```python
import functools

import jax
import jax.numpy as jnp
from jax import lax
from jax.experimental import pallas as pl
from jax.experimental.pallas import tpu as pltpu
from jax.sharding import PartitionSpec as P

MESH = pl.DeviceIdType.MESH
F32 = jnp.float32
BF16 = jnp.bfloat16
CORES = 2


def layer_kernel(
    nx,
    nz,
    nn,
    meta,
    coef,
    ids_in,
    coef_in,
    feat,
    cot,
    selfw,
    bases_flat,
    bases_split,
    values_hbm,
    out,
    out_basis,
    out_coef,
    ids_v,
    coef_v,
    ids,
    coefs,
    zfeat,
    zcot,
    picked,
    stage,
    ffeat,
    fcot,
    values,
    running,
    slot_g,
    weights,
    self_term,
    rx,
    rb,
    relay,
    grad_acc,
    grad_parts,
    grad_in,
    grad_sum,
    bases_q,
    coef_part,
    coef_recv,
    row_in,
    basis_part,
    basis_in,
    basis_sum,
    basis_rows,
    local_sem,
    id_send,
    id_recv,
    coef_send,
    coef_recv_sem,
    z_send,
    z_recv,
    x_send,
    x_recv,
    ret_send,
    ret_recv,
    relay_recv,
    fwd_send,
    rs_send,
    rs_recv,
    y_send,
    y_recv,
    cp_send,
    cp_recv,
    row_send,
    row_recv,
    zb_send,
    zb_recv,
    xb_send,
    xb_recv,
):
    w = lax.axis_index("wide")
    n = lax.axis_index("narrow")
    x, z, c = w // (CORES * nz), (w // CORES) % nz, w % CORES
    peers = nx * CORES
    owned, block, width = feat.shape
    slots = ffeat.shape[0]
    rels = slot_g.shape[0]
    blocks = values.shape[1]
    nb = basis_part.shape[0] * basis_part.shape[1]
    group = grad_sum.shape[3]
    half = nz // 2
    opposite = 2 * CORES if nx == 4 else peers
    cut = owned // 2

    def slot(xs, zs, cs):
        return (xs * nz + zs) * CORES + cs

    def peer(p):
        return (x + p // CORES) % nx, (c + p % CORES) % CORES

    def row_dev(p):
        xp, cp = peer(p)
        return (slot(xp, z, cp), n)

    def back(p):
        return ((nx - p // CORES) % nx) * CORES + p % CORES

    def z_dev(dz):
        return (slot(x, (z + dz + nz) % nz, c), n)

    def y_dev(dn):
        return (w, (n + dn) % nn)

    def remote(src, dst, ssem, rsem, dev):
        return pltpu.make_async_remote_copy(
            src_ref=src, dst_ref=dst, send_sem=ssem, recv_sem=rsem, device_id=dev, device_id_type=MESH
        )

    def each(lo, hi, body):
        def step(i, carry):
            body(i)
            return carry

        lax.fori_loop(lo, hi, step, 0)

    slot_sums = zfeat

    load_bases = pltpu.make_async_copy(bases_flat, slot_g.at[1], local_sem.at[0])
    load_values = pltpu.make_async_copy(values_hbm, values, local_sem.at[1])
    load_bases_q = pltpu.make_async_copy(bases_split.at[:, :, n], bases_q, local_sem.at[2])
    load_bases.start()
    load_values.start()
    load_bases_q.start()

    barrier = pltpu.get_barrier_semaphore()
    for p in range(1, peers):
        pl.semaphore_signal(barrier, inc=1, device_id=row_dev(p), device_id_type=MESH)
    for dz in range(1, nz):
        pl.semaphore_signal(barrier, inc=1, device_id=z_dev(dz), device_id_type=MESH)
    for dn in range(1, nn):
        pl.semaphore_signal(barrier, inc=1, device_id=y_dev(dn), device_id_type=MESH)
    pl.semaphore_wait(barrier, peers + nz + nn - 3)

    def z_copy(which, own, buf, to, way):
        frm = to - 1 if way > 0 else (to + 1) % nz
        src = own if frm == 0 else buf.at[frm]
        dst = buf.at[to]
        sem = to
        if to == half:
            part = pl.ds(0, cut) if way > 0 else pl.ds(cut, cut)
            src, dst = src.at[part], dst.at[part]
            sem = half if way > 0 else 0
        return remote(src, dst, z_send.at[which, sem], z_recv.at[which, sem], z_dev(way))

    zf = functools.partial(z_copy, 0, feat, zfeat)
    zc = functools.partial(z_copy, 1, cot, zcot)

    def z_first(zcp):
        zcp(1, 1).start()
        zcp(nz - 1, -1).start()

    def z_step(zcp, d):
        if d < half:
            zcp(d, 1).wait_recv()
            zcp(d + 1, 1).start()
            zcp(nz - d, -1).wait_recv()
            zcp(nz - d - 1, -1).start()
        else:
            zcp(half, 1).wait_recv()
            zcp(half, -1).wait_recv()

    def z_done(zcp):
        for d in range(1, half + 1):
            zcp(d, 1).wait_send()
            zcp(nz - d, -1).wait_send()

    def x_copy(which, dst, j, p):
        at = nz if which == 1 and j == 0 else j
        s = slot(x, (z - j + nz) % nz, c)
        return remote(
            stage.at[at, p], dst.at[s], x_send.at[which, j, p], x_recv.at[which, s], row_dev(p)
        )

    def relay_copy(which, j, k):
        p = opposite + k
        if which < 2:
            src, sem = stage.at[nz if which == 1 and j == 0 else j, p], x_send.at[which, j, p]
        else:
            xp, cp = peer(p)
            s = slot(xp, (z - j + nz) % nz, cp)
            src, sem = slot_sums.at[s // owned, s % owned], ret_send.at[j, p]
        by = row_dev(CORES if k == 0 else (nx - 1) * CORES)
        return remote(src, relay.at[which, j, k], sem, relay_recv.at[which, j, k], by)

    def forward_copy(which, j, k):
        to = row_dev(CORES if k == 0 else (nx - 1) * CORES + 1)
        if which < 2:
            s = slot((x + (nx - 1 if k == 0 else 1)) % nx, (z - j + nz) % nz, c)
            dst, sem = (ffeat, fcot)[which].at[s], x_recv.at[which, s]
        else:
            dst, sem = rx.at[j, opposite + k], ret_recv.at[j, opposite + k]
        return remote(relay.at[which, j, k], dst, fwd_send.at[which, j, k], sem, to)

    def forward(which, *chunks):
        if opposite < peers:
            for j in chunks:
                for k in range(CORES):
                    relay_copy(which, j, k).wait_recv()
                    forward_copy(which, j, k).start()

    def x_step(which, own, buf, dst, j):
        src = own
        if j > 0:
            picked[...] = buf[j]
            src = picked
        at = nz if which == 1 and j == 0 else j
        s = slot(x, (z - j + nz) % nz, c)
        if which == 1 and j > 0:
            each(1, peers, lambda p: x_copy(0, ffeat, j, p).wait_send())

        def send(p):
            stage[at, p] = src[ids[p, 0, s]]
            x_copy(which, dst, j, p).start()

        each(1, opposite, send)
        each(opposite + CORES, peers, send)
        if opposite < peers:
            for k in range(CORES):
                stage[at, opposite + k] = src[ids[opposite + k, 0, s]]
                relay_copy(which, j, k).start()
        dst[s] = src[ids[0, 0, s]]

    xf = functools.partial(x_step, 0, feat, zfeat, ffeat)
    xc = functools.partial(x_step, 1, cot, zcot, fcot)

    def x_arrived(which, dst):
        def arrived(q):
            p = q // nz + 1
            xp, cp = peer(p)
            s = slot(xp, q % nz, cp)
            remote(
                stage.at[0, 0], dst.at[s], x_send.at[which, 0, 0], x_recv.at[which, s], row_dev(p)
            ).wait_recv()

        each(0, (peers - 1) * nz, arrived)

    z_first(zf)
    ids_v[0] = ids_in[...]
    coef_v[0] = coef_in[...]

    def small(p):
        return (
            remote(ids_in, ids_v.at[back(p)], id_send.at[p], id_recv.at[back(p)], row_dev(p)),
            remote(coef_in, coef_v.at[back(p)], coef_send.at[p], coef_recv_sem.at[back(p)], row_dev(p)),
        )

    for p in range(1, peers):
        for copy in small(p):
            copy.start()

    load_bases.wait()
    tile = 16
    per = block // tile
    parts = width // block

    def weigh(t):
        hb = t // per
        row = pl.multiple_of((t % per) * tile, tile)
        acc = [jnp.zeros((tile, width), F32) for _ in range(rels)]
        for b in range(nb):
            v = slot_g[1, b * parts + hb, pl.ds(row, tile), :].astype(F32)
            for r in range(rels):
                acc[r] = acc[r] + coef[r * nb + b] * v
        for r in range(rels):
            weights[r, pl.ds(pl.multiple_of(hb * block + row, tile), tile), :] = acc[r].astype(BF16)

    each(0, parts * per, weigh)

    for p in range(1, peers):
        for copy in small(p):
            copy.wait_recv()
    ids_down = pltpu.make_async_copy(ids_v, ids, local_sem.at[3])
    coef_down = pltpu.make_async_copy(coef_v, coefs, local_sem.at[4])
    ids_down.start()
    coef_down.start()
    ids_down.wait()
    coef_down.wait()

    xf(0)
    xc(0)

    def own_term(o):
        self_term[o] = jnp.dot(feat[o], selfw[...], preferred_element_type=F32)

    each(0, owned, own_term)

    for d in range(1, half):
        z_step(zf, d)
        if d == half - 1:
            z_first(zc)
        xf(d)
        xf(nz - d)
        if d == 1:
            forward(0, 0)
            forward(1, 0)
        else:
            forward(0, d - 1, nz - d + 1)
    z_step(zf, half)
    xf(half)
    forward(0, half - 1, nz - half + 1)
    forward(0, half)

    load_values.wait()
    x_arrived(0, ffeat)

    burst = 4

    def messages(r):
        def some(q):
            found = []
            for u in range(burst):
                j = q * burst + u
                found.append(
                    jnp.dot(values[r, j], ffeat[meta[r, j]], preferred_element_type=F32).astype(BF16)
                )
            for u in range(burst):
                j = q * burst + u
                before = meta[rels + r, j]
                earlier = running[jnp.maximum(before, 0)]
                running[j] = jnp.where(before >= 0, earlier, 0.0) + found[u].astype(F32)

        each(0, blocks // burst, some)

        def pick(s):
            at = meta[2 * rels + r, s]
            slot_g[r, s] = jnp.where(at >= 0, running[jnp.maximum(at, 0)], 0.0).astype(BF16)

        each(0, slots, pick)

    messages(0)
    z_step(zc, 1)
    xc(1)
    xc(nz - 1)
    messages(1)
    if half > 2:
        z_step(zc, 2)
        xc(2)
        xc(nz - 2)
    forward(1, 1, nz - 1)

    z_done(zf)

    def sum_slots(m):
        rows = (owned * block, width)
        at = pl.ds(m * owned, owned)
        total = jnp.dot(slot_g[0, at].reshape(rows), weights[0], preferred_element_type=F32)
        for r in range(1, rels):
            total += jnp.dot(slot_g[r, at].reshape(rows), weights[r], preferred_element_type=F32)
        slot_sums[m] = total.astype(BF16).reshape(owned, block, width)

    each(0, nz, sum_slots)

    def ret_copy(j, p):
        xp, cp = peer(p)
        s = slot(xp, (z - j + nz) % nz, cp)
        return remote(
            slot_sums.at[s // owned, s % owned],
            rx.at[j, back(p)],
            ret_send.at[j, p],
            ret_recv.at[j, back(p)],
            row_dev(p),
        )

    def ret_go(*chunks):
        for j in chunks:
            each(1, opposite, lambda p: ret_copy(j, p).start())
            each(opposite + CORES, peers, lambda p: ret_copy(j, p).start())
            if opposite < peers:
                for k in range(CORES):
                    relay_copy(2, j, k).start()

    ret_go(half)
    ret_go(half - 1, half + 1)
    for d in range(3, half):
        z_step(zc, d)
        xc(d)
        xc(nz - d)
        forward(1, d - 1, nz - d + 1)
    if half > 2:
        ret_go(half - 2, half + 2)
    z_step(zc, half)
    xc(half)
    if half > 2:
        forward(1, half - 1, half + 1)
    forward(2, half)
    for d in range(half - 3, 0, -1):
        ret_go(d, nz - d)
    ret_go(0)
    forward(1, half)

    def rs_copy(j, way):
        to = j - 1 if way < 0 else (j + 1) % nz
        at = half if way > 0 and to == 0 else to
        src, dst = ffeat.at[pl.ds(j * owned, owned)], rb.at[at]
        if j == half:
            first = 0 if way < 0 else cut
            src, dst = ffeat.at[pl.ds(j * owned + first, cut)], rb.at[at, pl.ds(first, cut)]
        return remote(src, dst, rs_send.at[at], rs_recv.at[at], z_dev(way))

    def collect(j, o):
        s = slot(x, (z - j + nz) % nz, c)
        total = None
        for p in range(peers):
            weight = jnp.where(ids[p, 0, s] == o, 1.0, 0.0).astype(F32)
            term = (slot_sums[s // owned, s % owned] if p == 0 else rx[j, p]).astype(F32) * weight
            total = term if total is None else total + term
        return total

    def rx_arrived(j):
        each(
            1,
            peers,
            lambda p: remote(
                stage.at[0, 0], rx.at[j, p], ret_send.at[j, 0], ret_recv.at[j, p], row_dev(p)
            ).wait_recv(),
        )

    def reduce_step(j):
        rx_arrived(j)
        lo, hi = 0, 0
        if 0 < j < half:
            rs_copy(j + 1, -1).wait_recv()
            lo, hi = 0, (cut if j + 1 == half else owned)
        elif j > half:
            rs_copy(j - 1, 1).wait_recv()
            lo, hi = (cut if j - 1 == half else 0), owned

        def plain(o):
            ffeat[j * owned + o] = collect(j, o).astype(BF16)

        def more(o):
            ffeat[j * owned + o] = (collect(j, o) + rb[j, o].astype(F32)).astype(BF16)

        if lo > 0:
            each(0, lo, plain)
        if hi > lo:
            each(lo, hi, more)
        if hi < owned:
            each(hi, owned, plain)
        if j <= half:
            rs_copy(j, -1).start()
        if j >= half:
            rs_copy(j, 1).start()

    def reduce_pair(d):
        forward(2, d, nz - d)
        reduce_step(d)
        reduce_step(nz - d)

    reduce_step(half)
    reduce_pair(half - 1)

    x_arrived(1, fcot)

    def relation_grad(r):
        grad_acc[...] = jnp.zeros_like(grad_acc)

        def add(m):
            at = pl.ds(m * owned, owned)
            rows = (owned * block, width)
            grad_acc[...] += lax.dot_general(
                slot_g[r, at].reshape(rows),
                fcot[at].reshape(rows),
                (((0,), (0,)), ((), ())),
                preferred_element_type=F32,
            )

        each(0, nz, add)
        rows = grad_parts.shape[3]
        for h in range(CORES):
            for m in range(nn):
                grad_parts[m, r, h] = grad_acc[pl.ds((h * nn + m) * rows, rows), :]

    relation_grad(0)
    if half > 2:
        reduce_pair(half - 2)
    for r in range(1, rels):
        relation_grad(r)

    def y_copy(dn):
        return remote(
            grad_parts.at[(n + dn) % nn],
            grad_in.at[nn - dn],
            y_send.at[dn],
            y_recv.at[nn - dn],
            y_dev(dn),
        )

    for dn in range(1, nn):
        y_copy(dn).start()

    for d in range(half - 3, 0, -1):
        reduce_pair(d)
    forward(2, 0)

    for dn in range(1, nn):
        y_copy(dn).wait_recv()
    rows = grad_parts.shape[3]
    for r in range(rels):
        for h in range(CORES):
            total = grad_parts[n, r, h]
            for dn in range(1, nn):
                total = total + grad_in[dn, r, h]
            grad_sum[r, h] = total.reshape(nx, group, width)

    def row_copy(p):
        xp, cp = peer(p)
        return remote(
            grad_sum.at[:, cp, xp], row_in.at[back(p)], row_send.at[p], row_recv.at[back(p)], row_dev(p)
        )

    for p in range(1, peers):
        row_copy(p).start()
    row_in[0] = grad_sum[:, c, x]

    load_bases_q.wait()

    def coef_sums(b):
        for r in range(rels):
            total = None
            for h in range(CORES):
                term = (grad_sum[r, h].reshape(rows, width) * bases_q[b, h].astype(F32)).sum(
                    axis=0, keepdims=True
                )
                total = term if total is None else total + term
            line = total[:, :128]
            for k in range(1, width // 128):
                line = line + total[:, k * 128 : (k + 1) * 128]
            coef_part[pl.ds(r * nb + b, 1), :] = line

    each(0, nb, coef_sums)

    def cp_copy(dn):
        return remote(
            coef_part, coef_recv.at[nn - dn], cp_send.at[dn], cp_recv.at[nn - dn], y_dev(dn)
        )

    for dn in range(1, nn):
        cp_copy(dn).start()

    for p in range(1, peers):
        row_copy(p).wait_recv()

    def basis_sums(b):
        total = jnp.zeros((group, width), F32)
        for p in range(peers):
            for r in range(rels):
                total = total + coefs[p, 0, r * nb + b] * row_in[p, r]
        basis_part[b % nz, b // nz] = total

    each(0, nb, basis_sums)

    def zb_copy(dz):
        return remote(
            basis_part.at[(z + dz) % nz],
            basis_in.at[nz - dz],
            zb_send.at[dz],
            zb_recv.at[nz - dz],
            z_dev(dz),
        )

    for dz in range(1, nz):
        zb_copy(dz).start()

    for dz in range(1, nz):
        zb_copy(dz).wait_recv()
    total = basis_part[z]
    for dz in range(1, nz):
        total = total + basis_in[dz]
    basis_sum[...] = total

    def xb_copy(dx):
        return remote(
            basis_sum.at[(x + dx) % nx],
            basis_rows.at[x],
            xb_send.at[dx],
            xb_recv.at[nx - dx],
            row_dev(dx * CORES),
        )

    for dx in range(1, nx):
        xb_copy(dx).start()
    basis_rows[x] = basis_sum[x]

    rx_arrived(0)
    rs_copy(1, -1).wait_recv()
    rs_copy(nz - 1, 1).wait_recv()

    def finish(o):
        arrived = rb[0, o].astype(F32) + rb[half, o].astype(F32)
        out[o] = (self_term[o] + collect(0, o) + arrived).astype(BF16)

    each(0, owned, finish)

    for dx in range(1, nx):
        remote(
            basis_sum.at[0],
            basis_rows.at[(x + dx) % nx],
            xb_send.at[dx],
            xb_recv.at[dx],
            row_dev(dx * CORES),
        ).wait_recv()
    out_basis[...] = basis_rows[...]

    for dn in range(1, nn):
        cp_copy(dn).wait_recv()
    total = coef_part[...]
    for dn in range(1, nn):
        total = total + coef_recv[dn]
    out_coef[...] = total.sum(axis=1, keepdims=True)

    z_done(zc)
    each(1, peers, lambda p: x_copy(0, ffeat, 0, p).wait_send())
    for j in range(nz):
        each(1, peers, lambda p, j=j: x_copy(1, fcot, j, p).wait_send())
        each(1, peers, lambda p, j=j: ret_copy(j, p).wait_send())
        if opposite < peers:
            for which in range(3):
                for k in range(CORES):
                    forward_copy(which, j, k).wait_send()
    for j in range(1, half + 1):
        rs_copy(j, -1).wait_send()
        rs_copy(nz - j, 1).wait_send()
    for p in range(1, peers):
        for copy in small(p):
            copy.wait_send()
        row_copy(p).wait_send()
    for dn in range(1, nn):
        y_copy(dn).wait_send()
        cp_copy(dn).wait_send()
    for dz in range(1, nz):
        zb_copy(dz).wait_send()
    for dx in range(1, nx):
        xb_copy(dx).wait_send()


def per_device(
    nx, nz, nn, features, cotangent, self_weight, bases, basis_coef, block_values, block_slots, fetch_ids
):
    rels, blocks, block, _ = block_values.shape
    width = features.shape[1]
    slots = fetch_ids.shape[0]
    owned = features.shape[0] // block
    nb = bases.shape[0]
    peers = nx * CORES
    rows = width // (CORES * nn)
    group = rows // nx

    row_slot = block_slots[:, :, 0]
    col_slot = block_slots[:, :, 1]
    at = jnp.arange(blocks, dtype=jnp.int32)
    same = (row_slot[:, :, None] == row_slot[:, None, :]) & (at[None, None, :] < at[None, :, None])
    before = jnp.max(jnp.where(same, at[None, None, :], -1), axis=2)
    here = row_slot[:, None, :] == jnp.arange(slots, dtype=jnp.int32)[None, :, None]
    last = jnp.max(jnp.where(here, at[None, None, :], -1), axis=2)
    meta = jnp.concatenate([col_slot, before, last], axis=0)
    coef32 = basis_coef.astype(F32).reshape(rels * nb)
    ids_in = jnp.zeros((1, 128), jnp.int32).at[0, :slots].set(fetch_ids)
    coef_in = jnp.zeros((1, 128), F32).at[0, : rels * nb].set(coef32)

    vmem = pl.BlockSpec(memory_space=pltpu.VMEM)
    smem = pl.BlockSpec(memory_space=pltpu.SMEM)
    anywhere = pl.BlockSpec(memory_space=pl.ANY)
    dma = pltpu.SemaphoreType.DMA
    output, basis_grad, coef_grad = pl.pallas_call(
        functools.partial(layer_kernel, nx, nz, nn),
        out_shape=(
            jax.ShapeDtypeStruct((owned, block, width), BF16),
            jax.ShapeDtypeStruct((nx, group, width), F32),
            jax.ShapeDtypeStruct((rels * nb, 1), F32),
        ),
        in_specs=[smem, smem, vmem, vmem, vmem, vmem, vmem, anywhere, anywhere, anywhere],
        out_specs=(vmem, vmem, vmem),
        scratch_shapes=[
            pltpu.VMEM((peers, 1, 128), jnp.int32),
            pltpu.VMEM((peers, 1, 128), F32),
            pltpu.SMEM((peers, 1, 128), jnp.int32),
            pltpu.SMEM((peers, 1, 128), F32),
            pltpu.VMEM((nz, owned, block, width), BF16),
            pltpu.VMEM((nz, owned, block, width), BF16),
            pltpu.VMEM((owned, block, width), BF16),
            pltpu.VMEM((nz + 1, peers, block, width), BF16),
            pltpu.VMEM((slots, block, width), BF16),
            pltpu.VMEM((slots, block, width), BF16),
            pltpu.VMEM((rels, blocks, block, block), BF16),
            pltpu.VMEM((blocks, block, width), F32),
            pltpu.VMEM((rels, slots, block, width), BF16),
            pltpu.VMEM((rels, width, width), BF16),
            pltpu.VMEM((owned, block, width), F32),
            pltpu.VMEM((nz, peers, block, width), BF16),
            pltpu.VMEM((nz, owned, block, width), BF16),
            pltpu.VMEM((3, nz, CORES, block, width), BF16),
            pltpu.VMEM((width, width), F32),
            pltpu.VMEM((nn, rels, CORES, rows, width), F32),
            pltpu.VMEM((nn, rels, CORES, rows, width), F32),
            pltpu.VMEM((rels, CORES, nx, group, width), F32),
            pltpu.VMEM((nb, CORES, rows, width), BF16),
            pltpu.VMEM((rels * nb, 128), F32),
            pltpu.VMEM((nn, rels * nb, 128), F32),
            pltpu.VMEM((peers, rels, group, width), F32),
            pltpu.VMEM((nz, nx, group, width), F32),
            pltpu.VMEM((nz, nx, group, width), F32),
            pltpu.VMEM((nx, group, width), F32),
            pltpu.VMEM((nx, group, width), F32),
            dma((5,)),
            dma((peers,)),
            dma((peers,)),
            dma((peers,)),
            dma((peers,)),
            dma((2, nz)),
            dma((2, nz)),
            dma((2, nz, peers)),
            dma((2, slots)),
            dma((nz, peers)),
            dma((nz, peers)),
            dma((3, nz, CORES)),
            dma((3, nz, CORES)),
            dma((nz,)),
            dma((nz,)),
            dma((nn,)),
            dma((nn,)),
            dma((nn,)),
            dma((nn,)),
            dma((peers,)),
            dma((peers,)),
            dma((nz,)),
            dma((nz,)),
            dma((nx,)),
            dma((nx,)),
        ],
        compiler_params=pltpu.CompilerParams(
            collective_id=0, has_side_effects=True, vmem_limit_bytes=62 * 1024 * 1024
        ),
    )(
        meta,
        coef32,
        ids_in,
        coef_in,
        features.reshape(owned, block, width),
        cotangent.reshape(owned, block, width),
        self_weight,
        bases.reshape(nb * width // block, block, width),
        bases.reshape(nb, CORES, nn, rows, width),
        block_values,
    )
    return (
        output.reshape(owned * block, width),
        basis_grad.reshape(rows, width),
        coef_grad.reshape(rels, nb),
    )


def solution(mesh, nx=4):
    nz = mesh.shape["wide"] // (CORES * nx)
    return jax.shard_map(
        functools.partial(per_device, nx, nz, mesh.shape["narrow"]),
        mesh=mesh,
        in_specs=(
            P(("wide", "narrow"), None),
            P(("wide", "narrow"), None),
            P(),
            P(),
            P("wide", None),
            P("wide", "narrow", None, None),
            P("wide", "narrow", None),
            P(("wide", "narrow")),
        ),
        out_specs=(P(("wide", "narrow"), None), P(("wide", "narrow"), None), P("wide", None)),
        check_vma=False,
    )
```

```python
import functools

import jax
import jax.numpy as jnp
from jax import lax
from jax.experimental import pallas as pl
from jax.experimental.pallas import tpu as pltpu
from jax.sharding import PartitionSpec as P

MESH = pl.DeviceIdType.MESH
F32 = jnp.float32
BF16 = jnp.bfloat16
CORES = 2


def layer_kernel(
    nx,
    nz,
    nn,
    block_slots,
    ids_in,
    coef_in,
    feat,
    cot,
    selfw,
    bases_flat,
    bases_split,
    values_hbm,
    out,
    out_basis,
    out_coef,
    meta_v,
    ids_v,
    coef_v,
    meta,
    ids,
    coefs,
    zfeat,
    zcot,
    picked,
    stage,
    ffeat,
    fcot,
    values,
    running,
    slot_g,
    weights,
    self_term,
    rx,
    rb,
    grad_acc,
    grad_parts,
    grad_in,
    grad_sum,
    bases_q,
    coef_part,
    coef_recv,
    row_in,
    basis_part,
    basis_in,
    basis_sum,
    basis_rows,
    local_sem,
    id_send,
    id_recv,
    coef_send,
    coef_recv_sem,
    z_send,
    z_recv,
    x_send,
    x_recv,
    ret_send,
    ret_recv,
    rs_send,
    rs_recv,
    y_send,
    y_recv,
    cp_send,
    cp_recv,
    row_send,
    row_recv,
    zb_send,
    zb_recv,
    xb_send,
    xb_recv,
):
    w = lax.axis_index("wide")
    n = lax.axis_index("narrow")
    x, z, c = w // (CORES * nz), (w // CORES) % nz, w % CORES
    peers = nx * CORES
    owned, block, width = feat.shape
    slots = ffeat.shape[0]
    rels = slot_g.shape[0]
    blocks = values.shape[1]
    nb = basis_part.shape[0] * basis_part.shape[1]
    group = grad_sum.shape[3]
    half = nz // 2
    cut = owned // 2

    def slot(xs, zs, cs):
        return (xs * nz + zs) * CORES + cs

    def peer(p):
        return (x + p // CORES) % nx, (c + p % CORES) % CORES

    def row_dev(p):
        xp, cp = peer(p)
        return (slot(xp, z, cp), n)

    def back(p):
        return ((nx - p // CORES) % nx) * CORES + p % CORES

    def z_dev(dz):
        return (slot(x, (z + dz + nz) % nz, c), n)

    def y_dev(dn):
        return (w, (n + dn) % nn)

    def remote(src, dst, ssem, rsem, dev):
        return pltpu.make_async_remote_copy(
            src_ref=src, dst_ref=dst, send_sem=ssem, recv_sem=rsem, device_id=dev, device_id_type=MESH
        )

    def each(lo, hi, body):
        def step(i, carry):
            body(i)
            return carry

        lax.fori_loop(lo, hi, step, 0)

    load_bases = pltpu.make_async_copy(bases_flat, slot_g.at[1], local_sem.at[0])
    load_values = pltpu.make_async_copy(values_hbm, values, local_sem.at[1])
    load_bases_q = pltpu.make_async_copy(bases_split.at[:, :, n], bases_q, local_sem.at[2])
    load_bases.start()
    load_values.start()
    load_bases_q.start()

    barrier = pltpu.get_barrier_semaphore()
    for p in range(1, peers):
        pl.semaphore_signal(barrier, inc=1, device_id=row_dev(p), device_id_type=MESH)
    for dz in range(1, nz):
        pl.semaphore_signal(barrier, inc=1, device_id=z_dev(dz), device_id_type=MESH)
    for dn in range(1, nn):
        pl.semaphore_signal(barrier, inc=1, device_id=y_dev(dn), device_id_type=MESH)
    pl.semaphore_wait(barrier, peers + nz + nn - 3)

    def z_copy(which, own, buf, to, way):
        frm = to - 1 if way > 0 else (to + 1) % nz
        src = own if frm == 0 else buf.at[frm]
        dst = buf.at[to]
        sem = to
        if to == half:
            part = pl.ds(0, cut) if way > 0 else pl.ds(cut, cut)
            src, dst = src.at[part], dst.at[part]
            sem = half if way > 0 else 0
        return remote(src, dst, z_send.at[which, sem], z_recv.at[which, sem], z_dev(way))

    zf = functools.partial(z_copy, 0, feat, zfeat)
    zc = functools.partial(z_copy, 1, cot, zcot)

    def z_first(zcp):
        zcp(1, 1).start()
        zcp(nz - 1, -1).start()

    def z_step(zcp, d):
        if d < half:
            zcp(d, 1).wait_recv()
            zcp(d + 1, 1).start()
            zcp(nz - d, -1).wait_recv()
            zcp(nz - d - 1, -1).start()
        else:
            zcp(half, 1).wait_recv()
            zcp(half, -1).wait_recv()

    def z_done(zcp):
        for d in range(1, half + 1):
            zcp(d, 1).wait_send()
            zcp(nz - d, -1).wait_send()

    def x_copy(which, dst, j, p):
        at = nz if which == 1 and j == 0 else j
        s = slot(x, (z - j + nz) % nz, c)
        return remote(
            stage.at[at, p], dst.at[s], x_send.at[which, j, p], x_recv.at[which, s], row_dev(p)
        )

    def x_step(which, own, buf, dst, j):
        src = own
        if j > 0:
            picked[...] = buf[j]
            src = picked
        at = nz if which == 1 and j == 0 else j
        s = slot(x, (z - j + nz) % nz, c)
        if which == 1 and j > 0:
            each(1, peers, lambda p: x_copy(0, ffeat, j, p).wait_send())

        def send(p):
            stage[at, p] = src[ids[p, 0, s]]
            x_copy(which, dst, j, p).start()

        each(1, peers, send)
        dst[s] = src[ids[0, 0, s]]

    xf = functools.partial(x_step, 0, feat, zfeat, ffeat)
    xc = functools.partial(x_step, 1, cot, zcot, fcot)

    def x_arrived(which, dst):
        def arrived(q):
            p = q // nz + 1
            xp, cp = peer(p)
            s = slot(xp, q % nz, cp)
            remote(
                stage.at[0, 0], dst.at[s], x_send.at[which, 0, 0], x_recv.at[which, s], row_dev(p)
            ).wait_recv()

        each(0, (peers - 1) * nz, arrived)

    z_first(zf)
    ids_v[0] = jnp.zeros_like(ids_v[0])
    ids_v[0, :, :slots] = ids_in[...]
    coef_v[0] = jnp.zeros_like(coef_v[0])
    coef_v[0, :, :nb] = coef_in[...].astype(F32)

    def small(p):
        return (
            remote(ids_v.at[0], ids_v.at[back(p)], id_send.at[p], id_recv.at[back(p)], row_dev(p)),
            remote(
                coef_v.at[0], coef_v.at[back(p)], coef_send.at[p], coef_recv_sem.at[back(p)], row_dev(p)
            ),
        )

    for p in range(1, peers):
        for copy in small(p):
            copy.start()

    own_coef_down = pltpu.make_async_copy(coef_v.at[0], coefs.at[0], local_sem.at[4])
    own_coef_down.start()

    meta_v[...] = jnp.zeros_like(meta_v)
    down = lax.broadcasted_iota(jnp.int32, (blocks, blocks), 0)
    across = lax.broadcasted_iota(jnp.int32, (blocks, blocks), 1)
    down_slot = lax.broadcasted_iota(jnp.int32, (blocks, slots), 0)
    across_slot = lax.broadcasted_iota(jnp.int32, (blocks, slots), 1)
    for r in range(rels):
        row = block_slots[r, 0:1, :]
        spread = jnp.broadcast_to(row, (blocks, blocks))
        column = jnp.max(jnp.where(down == across, spread, -1), axis=1, keepdims=True)
        same = (column == spread) & (down < across)
        meta_v[r, :, :blocks] = block_slots[r, 1:2, :]
        meta_v[rels + r, :, :blocks] = jnp.max(jnp.where(same, down, -1), axis=0, keepdims=True)
        meta_v[2 * rels + r, :, :slots] = jnp.max(
            jnp.where(column == across_slot, down_slot, -1), axis=0, keepdims=True
        )
    meta_down = pltpu.make_async_copy(meta_v, meta, local_sem.at[5])
    meta_down.start()
    meta_down.wait()
    own_coef_down.wait()
    load_bases.wait()
    tile = 16
    per = block // tile
    parts = width // block

    def weigh(t):
        hb = t // per
        row = pl.multiple_of((t % per) * tile, tile)
        acc = [jnp.zeros((tile, width), F32) for _ in range(rels)]
        for b in range(nb):
            v = slot_g[1, b * parts + hb, pl.ds(row, tile), :].astype(F32)
            for r in range(rels):
                acc[r] = acc[r] + coefs[0, r, b] * v
        for r in range(rels):
            weights[r, pl.ds(pl.multiple_of(hb * block + row, tile), tile), :] = acc[r].astype(BF16)

    each(0, parts * per, weigh)

    for p in range(1, peers):
        for copy in small(p):
            copy.wait_recv()
    ids_down = pltpu.make_async_copy(ids_v, ids, local_sem.at[3])
    coef_down = pltpu.make_async_copy(
        coef_v.at[pl.ds(1, peers - 1)], coefs.at[pl.ds(1, peers - 1)], local_sem.at[4]
    )
    ids_down.start()
    coef_down.start()
    ids_down.wait()
    coef_down.wait()

    xf(0)
    xc(0)

    def own_term(o):
        self_term[o] = jnp.dot(feat[o], selfw[...], preferred_element_type=F32)

    each(0, owned, own_term)

    for d in range(1, half):
        z_step(zf, d)
        if d == half - 1:
            z_first(zc)
        xf(d)
        xf(nz - d)
    z_step(zf, half)
    xf(half)

    z_step(zc, 1)
    xc(1)
    xc(nz - 1)
    load_values.wait()
    x_arrived(0, ffeat)

    burst = 4

    def messages(r):
        def some(q):
            found = []
            for u in range(burst):
                j = q * burst + u
                found.append(
                    jnp.dot(values[r, j], ffeat[meta[r, 0, j]], preferred_element_type=F32).astype(BF16)
                )
            for u in range(burst):
                j = q * burst + u
                before = meta[rels + r, 0, j]
                earlier = running[jnp.maximum(before, 0)]
                running[j] = jnp.where(before >= 0, earlier, 0.0) + found[u].astype(F32)

        each(0, blocks // burst, some)

        def pick(s):
            at = meta[2 * rels + r, 0, s]
            slot_g[r, s] = jnp.where(at >= 0, running[jnp.maximum(at, 0)], 0.0).astype(BF16)

        each(0, slots, pick)

    messages(0)
    for d in range(2, half - 1):
        z_step(zc, d)
        xc(d)
        xc(nz - d)
    messages(1)
    if half > 2:
        z_step(zc, half - 1)
        xc(half - 1)
        xc(half + 1)
    z_done(zf)
    slot_sums = zfeat

    def sum_slots(m):
        rows = (owned * block, width)
        at = pl.ds(m * owned, owned)
        total = jnp.dot(slot_g[0, at].reshape(rows), weights[0], preferred_element_type=F32)
        for r in range(1, rels):
            total += jnp.dot(slot_g[r, at].reshape(rows), weights[r], preferred_element_type=F32)
        slot_sums[m] = total.astype(BF16).reshape(owned, block, width)

    each(0, nz, sum_slots)

    def ret_copy(j, p):
        xp, cp = peer(p)
        s = slot(xp, (z - j + nz) % nz, cp)
        return remote(
            slot_sums.at[s // owned, s % owned],
            rx.at[j, back(p)],
            ret_send.at[j, p],
            ret_recv.at[j, back(p)],
            row_dev(p),
        )

    def ret_go(j):
        each(1, peers, lambda p: ret_copy(j, p).start())

    z_step(zc, half)
    xc(half)
    ret_go(half)
    for d in range(half - 1, 0, -1):
        ret_go(d)
        ret_go(nz - d)
    ret_go(0)

    def rs_copy(j, way):
        to = j - 1 if way < 0 else (j + 1) % nz
        at = half if way > 0 and to == 0 else to
        src, dst = ffeat.at[pl.ds(j * owned, owned)], rb.at[at]
        if j == half:
            first = 0 if way < 0 else cut
            src, dst = ffeat.at[pl.ds(j * owned + first, cut)], rb.at[at, pl.ds(first, cut)]
        return remote(src, dst, rs_send.at[at], rs_recv.at[at], z_dev(way))

    def collect(j, o):
        s = slot(x, (z - j + nz) % nz, c)
        total = None
        for p in range(peers):
            weight = jnp.where(ids[p, 0, s] == o, 1.0, 0.0).astype(F32)
            term = (slot_sums[s // owned, s % owned] if p == 0 else rx[j, p]).astype(F32) * weight
            total = term if total is None else total + term
        return total

    def rx_arrived(j):
        each(
            1,
            peers,
            lambda p: remote(
                stage.at[0, 0], rx.at[j, p], ret_send.at[j, 0], ret_recv.at[j, p], row_dev(p)
            ).wait_recv(),
        )

    def reduce_step(j):
        rx_arrived(j)
        lo, hi = 0, 0
        if 0 < j < half:
            rs_copy(j + 1, -1).wait_recv()
            lo, hi = 0, (cut if j + 1 == half else owned)
        elif j > half:
            rs_copy(j - 1, 1).wait_recv()
            lo, hi = (cut if j - 1 == half else 0), owned

        def plain(o):
            ffeat[j * owned + o] = collect(j, o).astype(BF16)

        def more(o):
            ffeat[j * owned + o] = (collect(j, o) + rb[j, o].astype(F32)).astype(BF16)

        if lo > 0:
            each(0, lo, plain)
        if hi > lo:
            each(lo, hi, more)
        if hi < owned:
            each(hi, owned, plain)
        if j <= half:
            rs_copy(j, -1).start()
        if j >= half:
            rs_copy(j, 1).start()

    x_arrived(1, fcot)

    def relation_grad(r):
        grad_acc[...] = jnp.zeros_like(grad_acc)

        def add(m):
            at = pl.ds(m * owned, owned)
            rows = (owned * block, width)
            grad_acc[...] += lax.dot_general(
                slot_g[r, at].reshape(rows),
                fcot[at].reshape(rows),
                (((0,), (0,)), ((), ())),
                preferred_element_type=F32,
            )

        each(0, nz, add)
        rows = grad_parts.shape[3]
        for h in range(CORES):
            for m in range(nn):
                grad_parts[m, r, h] = grad_acc[pl.ds((h * nn + m) * rows, rows), :]

    relation_grad(0)
    reduce_step(half)
    for r in range(1, rels):
        relation_grad(r)

    def y_copy(dn):
        return remote(
            grad_parts.at[(n + dn) % nn],
            grad_in.at[nn - dn],
            y_send.at[dn],
            y_recv.at[nn - dn],
            y_dev(dn),
        )

    for dn in range(1, nn):
        y_copy(dn).start()

    def reduce_pair(d):
        reduce_step(d)
        reduce_step(nz - d)

    reduce_pair(half - 1)

    for dn in range(1, nn):
        y_copy(dn).wait_recv()
    rows = grad_parts.shape[3]
    for r in range(rels):
        for h in range(CORES):
            total = grad_parts[n, r, h]
            for dn in range(1, nn):
                total = total + grad_in[dn, r, h]
            grad_sum[r, h] = total.reshape(nx, group, width)

    def row_copy(p):
        xp, cp = peer(p)
        return remote(
            grad_sum.at[:, cp, xp], row_in.at[back(p)], row_send.at[p], row_recv.at[back(p)], row_dev(p)
        )

    for p in range(1, peers):
        row_copy(p).start()
    row_in[0] = grad_sum[:, c, x]

    load_bases_q.wait()

    def coef_sums(b):
        for r in range(rels):
            total = None
            for h in range(CORES):
                term = (grad_sum[r, h].reshape(rows, width) * bases_q[b, h].astype(F32)).sum(
                    axis=0, keepdims=True
                )
                total = term if total is None else total + term
            line = total[:, :128]
            for k in range(1, width // 128):
                line = line + total[:, k * 128 : (k + 1) * 128]
            coef_part[pl.ds(r * nb + b, 1), :] = line

    each(0, nb, coef_sums)

    def cp_copy(dn):
        return remote(
            coef_part, coef_recv.at[nn - dn], cp_send.at[dn], cp_recv.at[nn - dn], y_dev(dn)
        )

    for dn in range(1, nn):
        cp_copy(dn).start()

    if half > 2:
        reduce_pair(half - 2)

    for p in range(1, peers):
        row_copy(p).wait_recv()

    def basis_sums(b):
        total = jnp.zeros((group, width), F32)
        for p in range(peers):
            for r in range(rels):
                total = total + coefs[p, r, b] * row_in[p, r]
        basis_part[b % nz, b // nz] = total

    each(0, nb, basis_sums)

    def zb_copy(dz):
        return remote(
            basis_part.at[(z + dz) % nz],
            basis_in.at[nz - dz],
            zb_send.at[dz],
            zb_recv.at[nz - dz],
            z_dev(dz),
        )

    for dz in range(1, nz):
        zb_copy(dz).start()

    for d in range(half - 3, 0, -1):
        reduce_pair(d)

    for dz in range(1, nz):
        zb_copy(dz).wait_recv()
    total = basis_part[z]
    for dz in range(1, nz):
        total = total + basis_in[dz]
    basis_sum[...] = total

    def xb_copy(dx):
        return remote(
            basis_sum.at[(x + dx) % nx],
            basis_rows.at[x],
            xb_send.at[dx],
            xb_recv.at[nx - dx],
            row_dev(dx * CORES),
        )

    for dx in range(1, nx):
        xb_copy(dx).start()
    basis_rows[x] = basis_sum[x]

    rx_arrived(0)
    rs_copy(1, -1).wait_recv()
    rs_copy(nz - 1, 1).wait_recv()

    def finish(o):
        arrived = rb[0, o].astype(F32) + rb[half, o].astype(F32)
        out[o] = (self_term[o] + collect(0, o) + arrived).astype(BF16)

    each(0, owned, finish)

    for dx in range(1, nx):
        remote(
            basis_sum.at[0],
            basis_rows.at[(x + dx) % nx],
            xb_send.at[dx],
            xb_recv.at[dx],
            row_dev(dx * CORES),
        ).wait_recv()
    out_basis[...] = basis_rows[...]

    for dn in range(1, nn):
        cp_copy(dn).wait_recv()
    total = coef_part[...]
    for dn in range(1, nn):
        total = total + coef_recv[dn]
    column = total.sum(axis=1, keepdims=True)
    wide_shape = (rels * nb, rels * nb)
    diagonal = lax.broadcasted_iota(jnp.int32, wide_shape, 0) == lax.broadcasted_iota(
        jnp.int32, wide_shape, 1
    )
    line = jnp.where(diagonal, jnp.broadcast_to(column, wide_shape), 0.0).sum(axis=0, keepdims=True)
    for r in range(rels):
        out_coef[r : r + 1, :] = line[:, r * nb : (r + 1) * nb]

    z_done(zc)
    each(1, peers, lambda p: x_copy(0, ffeat, 0, p).wait_send())
    for j in range(nz):
        each(1, peers, lambda p, j=j: x_copy(1, fcot, j, p).wait_send())
        each(1, peers, lambda p, j=j: ret_copy(j, p).wait_send())
    for j in range(1, half + 1):
        rs_copy(j, -1).wait_send()
        rs_copy(nz - j, 1).wait_send()
    for p in range(1, peers):
        for copy in small(p):
            copy.wait_send()
        row_copy(p).wait_send()
    for dn in range(1, nn):
        y_copy(dn).wait_send()
        cp_copy(dn).wait_send()
    for dz in range(1, nz):
        zb_copy(dz).wait_send()
    for dx in range(1, nx):
        xb_copy(dx).wait_send()


def keep_kernel(a, b, c, a_out, b_out, c_out, sem):
    copies = [
        pltpu.make_async_copy(src, dst, sem.at[i])
        for i, (src, dst) in enumerate(((a, a_out), (b, b_out), (c, c_out)))
    ]
    for copy in copies:
        copy.start()
    for copy in copies:
        copy.wait()


def per_device(
    nx, nz, nn, features, cotangent, self_weight, bases, basis_coef, block_values, block_slots, fetch_ids
):
    rels, blocks, block, _ = block_values.shape
    width = features.shape[1]
    slots = fetch_ids.shape[0]
    owned = features.shape[0] // block
    nb = bases.shape[0]
    peers = nx * CORES
    rows = width // (CORES * nn)
    group = rows // nx

    vmem = pl.BlockSpec(memory_space=pltpu.VMEM)
    anywhere = pl.BlockSpec(memory_space=pl.ANY)
    dma = pltpu.SemaphoreType.DMA
    output, basis_grad, coef_grad = pl.pallas_call(
        functools.partial(layer_kernel, nx, nz, nn),
        out_shape=(
            jax.ShapeDtypeStruct((owned, block, width), BF16),
            jax.ShapeDtypeStruct((nx, group, width), F32),
            jax.ShapeDtypeStruct((rels, nb), F32),
        ),
        in_specs=[vmem, vmem, vmem, vmem, vmem, vmem, anywhere, anywhere, anywhere],
        out_specs=(vmem, vmem, vmem),
        scratch_shapes=[
            pltpu.VMEM((3 * rels, 1, 128), jnp.int32),
            pltpu.VMEM((peers, 1, 128), jnp.int32),
            pltpu.VMEM((peers, rels, 128), F32),
            pltpu.SMEM((3 * rels, 1, 128), jnp.int32),
            pltpu.SMEM((peers, 1, 128), jnp.int32),
            pltpu.SMEM((peers, rels, 128), F32),
            pltpu.VMEM((nz, owned, block, width), BF16),
            pltpu.VMEM((nz, owned, block, width), BF16),
            pltpu.VMEM((owned, block, width), BF16),
            pltpu.VMEM((nz + 1, peers, block, width), BF16),
            pltpu.VMEM((slots, block, width), BF16),
            pltpu.VMEM((slots, block, width), BF16),
            pltpu.VMEM((rels, blocks, block, block), BF16),
            pltpu.VMEM((blocks, block, width), F32),
            pltpu.VMEM((rels, slots, block, width), BF16),
            pltpu.VMEM((rels, width, width), BF16),
            pltpu.VMEM((owned, block, width), F32),
            pltpu.VMEM((nz, peers, block, width), BF16),
            pltpu.VMEM((nz, owned, block, width), BF16),
            pltpu.VMEM((width, width), F32),
            pltpu.VMEM((nn, rels, CORES, rows, width), F32),
            pltpu.VMEM((nn, rels, CORES, rows, width), F32),
            pltpu.VMEM((rels, CORES, nx, group, width), F32),
            pltpu.VMEM((nb, CORES, rows, width), BF16),
            pltpu.VMEM((rels * nb, 128), F32),
            pltpu.VMEM((nn, rels * nb, 128), F32),
            pltpu.VMEM((peers, rels, group, width), F32),
            pltpu.VMEM((nz, nx, group, width), F32),
            pltpu.VMEM((nz, nx, group, width), F32),
            pltpu.VMEM((nx, group, width), F32),
            pltpu.VMEM((nx, group, width), F32),
            dma((6,)),
            dma((peers,)),
            dma((peers,)),
            dma((peers,)),
            dma((peers,)),
            dma((2, nz)),
            dma((2, nz)),
            dma((2, nz, peers)),
            dma((2, slots)),
            dma((nz, peers)),
            dma((nz, peers)),
            dma((nz,)),
            dma((nz,)),
            dma((nn,)),
            dma((nn,)),
            dma((nn,)),
            dma((nn,)),
            dma((peers,)),
            dma((peers,)),
            dma((nz,)),
            dma((nz,)),
            dma((nx,)),
            dma((nx,)),
        ],
        compiler_params=pltpu.CompilerParams(
            collective_id=0, has_side_effects=True, vmem_limit_bytes=62 * 1024 * 1024
        ),
    )(
        block_slots.transpose(0, 2, 1),
        fetch_ids.reshape(1, slots),
        basis_coef,
        features.reshape(owned, block, width),
        cotangent.reshape(owned, block, width),
        self_weight,
        bases.reshape(nb * width // block, block, width),
        bases.reshape(nb, CORES, nn, rows, width),
        block_values,
    )
    output, basis_grad, coef_grad = pl.pallas_call(
        keep_kernel,
        out_shape=tuple(jax.ShapeDtypeStruct(a.shape, a.dtype) for a in (output, basis_grad, coef_grad)),
        in_specs=[anywhere] * 3,
        out_specs=(anywhere,) * 3,
        scratch_shapes=[dma((3,))],
        compiler_params=pltpu.CompilerParams(vmem_limit_bytes=62 * 1024 * 1024),
    )(output, basis_grad, coef_grad)
    return (
        output.reshape(owned * block, width),
        basis_grad.reshape(rows, width),
        coef_grad,
    )


def solution(mesh, nx=4):
    nz = mesh.shape["wide"] // (CORES * nx)
    return jax.shard_map(
        functools.partial(per_device, nx, nz, mesh.shape["narrow"]),
        mesh=mesh,
        in_specs=(
            P(("wide", "narrow"), None),
            P(("wide", "narrow"), None),
            P(),
            P(),
            P("wide", None),
            P("wide", "narrow", None, None),
            P("wide", "narrow", None),
            P(("wide", "narrow")),
        ),
        out_specs=(P(("wide", "narrow"), None), P(("wide", "narrow"), None), P("wide", None)),
        check_vma=False,
    )
```

```python
import functools

import jax
import jax.numpy as jnp
from jax import lax
from jax.experimental import pallas as pl
from jax.experimental.pallas import tpu as pltpu
from jax.sharding import PartitionSpec as P

MESH = pl.DeviceIdType.MESH
F32 = jnp.float32
BF16 = jnp.bfloat16
CORES = 2


def layer_kernel(
    nx,
    nz,
    nn,
    block_slots,
    ids_in,
    coef_in,
    feat,
    cot,
    selfw,
    bases_flat,
    bases_split,
    values_hbm,
    out,
    out_basis,
    out_coef,
    meta_v,
    ids_v,
    coef_v,
    meta,
    ids,
    coefs,
    zfeat,
    zcot,
    picked,
    stage,
    ffeat,
    fcot,
    values,
    running,
    slot_g,
    weights,
    self_term,
    rx,
    rb,
    grad_acc,
    grad_parts,
    grad_in,
    grad_sum,
    bases_q,
    coef_part,
    coef_recv,
    row_in,
    basis_part,
    basis_in,
    basis_sum,
    basis_rows,
    local_sem,
    id_send,
    id_recv,
    coef_send,
    coef_recv_sem,
    z_send,
    z_recv,
    x_send,
    x_recv,
    ret_send,
    ret_recv,
    rs_send,
    rs_recv,
    y_send,
    y_recv,
    cp_send,
    cp_recv,
    row_send,
    row_recv,
    zb_send,
    zb_recv,
    xb_send,
    xb_recv,
):
    w = lax.axis_index("wide")
    n = lax.axis_index("narrow")
    x, z, c = w // (CORES * nz), (w // CORES) % nz, w % CORES
    peers = nx * CORES
    owned, block, width = feat.shape
    slots = ffeat.shape[0]
    rels = slot_g.shape[0]
    blocks = values.shape[1]
    nb = basis_part.shape[0] * basis_part.shape[1]
    group = grad_sum.shape[3]
    half = nz // 2
    cut = owned // 2

    def slot(xs, zs, cs):
        return (xs * nz + zs) * CORES + cs

    def peer(p):
        return (x + p // CORES) % nx, (c + p % CORES) % CORES

    def row_dev(p):
        xp, cp = peer(p)
        return (slot(xp, z, cp), n)

    def back(p):
        return ((nx - p // CORES) % nx) * CORES + p % CORES

    def z_dev(dz):
        return (slot(x, (z + dz + nz) % nz, c), n)

    def y_dev(dn):
        return (w, (n + dn) % nn)

    def remote(src, dst, ssem, rsem, dev):
        return pltpu.make_async_remote_copy(
            src_ref=src, dst_ref=dst, send_sem=ssem, recv_sem=rsem, device_id=dev, device_id_type=MESH
        )

    def each(lo, hi, body):
        def step(i, carry):
            body(i)
            return carry

        lax.fori_loop(lo, hi, step, 0)

    load_bases = pltpu.make_async_copy(bases_flat, slot_g.at[1], local_sem.at[0])
    load_values = pltpu.make_async_copy(values_hbm, values, local_sem.at[1])
    load_bases_q = pltpu.make_async_copy(bases_split.at[:, :, n], bases_q, local_sem.at[2])
    load_bases.start()
    load_values.start()
    load_bases_q.start()

    barrier = pltpu.get_barrier_semaphore()
    for p in range(1, peers):
        pl.semaphore_signal(barrier, inc=1, device_id=row_dev(p), device_id_type=MESH)
    for dz in range(1, nz):
        pl.semaphore_signal(barrier, inc=1, device_id=z_dev(dz), device_id_type=MESH)
    for dn in range(1, nn):
        pl.semaphore_signal(barrier, inc=1, device_id=y_dev(dn), device_id_type=MESH)
    pl.semaphore_wait(barrier, peers + nz + nn - 3)

    def z_copy(which, own, buf, to, way):
        frm = to - 1 if way > 0 else (to + 1) % nz
        src = own if frm == 0 else buf.at[frm]
        dst = buf.at[to]
        sem = to
        if to == half:
            part = pl.ds(0, cut) if way > 0 else pl.ds(cut, cut)
            src, dst = src.at[part], dst.at[part]
            sem = half if way > 0 else 0
        return remote(src, dst, z_send.at[which, sem], z_recv.at[which, sem], z_dev(way))

    zf = functools.partial(z_copy, 0, feat, zfeat)
    zc = functools.partial(z_copy, 1, cot, zcot)

    def z_first(zcp):
        zcp(1, 1).start()
        zcp(nz - 1, -1).start()

    def z_step(zcp, d):
        if d < half:
            zcp(d, 1).wait_recv()
            zcp(d + 1, 1).start()
            zcp(nz - d, -1).wait_recv()
            zcp(nz - d - 1, -1).start()
        else:
            zcp(half, 1).wait_recv()
            zcp(half, -1).wait_recv()

    def z_done(zcp):
        for d in range(1, half + 1):
            zcp(d, 1).wait_send()
            zcp(nz - d, -1).wait_send()

    def x_copy(which, dst, j, p):
        at = nz if which == 1 and j == 0 else j
        s = slot(x, (z - j + nz) % nz, c)
        return remote(
            stage.at[at, p], dst.at[s], x_send.at[which, j, p], x_recv.at[which, s], row_dev(p)
        )

    def x_step(which, own, buf, dst, j):
        src = own
        if j > 0:
            picked[...] = buf[j]
            src = picked
        at = nz if which == 1 and j == 0 else j
        s = slot(x, (z - j + nz) % nz, c)
        if which == 1 and j > 0:
            each(1, peers, lambda p: x_copy(0, ffeat, j, p).wait_send())

        def send(p):
            stage[at, p] = src[ids[p, 0, s]]
            x_copy(which, dst, j, p).start()

        each(1, peers, send)
        dst[s] = src[ids[0, 0, s]]

    xf = functools.partial(x_step, 0, feat, zfeat, ffeat)
    xc = functools.partial(x_step, 1, cot, zcot, fcot)

    def x_arrived(which, dst):
        def arrived(q):
            p = q // nz + 1
            xp, cp = peer(p)
            s = slot(xp, q % nz, cp)
            remote(
                stage.at[0, 0], dst.at[s], x_send.at[which, 0, 0], x_recv.at[which, s], row_dev(p)
            ).wait_recv()

        each(0, (peers - 1) * nz, arrived)

    z_first(zf)
    ids_v[0] = jnp.zeros_like(ids_v[0])
    ids_v[0, :, :slots] = ids_in[...]
    coef_v[0] = jnp.zeros_like(coef_v[0])
    coef_v[0, :, :nb] = coef_in[...].astype(F32)

    def small(p):
        return (
            remote(ids_v.at[0], ids_v.at[back(p)], id_send.at[p], id_recv.at[back(p)], row_dev(p)),
            remote(
                coef_v.at[0], coef_v.at[back(p)], coef_send.at[p], coef_recv_sem.at[back(p)], row_dev(p)
            ),
        )

    for p in range(1, peers):
        for copy in small(p):
            copy.start()

    own_coef_down = pltpu.make_async_copy(coef_v.at[0], coefs.at[0], local_sem.at[4])
    own_coef_down.start()

    meta_v[...] = jnp.zeros_like(meta_v)
    down = lax.broadcasted_iota(jnp.int32, (blocks, blocks), 0)
    across = lax.broadcasted_iota(jnp.int32, (blocks, blocks), 1)
    down_slot = lax.broadcasted_iota(jnp.int32, (blocks, slots), 0)
    across_slot = lax.broadcasted_iota(jnp.int32, (blocks, slots), 1)
    for r in range(rels):
        row = block_slots[r, 0:1, :]
        spread = jnp.broadcast_to(row, (blocks, blocks))
        column = jnp.max(jnp.where(down == across, spread, -1), axis=1, keepdims=True)
        same = (column == spread) & (down < across)
        meta_v[r, :, :blocks] = block_slots[r, 1:2, :]
        meta_v[rels + r, :, :blocks] = jnp.max(jnp.where(same, down, -1), axis=0, keepdims=True)
        meta_v[2 * rels + r, :, :slots] = jnp.max(
            jnp.where(column == across_slot, down_slot, -1), axis=0, keepdims=True
        )
    meta_down = pltpu.make_async_copy(meta_v, meta, local_sem.at[5])
    meta_down.start()
    meta_down.wait()
    own_coef_down.wait()

    for p in range(1, peers):
        for copy in small(p):
            copy.wait_recv()
    ids_down = pltpu.make_async_copy(ids_v, ids, local_sem.at[3])
    coef_down = pltpu.make_async_copy(
        coef_v.at[pl.ds(1, peers - 1)], coefs.at[pl.ds(1, peers - 1)], local_sem.at[4]
    )
    ids_down.start()
    coef_down.start()
    ids_down.wait()
    coef_down.wait()

    xf(0)
    xc(0)

    load_bases.wait()
    tile = 16
    per = block // tile
    parts = width // block

    def weigh(t):
        hb = t // per
        row = pl.multiple_of((t % per) * tile, tile)
        acc = [jnp.zeros((tile, width), F32) for _ in range(rels)]
        for b in range(nb):
            v = slot_g[1, b * parts + hb, pl.ds(row, tile), :].astype(F32)
            for r in range(rels):
                acc[r] = acc[r] + coefs[0, r, b] * v
        for r in range(rels):
            weights[r, pl.ds(pl.multiple_of(hb * block + row, tile), tile), :] = acc[r].astype(BF16)

    each(0, parts * per, weigh)

    def own_term(o):
        self_term[o] = jnp.dot(feat[o], selfw[...], preferred_element_type=F32)

    each(0, owned, own_term)

    for d in range(1, half):
        z_step(zf, d)
        if d == half - 1:
            z_first(zc)
        xf(d)
        xf(nz - d)
    z_step(zf, half)
    xf(half)

    z_step(zc, 1)
    xc(1)
    xc(nz - 1)
    load_values.wait()
    x_arrived(0, ffeat)

    burst = 4

    def messages(r):
        def some(q):
            found = []
            for u in range(burst):
                j = q * burst + u
                found.append(
                    jnp.dot(values[r, j], ffeat[meta[r, 0, j]], preferred_element_type=F32).astype(BF16)
                )
            for u in range(burst):
                j = q * burst + u
                before = meta[rels + r, 0, j]
                earlier = running[jnp.maximum(before, 0)]
                running[j] = jnp.where(before >= 0, earlier, 0.0) + found[u].astype(F32)

        each(0, blocks // burst, some)

        def pick(s):
            at = meta[2 * rels + r, 0, s]
            slot_g[r, s] = jnp.where(at >= 0, running[jnp.maximum(at, 0)], 0.0).astype(BF16)

        each(0, slots, pick)

    messages(0)
    for d in range(2, half - 1):
        z_step(zc, d)
        xc(d)
        xc(nz - d)
    messages(1)
    if half > 2:
        z_step(zc, half - 1)
        xc(half - 1)
        xc(half + 1)
    z_done(zf)
    slot_sums = zfeat

    def sum_slots(m):
        rows = (owned * block, width)
        at = pl.ds(m * owned, owned)
        total = jnp.dot(slot_g[0, at].reshape(rows), weights[0], preferred_element_type=F32)
        for r in range(1, rels):
            total += jnp.dot(slot_g[r, at].reshape(rows), weights[r], preferred_element_type=F32)
        slot_sums[m] = total.astype(BF16).reshape(owned, block, width)

    each(0, nz, sum_slots)

    def ret_copy(j, p):
        xp, cp = peer(p)
        s = slot(xp, (z - j + nz) % nz, cp)
        return remote(
            slot_sums.at[s // owned, s % owned],
            rx.at[j, back(p)],
            ret_send.at[j, p],
            ret_recv.at[j, back(p)],
            row_dev(p),
        )

    def ret_go(j):
        each(1, peers, lambda p: ret_copy(j, p).start())

    z_step(zc, half)
    xc(half)
    def ret_pair(d):
        if d > 0:
            ret_go(d)
            ret_go(nz - d)
        elif d == 0:
            ret_go(0)

    ret_go(half)
    ret_pair(half - 1)

    def rs_copy(j, way):
        to = j - 1 if way < 0 else (j + 1) % nz
        at = half if way > 0 and to == 0 else to
        src, dst = ffeat.at[pl.ds(j * owned, owned)], rb.at[at]
        if j == half:
            first = 0 if way < 0 else cut
            src, dst = ffeat.at[pl.ds(j * owned + first, cut)], rb.at[at, pl.ds(first, cut)]
        return remote(src, dst, rs_send.at[at], rs_recv.at[at], z_dev(way))

    def collect(j, o):
        s = slot(x, (z - j + nz) % nz, c)
        total = None
        for p in range(peers):
            weight = jnp.where(ids[p, 0, s] == o, 1.0, 0.0).astype(F32)
            term = (slot_sums[s // owned, s % owned] if p == 0 else rx[j, p]).astype(F32) * weight
            total = term if total is None else total + term
        return total

    def rx_arrived(j):
        each(
            1,
            peers,
            lambda p: remote(
                stage.at[0, 0], rx.at[j, p], ret_send.at[j, 0], ret_recv.at[j, p], row_dev(p)
            ).wait_recv(),
        )

    def reduce_step(j):
        rx_arrived(j)
        lo, hi = 0, 0
        if 0 < j < half:
            rs_copy(j + 1, -1).wait_recv()
            lo, hi = 0, (cut if j + 1 == half else owned)
        elif j > half:
            rs_copy(j - 1, 1).wait_recv()
            lo, hi = (cut if j - 1 == half else 0), owned

        def plain(o):
            ffeat[j * owned + o] = collect(j, o).astype(BF16)

        def more(o):
            ffeat[j * owned + o] = (collect(j, o) + rb[j, o].astype(F32)).astype(BF16)

        if lo > 0:
            each(0, lo, plain)
        if hi > lo:
            each(lo, hi, more)
        if hi < owned:
            each(hi, owned, plain)
        if j <= half:
            rs_copy(j, -1).start()
        if j >= half:
            rs_copy(j, 1).start()

    x_arrived(1, fcot)

    def relation_grad(r):
        grad_acc[...] = jnp.zeros_like(grad_acc)

        def add(m):
            at = pl.ds(m * owned, owned)
            rows = (owned * block, width)
            grad_acc[...] += lax.dot_general(
                slot_g[r, at].reshape(rows),
                fcot[at].reshape(rows),
                (((0,), (0,)), ((), ())),
                preferred_element_type=F32,
            )

        each(0, nz, add)
        rows = grad_parts.shape[3]
        for h in range(CORES):
            for m in range(nn):
                grad_parts[m, r, h] = grad_acc[pl.ds((h * nn + m) * rows, rows), :]

    relation_grad(0)
    reduce_step(half)
    ret_pair(half - 2)
    for r in range(1, rels):
        relation_grad(r)

    def y_copy(dn):
        return remote(
            grad_parts.at[(n + dn) % nn],
            grad_in.at[nn - dn],
            y_send.at[dn],
            y_recv.at[nn - dn],
            y_dev(dn),
        )

    for dn in range(1, nn):
        y_copy(dn).start()

    def reduce_pair(d):
        reduce_step(d)
        reduce_step(nz - d)
        ret_pair(d - 2)

    reduce_pair(half - 1)

    for dn in range(1, nn):
        y_copy(dn).wait_recv()
    rows = grad_parts.shape[3]
    for r in range(rels):
        for h in range(CORES):
            total = grad_parts[n, r, h]
            for dn in range(1, nn):
                total = total + grad_in[dn, r, h]
            grad_sum[r, h] = total.reshape(nx, group, width)

    def row_copy(p):
        xp, cp = peer(p)
        return remote(
            grad_sum.at[:, cp, xp], row_in.at[back(p)], row_send.at[p], row_recv.at[back(p)], row_dev(p)
        )

    for p in range(1, peers):
        row_copy(p).start()
    row_in[0] = grad_sum[:, c, x]

    load_bases_q.wait()

    def coef_sums(b):
        for r in range(rels):
            total = None
            for h in range(CORES):
                term = (grad_sum[r, h].reshape(rows, width) * bases_q[b, h].astype(F32)).sum(
                    axis=0, keepdims=True
                )
                total = term if total is None else total + term
            line = total[:, :128]
            for k in range(1, width // 128):
                line = line + total[:, k * 128 : (k + 1) * 128]
            coef_part[pl.ds(r * nb + b, 1), :] = line

    each(0, nb, coef_sums)

    def cp_copy(dn):
        return remote(
            coef_part, coef_recv.at[nn - dn], cp_send.at[dn], cp_recv.at[nn - dn], y_dev(dn)
        )

    for dn in range(1, nn):
        cp_copy(dn).start()

    if half > 2:
        reduce_pair(half - 2)

    for p in range(1, peers):
        row_copy(p).wait_recv()

    def basis_sums(b):
        total = jnp.zeros((group, width), F32)
        for p in range(peers):
            for r in range(rels):
                total = total + coefs[p, r, b] * row_in[p, r]
        basis_part[b % nz, b // nz] = total

    each(0, nb, basis_sums)

    def zb_copy(dz):
        return remote(
            basis_part.at[(z + dz) % nz],
            basis_in.at[nz - dz],
            zb_send.at[dz],
            zb_recv.at[nz - dz],
            z_dev(dz),
        )

    for dz in range(1, nz):
        zb_copy(dz).start()

    for d in range(half - 3, 0, -1):
        reduce_pair(d)

    for dz in range(1, nz):
        zb_copy(dz).wait_recv()
    total = basis_part[z]
    for dz in range(1, nz):
        total = total + basis_in[dz]
    basis_sum[...] = total

    def xb_copy(dx):
        return remote(
            basis_sum.at[(x + dx) % nx],
            basis_rows.at[x],
            xb_send.at[dx],
            xb_recv.at[nx - dx],
            row_dev(dx * CORES),
        )

    for dx in range(1, nx):
        xb_copy(dx).start()
    basis_rows[x] = basis_sum[x]

    rx_arrived(0)
    rs_copy(1, -1).wait_recv()
    rs_copy(nz - 1, 1).wait_recv()

    def finish(o):
        arrived = rb[0, o].astype(F32) + rb[half, o].astype(F32)
        out[o] = (self_term[o] + collect(0, o) + arrived).astype(BF16)

    each(0, owned, finish)

    for dx in range(1, nx):
        remote(
            basis_sum.at[0],
            basis_rows.at[(x + dx) % nx],
            xb_send.at[dx],
            xb_recv.at[dx],
            row_dev(dx * CORES),
        ).wait_recv()
    out_basis[...] = basis_rows[...]

    for dn in range(1, nn):
        cp_copy(dn).wait_recv()
    total = coef_part[...]
    for dn in range(1, nn):
        total = total + coef_recv[dn]
    column = total.sum(axis=1, keepdims=True)
    wide_shape = (rels * nb, rels * nb)
    diagonal = lax.broadcasted_iota(jnp.int32, wide_shape, 0) == lax.broadcasted_iota(
        jnp.int32, wide_shape, 1
    )
    line = jnp.where(diagonal, jnp.broadcast_to(column, wide_shape), 0.0).sum(axis=0, keepdims=True)
    for r in range(rels):
        out_coef[r : r + 1, :] = line[:, r * nb : (r + 1) * nb]

    z_done(zc)
    each(1, peers, lambda p: x_copy(0, ffeat, 0, p).wait_send())
    for j in range(nz):
        each(1, peers, lambda p, j=j: x_copy(1, fcot, j, p).wait_send())
        each(1, peers, lambda p, j=j: ret_copy(j, p).wait_send())
    for j in range(1, half + 1):
        rs_copy(j, -1).wait_send()
        rs_copy(nz - j, 1).wait_send()
    for p in range(1, peers):
        for copy in small(p):
            copy.wait_send()
        row_copy(p).wait_send()
    for dn in range(1, nn):
        y_copy(dn).wait_send()
        cp_copy(dn).wait_send()
    for dz in range(1, nz):
        zb_copy(dz).wait_send()
    for dx in range(1, nx):
        xb_copy(dx).wait_send()


def keep_kernel(a, b, c, a_out, b_out, c_out):
    a_out[...] = a[...]
    b_out[...] = b[...]
    c_out[...] = c[...]


def per_device(
    nx, nz, nn, features, cotangent, self_weight, bases, basis_coef, block_values, block_slots, fetch_ids
):
    rels, blocks, block, _ = block_values.shape
    width = features.shape[1]
    slots = fetch_ids.shape[0]
    owned = features.shape[0] // block
    nb = bases.shape[0]
    peers = nx * CORES
    rows = width // (CORES * nn)
    group = rows // nx

    vmem = pl.BlockSpec(memory_space=pltpu.VMEM)
    anywhere = pl.BlockSpec(memory_space=pl.ANY)
    dma = pltpu.SemaphoreType.DMA
    output, basis_grad, coef_grad = pl.pallas_call(
        functools.partial(layer_kernel, nx, nz, nn),
        out_shape=(
            jax.ShapeDtypeStruct((owned, block, width), BF16),
            jax.ShapeDtypeStruct((nx, group, width), F32),
            jax.ShapeDtypeStruct((rels, nb), F32),
        ),
        in_specs=[vmem, vmem, vmem, vmem, vmem, vmem, anywhere, anywhere, anywhere],
        out_specs=(vmem, vmem, vmem),
        scratch_shapes=[
            pltpu.VMEM((3 * rels, 1, 128), jnp.int32),
            pltpu.VMEM((peers, 1, 128), jnp.int32),
            pltpu.VMEM((peers, rels, 128), F32),
            pltpu.SMEM((3 * rels, 1, 128), jnp.int32),
            pltpu.SMEM((peers, 1, 128), jnp.int32),
            pltpu.SMEM((peers, rels, 128), F32),
            pltpu.VMEM((nz, owned, block, width), BF16),
            pltpu.VMEM((nz, owned, block, width), BF16),
            pltpu.VMEM((owned, block, width), BF16),
            pltpu.VMEM((nz + 1, peers, block, width), BF16),
            pltpu.VMEM((slots, block, width), BF16),
            pltpu.VMEM((slots, block, width), BF16),
            pltpu.VMEM((rels, blocks, block, block), BF16),
            pltpu.VMEM((blocks, block, width), F32),
            pltpu.VMEM((rels, slots, block, width), BF16),
            pltpu.VMEM((rels, width, width), BF16),
            pltpu.VMEM((owned, block, width), F32),
            pltpu.VMEM((nz, peers, block, width), BF16),
            pltpu.VMEM((nz, owned, block, width), BF16),
            pltpu.VMEM((width, width), F32),
            pltpu.VMEM((nn, rels, CORES, rows, width), F32),
            pltpu.VMEM((nn, rels, CORES, rows, width), F32),
            pltpu.VMEM((rels, CORES, nx, group, width), F32),
            pltpu.VMEM((nb, CORES, rows, width), BF16),
            pltpu.VMEM((rels * nb, 128), F32),
            pltpu.VMEM((nn, rels * nb, 128), F32),
            pltpu.VMEM((peers, rels, group, width), F32),
            pltpu.VMEM((nz, nx, group, width), F32),
            pltpu.VMEM((nz, nx, group, width), F32),
            pltpu.VMEM((nx, group, width), F32),
            pltpu.VMEM((nx, group, width), F32),
            dma((6,)),
            dma((peers,)),
            dma((peers,)),
            dma((peers,)),
            dma((peers,)),
            dma((2, nz)),
            dma((2, nz)),
            dma((2, nz, peers)),
            dma((2, slots)),
            dma((nz, peers)),
            dma((nz, peers)),
            dma((nz,)),
            dma((nz,)),
            dma((nn,)),
            dma((nn,)),
            dma((nn,)),
            dma((nn,)),
            dma((peers,)),
            dma((peers,)),
            dma((nz,)),
            dma((nz,)),
            dma((nx,)),
            dma((nx,)),
        ],
        compiler_params=pltpu.CompilerParams(
            collective_id=0, has_side_effects=True, vmem_limit_bytes=62 * 1024 * 1024
        ),
    )(
        block_slots.transpose(0, 2, 1),
        fetch_ids.reshape(1, slots),
        basis_coef,
        features.reshape(owned, block, width),
        cotangent.reshape(owned, block, width),
        self_weight,
        bases.reshape(nb * width // block, block, width),
        bases.reshape(nb, CORES, nn, rows, width),
        block_values,
    )
    output, basis_grad, coef_grad = pl.pallas_call(
        keep_kernel,
        out_shape=tuple(jax.ShapeDtypeStruct(a.shape, a.dtype) for a in (output, basis_grad, coef_grad)),
        in_specs=[vmem] * 3,
        out_specs=(vmem,) * 3,
    )(output, basis_grad, coef_grad)
    return (
        output.reshape(owned * block, width),
        basis_grad.reshape(rows, width),
        coef_grad,
    )


def solution(mesh, nx=4):
    nz = mesh.shape["wide"] // (CORES * nx)
    return jax.shard_map(
        functools.partial(per_device, nx, nz, mesh.shape["narrow"]),
        mesh=mesh,
        in_specs=(
            P(("wide", "narrow"), None),
            P(("wide", "narrow"), None),
            P(),
            P(),
            P("wide", None),
            P("wide", "narrow", None, None),
            P("wide", "narrow", None),
            P(("wide", "narrow")),
        ),
        out_specs=(P(("wide", "narrow"), None), P(("wide", "narrow"), None), P("wide", None)),
        check_vma=False,
    )
```

```python
import functools

import jax
import jax.numpy as jnp
from jax import lax
from jax.experimental import pallas as pl
from jax.experimental.pallas import tpu as pltpu
from jax.sharding import PartitionSpec as P

MESH = pl.DeviceIdType.MESH
F32 = jnp.float32
BF16 = jnp.bfloat16
CORES = 2


def layer_kernel(
    nx,
    nz,
    nn,
    block_slots,
    ids_in,
    coef_in,
    feat,
    cot,
    selfw,
    bases_flat,
    bases_split,
    values_hbm,
    out,
    out_basis,
    out_coef,
    meta_v,
    ids_v,
    coef_v,
    meta,
    ids,
    coefs,
    zfeat,
    zcot,
    picked,
    stage,
    ffeat,
    fcot,
    values,
    running,
    slot_g,
    weights,
    self_term,
    rx,
    rb,
    grad_acc,
    grad_parts,
    grad_in,
    grad_sum,
    bases_q,
    coef_part,
    coef_recv,
    row_in,
    basis_part,
    basis_in,
    basis_sum,
    basis_rows,
    local_sem,
    id_send,
    id_recv,
    coef_send,
    coef_recv_sem,
    z_send,
    z_recv,
    x_send,
    x_recv,
    ret_send,
    ret_recv,
    rs_send,
    rs_recv,
    y_send,
    y_recv,
    cp_send,
    cp_recv,
    row_send,
    row_recv,
    zb_send,
    zb_recv,
    xb_send,
    xb_recv,
):
    w = lax.axis_index("wide")
    n = lax.axis_index("narrow")
    x, z, c = w // (CORES * nz), (w // CORES) % nz, w % CORES
    peers = nx * CORES
    owned, block, width = feat.shape
    slots = ffeat.shape[0]
    rels = slot_g.shape[0]
    blocks = values.shape[1]
    nb = basis_part.shape[0] * basis_part.shape[1]
    group = grad_sum.shape[3]
    half = nz // 2
    cut = owned // 2

    def slot(xs, zs, cs):
        return (xs * nz + zs) * CORES + cs

    def peer(p):
        return (x + p // CORES) % nx, (c + p % CORES) % CORES

    def row_dev(p):
        xp, cp = peer(p)
        return (slot(xp, z, cp), n)

    def back(p):
        return ((nx - p // CORES) % nx) * CORES + p % CORES

    def z_dev(dz):
        return (slot(x, (z + dz + nz) % nz, c), n)

    def y_dev(dn):
        return (w, (n + dn) % nn)

    def remote(src, dst, ssem, rsem, dev):
        return pltpu.make_async_remote_copy(
            src_ref=src, dst_ref=dst, send_sem=ssem, recv_sem=rsem, device_id=dev, device_id_type=MESH
        )

    def each_peer(body):
        if nx == 4:

            def some(i):
                q = i % 3
                body((1 + 2 * q - 3 * (q // 2)) * CORES + i // 3)

            each(0, 3 * CORES, some)
            body(1)
        else:
            each(1, peers, body)

    def each(lo, hi, body):
        def step(i, carry):
            body(i)
            return carry

        lax.fori_loop(lo, hi, step, 0)

    load_bases = pltpu.make_async_copy(bases_flat, slot_g.at[1], local_sem.at[0])
    load_values = pltpu.make_async_copy(values_hbm, values, local_sem.at[1])
    load_bases_q = pltpu.make_async_copy(bases_split.at[:, :, n], bases_q, local_sem.at[2])
    load_bases.start()
    load_values.start()
    load_bases_q.start()

    barrier = pltpu.get_barrier_semaphore()
    for p in range(1, peers):
        pl.semaphore_signal(barrier, inc=1, device_id=row_dev(p), device_id_type=MESH)
    for dz in range(1, nz):
        pl.semaphore_signal(barrier, inc=1, device_id=z_dev(dz), device_id_type=MESH)
    for dn in range(1, nn):
        pl.semaphore_signal(barrier, inc=1, device_id=y_dev(dn), device_id_type=MESH)
    pl.semaphore_wait(barrier, peers + nz + nn - 3)

    def z_copy(which, own, buf, to, way):
        frm = to - 1 if way > 0 else (to + 1) % nz
        src = own if frm == 0 else buf.at[frm]
        dst = buf.at[to]
        sem = to
        if to == half:
            part = pl.ds(0, cut) if way > 0 else pl.ds(cut, cut)
            src, dst = src.at[part], dst.at[part]
            sem = half if way > 0 else 0
        return remote(src, dst, z_send.at[which, sem], z_recv.at[which, sem], z_dev(way))

    zf = functools.partial(z_copy, 0, feat, zfeat)
    zc = functools.partial(z_copy, 1, cot, zcot)

    def z_first(zcp):
        zcp(1, 1).start()
        zcp(nz - 1, -1).start()

    def z_step(zcp, d):
        if d < half:
            zcp(d, 1).wait_recv()
            zcp(d + 1, 1).start()
            zcp(nz - d, -1).wait_recv()
            zcp(nz - d - 1, -1).start()
        else:
            zcp(half, 1).wait_recv()
            zcp(half, -1).wait_recv()

    def z_done(zcp):
        for d in range(1, half + 1):
            zcp(d, 1).wait_send()
            zcp(nz - d, -1).wait_send()

    def x_copy(which, dst, j, p):
        at = nz if which == 1 and j == 0 else j
        s = slot(x, (z - j + nz) % nz, c)
        return remote(
            stage.at[at, p], dst.at[s], x_send.at[which, j, p], x_recv.at[which, s], row_dev(p)
        )

    def x_step(which, own, buf, dst, j):
        src = own
        if j > 0:
            picked[...] = buf[j]
            src = picked
        at = nz if which == 1 and j == 0 else j
        s = slot(x, (z - j + nz) % nz, c)
        if which == 1 and j > 0:
            each(1, peers, lambda p: x_copy(0, ffeat, j, p).wait_send())

        def send(p):
            stage[at, p] = src[ids[p, 0, s]]
            x_copy(which, dst, j, p).start()

        each_peer(send)
        dst[s] = src[ids[0, 0, s]]

    xf = functools.partial(x_step, 0, feat, zfeat, ffeat)
    xc = functools.partial(x_step, 1, cot, zcot, fcot)

    def x_arrived(which, dst, j):
        def arrived(p):
            xp, cp = peer(p)
            s = slot(xp, (z - j + nz) % nz, cp)
            remote(
                stage.at[0, 0], dst.at[s], x_send.at[which, 0, 0], x_recv.at[which, s], row_dev(p)
            ).wait_recv()

        each(1, peers, arrived)

    z_first(zf)
    ids_v[0] = jnp.zeros_like(ids_v[0])
    ids_v[0, :, :slots] = ids_in[...]
    coef_v[0] = jnp.zeros_like(coef_v[0])
    coef_v[0, :, :nb] = coef_in[...].astype(F32)

    def small(p):
        return (
            remote(ids_v.at[0], ids_v.at[back(p)], id_send.at[p], id_recv.at[back(p)], row_dev(p)),
            remote(
                coef_v.at[0], coef_v.at[back(p)], coef_send.at[p], coef_recv_sem.at[back(p)], row_dev(p)
            ),
        )

    for p in range(1, peers):
        for copy in small(p):
            copy.start()

    own_coef_down = pltpu.make_async_copy(coef_v.at[0], coefs.at[0], local_sem.at[4])
    own_coef_down.start()

    meta_v[...] = jnp.zeros_like(meta_v)
    down = lax.broadcasted_iota(jnp.int32, (blocks, blocks), 0)
    across = lax.broadcasted_iota(jnp.int32, (blocks, blocks), 1)
    down_slot = lax.broadcasted_iota(jnp.int32, (blocks, slots), 0)
    across_slot = lax.broadcasted_iota(jnp.int32, (blocks, slots), 1)
    for r in range(rels):
        row = block_slots[r, 0:1, :]
        spread = jnp.broadcast_to(row, (blocks, blocks))
        column = jnp.max(jnp.where(down == across, spread, -1), axis=1, keepdims=True)
        same = (column == spread) & (down < across)
        meta_v[r, :, :blocks] = block_slots[r, 1:2, :]
        meta_v[rels + r, :, :blocks] = jnp.max(jnp.where(same, down, -1), axis=0, keepdims=True)
        meta_v[2 * rels + r, :, :slots] = jnp.max(
            jnp.where(column == across_slot, down_slot, -1), axis=0, keepdims=True
        )
    meta_down = pltpu.make_async_copy(meta_v, meta, local_sem.at[5])
    meta_down.start()
    meta_down.wait()
    own_coef_down.wait()

    for p in range(1, peers):
        for copy in small(p):
            copy.wait_recv()
    ids_down = pltpu.make_async_copy(ids_v, ids, local_sem.at[3])
    coef_down = pltpu.make_async_copy(
        coef_v.at[pl.ds(1, peers - 1)], coefs.at[pl.ds(1, peers - 1)], local_sem.at[4]
    )
    ids_down.start()
    coef_down.start()
    ids_down.wait()
    coef_down.wait()

    xf(0)
    xc(0)

    load_bases.wait()
    tile = 16
    per = block // tile
    parts = width // block

    def weigh(t):
        hb = t // per
        row = pl.multiple_of((t % per) * tile, tile)
        acc = [jnp.zeros((tile, width), F32) for _ in range(rels)]
        for b in range(nb):
            v = slot_g[1, b * parts + hb, pl.ds(row, tile), :].astype(F32)
            for r in range(rels):
                acc[r] = acc[r] + coefs[0, r, b] * v
        for r in range(rels):
            weights[r, pl.ds(pl.multiple_of(hb * block + row, tile), tile), :] = acc[r].astype(BF16)

    each(0, parts * per, weigh)

    def own_term(o):
        self_term[o] = jnp.dot(feat[o], selfw[...], preferred_element_type=F32)

    each(0, owned, own_term)

    for d in range(1, half):
        z_step(zf, d)
        if d == half - 1:
            z_first(zc)
        xf(d)
        xf(nz - d)
    z_step(zf, half)
    xf(half)

    z_step(zc, 1)
    xc(1)
    xc(nz - 1)
    load_values.wait()
    for j in range(nz):
        x_arrived(0, ffeat, j)

    burst = 4

    def messages(r):
        def some(q):
            found = []
            for u in range(burst):
                j = q * burst + u
                found.append(
                    jnp.dot(values[r, j], ffeat[meta[r, 0, j]], preferred_element_type=F32).astype(BF16)
                )
            for u in range(burst):
                j = q * burst + u
                before = meta[rels + r, 0, j]
                earlier = running[jnp.maximum(before, 0)]
                running[j] = jnp.where(before >= 0, earlier, 0.0) + found[u].astype(F32)

        each(0, blocks // burst, some)

        def pick(s):
            at = meta[2 * rels + r, 0, s]
            slot_g[r, s] = jnp.where(at >= 0, running[jnp.maximum(at, 0)], 0.0).astype(BF16)

        each(0, slots, pick)

    messages(0)
    for d in range(2, half - 1):
        z_step(zc, d)
        xc(d)
        xc(nz - d)
    messages(1)
    if half > 2:
        z_step(zc, half - 1)
    z_done(zf)
    slot_sums = zfeat

    def sum_slots(m):
        rows = (owned * block, width)
        at = pl.ds(m * owned, owned)
        total = jnp.dot(slot_g[0, at].reshape(rows), weights[0], preferred_element_type=F32)
        for r in range(1, rels):
            total += jnp.dot(slot_g[r, at].reshape(rows), weights[r], preferred_element_type=F32)
        slot_sums[m] = total.astype(BF16).reshape(owned, block, width)

    each(0, nz, sum_slots)

    def ret_copy(j, p):
        xp, cp = peer(p)
        s = slot(xp, (z - j + nz) % nz, cp)
        return remote(
            slot_sums.at[s // owned, s % owned],
            rx.at[j, back(p)],
            ret_send.at[j, p],
            ret_recv.at[j, back(p)],
            row_dev(p),
        )

    def ret_go(j):
        each_peer(lambda p: ret_copy(j, p).start())

    def ret_pair(d):
        if d > 0:
            ret_go(d)
            ret_go(nz - d)
        elif d == 0:
            ret_go(0)

    ret_go(half)
    ret_pair(half - 1)

    def grads(*chunks):
        for j in chunks:
            x_arrived(1, fcot, j)
            zo = (z - j + nz) % nz

            def add(r):
                total = None
                for xs in range(nx):
                    at = pl.ds(slot(xs, zo, 0), CORES)
                    rows = (CORES * block, width)
                    term = lax.dot_general(
                        slot_g[r, at].reshape(rows),
                        fcot[at].reshape(rows),
                        (((0,), (0,)), ((), ())),
                        preferred_element_type=F32,
                    )
                    total = term if total is None else total + term
                grad_acc[r] = total if j == 0 else grad_acc[r] + total

            each(0, rels, add)

    if half > 2:
        grads(0, 1, nz - 1)
    else:
        grads(0)

    def rs_copy(j, way):
        to = j - 1 if way < 0 else (j + 1) % nz
        at = half if way > 0 and to == 0 else to
        src, dst = ffeat.at[pl.ds(j * owned, owned)], rb.at[at]
        if j == half:
            first = 0 if way < 0 else cut
            src, dst = ffeat.at[pl.ds(j * owned + first, cut)], rb.at[at, pl.ds(first, cut)]
        return remote(src, dst, rs_send.at[at], rs_recv.at[at], z_dev(way))

    def collect(j, o):
        s = slot(x, (z - j + nz) % nz, c)
        total = None
        for p in range(peers):
            weight = jnp.where(ids[p, 0, s] == o, 1.0, 0.0).astype(F32)
            term = (slot_sums[s // owned, s % owned] if p == 0 else rx[j, p]).astype(F32) * weight
            total = term if total is None else total + term
        return total

    def rx_arrived(j):
        each(
            1,
            peers,
            lambda p: remote(
                stage.at[0, 0], rx.at[j, p], ret_send.at[j, 0], ret_recv.at[j, p], row_dev(p)
            ).wait_recv(),
        )

    def reduce_step(j):
        rx_arrived(j)
        lo, hi = 0, 0
        if 0 < j < half:
            rs_copy(j + 1, -1).wait_recv()
            lo, hi = 0, (cut if j + 1 == half else owned)
        elif j > half:
            rs_copy(j - 1, 1).wait_recv()
            lo, hi = (cut if j - 1 == half else 0), owned

        def plain(o):
            ffeat[j * owned + o] = collect(j, o).astype(BF16)

        def more(o):
            ffeat[j * owned + o] = (collect(j, o) + rb[j, o].astype(F32)).astype(BF16)

        if lo > 0:
            each(0, lo, plain)
        if hi > lo:
            each(lo, hi, more)
        if hi < owned:
            each(hi, owned, plain)
        if j <= half:
            rs_copy(j, -1).start()
        if j >= half:
            rs_copy(j, 1).start()

    def reduce_pair(d):
        reduce_step(d)
        reduce_step(nz - d)

    reduce_step(half)
    if half > 2:
        xc(half - 1)
        xc(half + 1)
    ret_pair(half - 2)
    z_step(zc, half)
    xc(half)
    for d in range(2, half - 1):
        grads(d, nz - d)
    if half > 2:
        reduce_pair(half - 1)
        ret_pair(half - 3)
    grads(half - 1, half + 1)
    for d in range(half - 2, 1, -1):
        reduce_pair(d)
        ret_pair(d - 2)
    grads(half)
    rows = grad_parts.shape[3]
    for r in range(rels):
        for h in range(CORES):
            for m in range(nn):
                grad_parts[m, r, h] = grad_acc[r, pl.ds((h * nn + m) * rows, rows), :]

    def y_copy(dn):
        return remote(
            grad_parts.at[(n + dn) % nn],
            grad_in.at[nn - dn],
            y_send.at[dn],
            y_recv.at[nn - dn],
            y_dev(dn),
        )

    for dn in range(1, nn):
        y_copy(dn).start()

    for dn in range(1, nn):
        y_copy(dn).wait_recv()
    for r in range(rels):
        for h in range(CORES):
            total = grad_parts[n, r, h]
            for dn in range(1, nn):
                total = total + grad_in[dn, r, h]
            grad_sum[r, h] = total.reshape(nx, group, width)

    def row_copy(p):
        xp, cp = peer(p)
        return remote(
            grad_sum.at[:, cp, xp], row_in.at[back(p)], row_send.at[p], row_recv.at[back(p)], row_dev(p)
        )

    for p in range(1, peers):
        row_copy(p).start()
    row_in[0] = grad_sum[:, c, x]

    load_bases_q.wait()

    def coef_sums(b):
        for r in range(rels):
            total = None
            for h in range(CORES):
                term = (grad_sum[r, h].reshape(rows, width) * bases_q[b, h].astype(F32)).sum(
                    axis=0, keepdims=True
                )
                total = term if total is None else total + term
            line = total[:, :128]
            for k in range(1, width // 128):
                line = line + total[:, k * 128 : (k + 1) * 128]
            coef_part[pl.ds(r * nb + b, 1), :] = line

    each(0, nb, coef_sums)

    def cp_copy(dn):
        return remote(
            coef_part, coef_recv.at[nn - dn], cp_send.at[dn], cp_recv.at[nn - dn], y_dev(dn)
        )

    for dn in range(1, nn):
        cp_copy(dn).start()

    for p in range(1, peers):
        row_copy(p).wait_recv()

    def basis_sums(b):
        total = jnp.zeros((group, width), F32)
        for p in range(peers):
            for r in range(rels):
                total = total + coefs[p, r, b] * row_in[p, r]
        basis_part[b % nz, b // nz] = total

    each(0, nb, basis_sums)

    def zb_copy(dz):
        return remote(
            basis_part.at[(z + dz) % nz],
            basis_in.at[nz - dz],
            zb_send.at[dz],
            zb_recv.at[nz - dz],
            z_dev(dz),
        )

    for dz in range(1, nz):
        zb_copy(dz).start()

    reduce_pair(1)

    for dz in range(1, nz):
        zb_copy(dz).wait_recv()
    total = basis_part[z]
    for dz in range(1, nz):
        total = total + basis_in[dz]
    basis_sum[...] = total

    def xb_copy(dx):
        return remote(
            basis_sum.at[(x + dx) % nx],
            basis_rows.at[x],
            xb_send.at[dx],
            xb_recv.at[nx - dx],
            row_dev(dx * CORES),
        )

    for dx in range(1, nx):
        xb_copy(dx).start()
    basis_rows[x] = basis_sum[x]

    rx_arrived(0)
    rs_copy(1, -1).wait_recv()
    rs_copy(nz - 1, 1).wait_recv()

    def finish(o):
        arrived = rb[0, o].astype(F32) + rb[half, o].astype(F32)
        out[o] = (self_term[o] + collect(0, o) + arrived).astype(BF16)

    each(0, owned, finish)

    for dx in range(1, nx):
        remote(
            basis_sum.at[0],
            basis_rows.at[(x + dx) % nx],
            xb_send.at[dx],
            xb_recv.at[dx],
            row_dev(dx * CORES),
        ).wait_recv()
    out_basis[...] = basis_rows[...]

    for dn in range(1, nn):
        cp_copy(dn).wait_recv()
    total = coef_part[...]
    for dn in range(1, nn):
        total = total + coef_recv[dn]
    column = total.sum(axis=1, keepdims=True)
    wide_shape = (rels * nb, rels * nb)
    diagonal = lax.broadcasted_iota(jnp.int32, wide_shape, 0) == lax.broadcasted_iota(
        jnp.int32, wide_shape, 1
    )
    line = jnp.where(diagonal, jnp.broadcast_to(column, wide_shape), 0.0).sum(axis=0, keepdims=True)
    for r in range(rels):
        out_coef[r : r + 1, :] = line[:, r * nb : (r + 1) * nb]

    z_done(zc)
    each(1, peers, lambda p: x_copy(0, ffeat, 0, p).wait_send())
    for j in range(nz):
        each(1, peers, lambda p, j=j: x_copy(1, fcot, j, p).wait_send())
        each(1, peers, lambda p, j=j: ret_copy(j, p).wait_send())
    for j in range(1, half + 1):
        rs_copy(j, -1).wait_send()
        rs_copy(nz - j, 1).wait_send()
    for p in range(1, peers):
        for copy in small(p):
            copy.wait_send()
        row_copy(p).wait_send()
    for dn in range(1, nn):
        y_copy(dn).wait_send()
        cp_copy(dn).wait_send()
    for dz in range(1, nz):
        zb_copy(dz).wait_send()
    for dx in range(1, nx):
        xb_copy(dx).wait_send()


def keep_kernel(a, b, c, a_out, b_out, c_out):
    a_out[...] = a[...]
    b_out[...] = b[...]
    c_out[...] = c[...]


def per_device(
    nx, nz, nn, features, cotangent, self_weight, bases, basis_coef, block_values, block_slots, fetch_ids
):
    rels, blocks, block, _ = block_values.shape
    width = features.shape[1]
    slots = fetch_ids.shape[0]
    owned = features.shape[0] // block
    nb = bases.shape[0]
    peers = nx * CORES
    rows = width // (CORES * nn)
    group = rows // nx

    vmem = pl.BlockSpec(memory_space=pltpu.VMEM)
    anywhere = pl.BlockSpec(memory_space=pl.ANY)
    dma = pltpu.SemaphoreType.DMA
    output, basis_grad, coef_grad = pl.pallas_call(
        functools.partial(layer_kernel, nx, nz, nn),
        out_shape=(
            jax.ShapeDtypeStruct((owned, block, width), BF16),
            jax.ShapeDtypeStruct((nx, group, width), F32),
            jax.ShapeDtypeStruct((rels, nb), F32),
        ),
        in_specs=[vmem, vmem, vmem, vmem, vmem, vmem, anywhere, anywhere, anywhere],
        out_specs=(vmem, vmem, vmem),
        scratch_shapes=[
            pltpu.VMEM((3 * rels, 1, 128), jnp.int32),
            pltpu.VMEM((peers, 1, 128), jnp.int32),
            pltpu.VMEM((peers, rels, 128), F32),
            pltpu.SMEM((3 * rels, 1, 128), jnp.int32),
            pltpu.SMEM((peers, 1, 128), jnp.int32),
            pltpu.SMEM((peers, rels, 128), F32),
            pltpu.VMEM((nz, owned, block, width), BF16),
            pltpu.VMEM((nz, owned, block, width), BF16),
            pltpu.VMEM((owned, block, width), BF16),
            pltpu.VMEM((nz + 1, peers, block, width), BF16),
            pltpu.VMEM((slots, block, width), BF16),
            pltpu.VMEM((slots, block, width), BF16),
            pltpu.VMEM((rels, blocks, block, block), BF16),
            pltpu.VMEM((blocks, block, width), F32),
            pltpu.VMEM((rels, slots, block, width), BF16),
            pltpu.VMEM((rels, width, width), BF16),
            pltpu.VMEM((owned, block, width), F32),
            pltpu.VMEM((nz, peers, block, width), BF16),
            pltpu.VMEM((nz, owned, block, width), BF16),
            pltpu.VMEM((rels, width, width), F32),
            pltpu.VMEM((nn, rels, CORES, rows, width), F32),
            pltpu.VMEM((nn, rels, CORES, rows, width), F32),
            pltpu.VMEM((rels, CORES, nx, group, width), F32),
            pltpu.VMEM((nb, CORES, rows, width), BF16),
            pltpu.VMEM((rels * nb, 128), F32),
            pltpu.VMEM((nn, rels * nb, 128), F32),
            pltpu.VMEM((peers, rels, group, width), F32),
            pltpu.VMEM((nz, nx, group, width), F32),
            pltpu.VMEM((nz, nx, group, width), F32),
            pltpu.VMEM((nx, group, width), F32),
            pltpu.VMEM((nx, group, width), F32),
            dma((6,)),
            dma((peers,)),
            dma((peers,)),
            dma((peers,)),
            dma((peers,)),
            dma((2, nz)),
            dma((2, nz)),
            dma((2, nz, peers)),
            dma((2, slots)),
            dma((nz, peers)),
            dma((nz, peers)),
            dma((nz,)),
            dma((nz,)),
            dma((nn,)),
            dma((nn,)),
            dma((nn,)),
            dma((nn,)),
            dma((peers,)),
            dma((peers,)),
            dma((nz,)),
            dma((nz,)),
            dma((nx,)),
            dma((nx,)),
        ],
        compiler_params=pltpu.CompilerParams(
            collective_id=0, has_side_effects=True, vmem_limit_bytes=62 * 1024 * 1024
        ),
    )(
        block_slots.transpose(0, 2, 1),
        fetch_ids.reshape(1, slots),
        basis_coef,
        features.reshape(owned, block, width),
        cotangent.reshape(owned, block, width),
        self_weight,
        bases.reshape(nb * width // block, block, width),
        bases.reshape(nb, CORES, nn, rows, width),
        block_values,
    )
    output, basis_grad, coef_grad = pl.pallas_call(
        keep_kernel,
        out_shape=tuple(jax.ShapeDtypeStruct(a.shape, a.dtype) for a in (output, basis_grad, coef_grad)),
        in_specs=[vmem] * 3,
        out_specs=(vmem,) * 3,
    )(output, basis_grad, coef_grad)
    return (
        output.reshape(owned * block, width),
        basis_grad.reshape(rows, width),
        coef_grad,
    )


def solution(mesh, nx=4):
    nz = mesh.shape["wide"] // (CORES * nx)
    return jax.shard_map(
        functools.partial(per_device, nx, nz, mesh.shape["narrow"]),
        mesh=mesh,
        in_specs=(
            P(("wide", "narrow"), None),
            P(("wide", "narrow"), None),
            P(),
            P(),
            P("wide", None),
            P("wide", "narrow", None, None),
            P("wide", "narrow", None),
            P(("wide", "narrow")),
        ),
        out_specs=(P(("wide", "narrow"), None), P(("wide", "narrow"), None), P("wide", None)),
        check_vma=False,
    )
```

```python
import functools

import jax
import jax.numpy as jnp
from jax import lax
from jax.experimental import pallas as pl
from jax.experimental.pallas import tpu as pltpu
from jax.sharding import PartitionSpec as P

MESH = pl.DeviceIdType.MESH
F32 = jnp.float32
BF16 = jnp.bfloat16
CORES = 2


def layer_kernel(
    nx,
    nz,
    nn,
    block_slots,
    ids_in,
    coef_in,
    feat,
    cot,
    selfw,
    bases_flat,
    bases_split,
    values_hbm,
    out,
    out_basis,
    out_coef,
    meta_v,
    ids_v,
    coef_v,
    meta,
    ids,
    coefs,
    zfeat,
    zcot,
    picked,
    stage,
    ffeat,
    fcot,
    values,
    running,
    slot_g,
    weights,
    self_term,
    rx,
    rb,
    grad_acc,
    grad_parts,
    grad_in,
    grad_sum,
    bases_q,
    coef_part,
    coef_recv,
    row_in,
    basis_part,
    basis_in,
    basis_sum,
    basis_rows,
    local_sem,
    id_send,
    id_recv,
    coef_send,
    coef_recv_sem,
    z_send,
    z_recv,
    x_send,
    x_recv,
    ret_send,
    ret_recv,
    rs_send,
    rs_recv,
    y_send,
    y_recv,
    cp_send,
    cp_recv,
    row_send,
    row_recv,
    zb_send,
    zb_recv,
    xb_send,
    xb_recv,
):
    w = lax.axis_index("wide")
    n = lax.axis_index("narrow")
    x, z, c = w // (CORES * nz), (w // CORES) % nz, w % CORES
    peers = nx * CORES
    owned, block, width = feat.shape
    slots = ffeat.shape[0]
    rels = slot_g.shape[0]
    blocks = values.shape[1]
    nb = basis_part.shape[0] * basis_part.shape[1]
    group = grad_sum.shape[3]
    half = nz // 2
    cut = owned // 2

    zs = [(z + nz - j) % nz for j in range(nz)]
    along = [
        ((x + p // CORES) % nx) * (nz * CORES) + (c + p % CORES) % CORES for p in range(peers)
    ]

    def slot(p, j):
        return along[p] + zs[j] * CORES

    def row_dev(p):
        return (along[p] + z * CORES, n)

    def back(p):
        return ((nx - p // CORES) % nx) * CORES + p % CORES

    def z_dev(dz):
        return (along[0] + zs[(nz - dz) % nz] * CORES, n)

    def y_dev(dn):
        return (w, (n + dn) % nn)

    def remote(src, dst, ssem, rsem, dev):
        return pltpu.make_async_remote_copy(
            src_ref=src, dst_ref=dst, send_sem=ssem, recv_sem=rsem, device_id=dev, device_id_type=MESH
        )

    def sent(block_ref, sem):
        remote(block_ref, block_ref, sem, sem, row_dev(1)).wait_send()

    def landed(block_ref, sem):
        remote(block_ref, block_ref, sem, sem, row_dev(1)).wait_recv()

    def each(lo, hi, body):
        def step(i, carry):
            body(i)
            return carry

        lax.fori_loop(lo, hi, step, 0)

    load_bases = pltpu.make_async_copy(bases_flat, slot_g.at[1], local_sem.at[0])
    load_values = pltpu.make_async_copy(values_hbm, values, local_sem.at[1])
    load_bases_q = pltpu.make_async_copy(bases_split.at[:, :, n], bases_q, local_sem.at[2])
    load_bases.start()
    load_values.start()
    load_bases_q.start()

    barrier = pltpu.get_barrier_semaphore()
    for p in range(1, peers):
        pl.semaphore_signal(barrier, inc=1, device_id=row_dev(p), device_id_type=MESH)
    for dz in range(1, nz):
        pl.semaphore_signal(barrier, inc=1, device_id=z_dev(dz), device_id_type=MESH)
    for dn in range(1, nn):
        pl.semaphore_signal(barrier, inc=1, device_id=y_dev(dn), device_id_type=MESH)
    pl.semaphore_wait(barrier, peers + nz + nn - 3)

    def z_copy(which, own, buf, to, way):
        frm = to - 1 if way > 0 else (to + 1) % nz
        src = own if frm == 0 else buf.at[frm]
        dst = buf.at[to]
        sem = to
        if to == half:
            part = pl.ds(0, cut) if way > 0 else pl.ds(cut, cut)
            src, dst = src.at[part], dst.at[part]
            sem = half if way > 0 else 0
        return remote(src, dst, z_send.at[which, sem], z_recv.at[which, sem], z_dev(way))

    zf = functools.partial(z_copy, 0, feat, zfeat)
    zc = functools.partial(z_copy, 1, cot, zcot)

    def z_first(zcp):
        zcp(1, 1).start()
        zcp(nz - 1, -1).start()

    def z_step(zcp, d):
        if d < half:
            zcp(d, 1).wait_recv()
            zcp(d + 1, 1).start()
            zcp(nz - d, -1).wait_recv()
            zcp(nz - d - 1, -1).start()
        else:
            zcp(half, 1).wait_recv()
            zcp(half, -1).wait_recv()

    def z_done(zcp):
        for d in range(1, half + 1):
            zcp(d, 1).wait_send()
            zcp(nz - d, -1).wait_send()

    others = pl.ds(1, peers - 1)

    def x_step(which, own, buf, dst, j):
        src = own
        if j > 0:
            picked[...] = buf[j]
            src = picked
        at = nz if which == 1 and j == 0 else j
        s = slot(0, j)
        if which == 1 and j > 0:
            sent(stage.at[0, others], x_send.at[0, j])
        for p in range(1, peers):
            stage[at, p] = src[ids[p, 0, s]]
            remote(
                stage.at[at, p], dst.at[s], x_send.at[which, j], x_recv.at[which], row_dev(p)
            ).start()
        dst[s] = src[ids[0, 0, s]]

    xf = functools.partial(x_step, 0, feat, zfeat, ffeat)
    xc = functools.partial(x_step, 1, cot, zcot, fcot)

    def x_arrived(which, dst):
        landed(dst.at[pl.ds(0, (peers - 1) * nz)], x_recv.at[which])

    z_first(zf)
    ids_v[0] = jnp.zeros_like(ids_v[0])
    ids_v[0, :, :slots] = ids_in[...]
    coef_v[0] = jnp.zeros_like(coef_v[0])
    coef_v[0, :, :nb] = coef_in[...].astype(F32)

    for p in range(1, peers):
        remote(ids_v.at[0], ids_v.at[back(p)], id_send.at[0], id_recv.at[0], row_dev(p)).start()
        remote(coef_v.at[0], coef_v.at[back(p)], coef_send.at[0], coef_recv_sem.at[0], row_dev(p)).start()

    own_coef_down = pltpu.make_async_copy(coef_v.at[0], coefs.at[0], local_sem.at[4])
    own_coef_down.start()

    meta_v[...] = jnp.zeros_like(meta_v)
    down = lax.broadcasted_iota(jnp.int32, (blocks, blocks), 0)
    across = lax.broadcasted_iota(jnp.int32, (blocks, blocks), 1)
    down_slot = lax.broadcasted_iota(jnp.int32, (blocks, slots), 0)
    across_slot = lax.broadcasted_iota(jnp.int32, (blocks, slots), 1)
    for r in range(rels):
        row = block_slots[r, 0:1, :]
        spread = jnp.broadcast_to(row, (blocks, blocks))
        column = jnp.max(jnp.where(down == across, spread, -1), axis=1, keepdims=True)
        same = (column == spread) & (down < across)
        meta_v[r, :, :blocks] = block_slots[r, 1:2, :]
        meta_v[rels + r, :, :blocks] = jnp.max(jnp.where(same, down, -1), axis=0, keepdims=True)
        meta_v[2 * rels + r, :, :slots] = jnp.max(
            jnp.where(column == across_slot, down_slot, -1), axis=0, keepdims=True
        )
    meta_down = pltpu.make_async_copy(meta_v, meta, local_sem.at[5])
    meta_down.start()
    meta_down.wait()
    own_coef_down.wait()

    landed(ids_v.at[others], id_recv.at[0])
    landed(coef_v.at[others], coef_recv_sem.at[0])
    ids_down = pltpu.make_async_copy(ids_v, ids, local_sem.at[3])
    coef_down = pltpu.make_async_copy(
        coef_v.at[pl.ds(1, peers - 1)], coefs.at[pl.ds(1, peers - 1)], local_sem.at[4]
    )
    ids_down.start()
    coef_down.start()
    ids_down.wait()
    coef_down.wait()

    xf(0)
    xc(0)

    load_bases.wait()
    tile = 16
    per = block // tile
    parts = width // block

    def weigh(t):
        hb = t // per
        row = pl.multiple_of((t % per) * tile, tile)
        acc = [jnp.zeros((tile, width), F32) for _ in range(rels)]
        for b in range(nb):
            v = slot_g[1, b * parts + hb, pl.ds(row, tile), :].astype(F32)
            for r in range(rels):
                acc[r] = acc[r] + coefs[0, r, b] * v
        for r in range(rels):
            weights[r, pl.ds(pl.multiple_of(hb * block + row, tile), tile), :] = acc[r].astype(BF16)

    each(0, parts * per, weigh)

    def own_term(o):
        self_term[o] = jnp.dot(feat[o], selfw[...], preferred_element_type=F32)

    each(0, owned, own_term)

    for d in range(1, half):
        z_step(zf, d)
        if d == half - 1:
            z_first(zc)
        xf(d)
        xf(nz - d)
    z_step(zf, half)
    xf(half)

    z_step(zc, 1)
    xc(1)
    xc(nz - 1)
    load_values.wait()
    x_arrived(0, ffeat)

    burst = 4

    def messages(r):
        def some(q):
            found = []
            for u in range(burst):
                j = q * burst + u
                found.append(
                    jnp.dot(values[r, j], ffeat[meta[r, 0, j]], preferred_element_type=F32).astype(BF16)
                )
            for u in range(burst):
                j = q * burst + u
                before = meta[rels + r, 0, j]
                earlier = running[jnp.maximum(before, 0)]
                running[j] = jnp.where(before >= 0, earlier, 0.0) + found[u].astype(F32)

        each(0, blocks // burst, some)

        def pick(s):
            at = meta[2 * rels + r, 0, s]
            slot_g[r, s] = jnp.where(at >= 0, running[jnp.maximum(at, 0)], 0.0).astype(BF16)

        each(0, slots, pick)

    messages(0)
    for d in range(2, half - 1):
        z_step(zc, d)
        xc(d)
        xc(nz - d)
    messages(1)
    if half > 2:
        z_step(zc, half - 1)
        xc(half - 1)
        xc(half + 1)
    z_done(zf)
    slot_sums = zfeat

    def sum_slots(m):
        rows = (owned * block, width)
        at = pl.ds(m * owned, owned)
        total = jnp.dot(slot_g[0, at].reshape(rows), weights[0], preferred_element_type=F32)
        for r in range(1, rels):
            total += jnp.dot(slot_g[r, at].reshape(rows), weights[r], preferred_element_type=F32)
        slot_sums[m] = total.astype(BF16).reshape(owned, block, width)

    each(0, nz, sum_slots)

    def ret_go(j):
        for p in range(1, peers):
            s = slot(p, j)
            remote(
                slot_sums.at[s // owned, s % owned],
                rx.at[j, back(p)],
                ret_send.at[0],
                ret_recv.at[j],
                row_dev(p),
            ).start()

    z_step(zc, half)
    xc(half)
    def ret_pair(d):
        if d > 0:
            ret_go(d)
            ret_go(nz - d)
        elif d == 0:
            ret_go(0)

    ret_go(half)
    ret_pair(half - 1)

    def rs_copy(j, way):
        to = j - 1 if way < 0 else (j + 1) % nz
        at = half if way > 0 and to == 0 else to
        src, dst = ffeat.at[pl.ds(j * owned, owned)], rb.at[at]
        if j == half:
            first = 0 if way < 0 else cut
            src, dst = ffeat.at[pl.ds(j * owned + first, cut)], rb.at[at, pl.ds(first, cut)]
        return remote(src, dst, rs_send.at[at], rs_recv.at[at], z_dev(way))

    def collect(j, o):
        s = slot(0, j)
        total = None
        for p in range(peers):
            weight = jnp.where(ids[p, 0, s] == o, 1.0, 0.0).astype(F32)
            term = (slot_sums[s // owned, s % owned] if p == 0 else rx[j, p]).astype(F32) * weight
            total = term if total is None else total + term
        return total

    def rx_arrived(j):
        landed(rx.at[j, others], ret_recv.at[j])

    def reduce_step(j):
        rx_arrived(j)
        lo, hi = 0, 0
        if 0 < j < half:
            rs_copy(j + 1, -1).wait_recv()
            lo, hi = 0, (cut if j + 1 == half else owned)
        elif j > half:
            rs_copy(j - 1, 1).wait_recv()
            lo, hi = (cut if j - 1 == half else 0), owned

        def plain(o):
            ffeat[j * owned + o] = collect(j, o).astype(BF16)

        def more(o):
            ffeat[j * owned + o] = (collect(j, o) + rb[j, o].astype(F32)).astype(BF16)

        if lo > 0:
            each(0, lo, plain)
        if hi > lo:
            each(lo, hi, more)
        if hi < owned:
            each(hi, owned, plain)
        if j <= half:
            rs_copy(j, -1).start()
        if j >= half:
            rs_copy(j, 1).start()

    x_arrived(1, fcot)

    def relation_grad(r):
        grad_acc[...] = jnp.zeros_like(grad_acc)

        def add(m):
            at = pl.ds(m * owned, owned)
            rows = (owned * block, width)
            grad_acc[...] += lax.dot_general(
                slot_g[r, at].reshape(rows),
                fcot[at].reshape(rows),
                (((0,), (0,)), ((), ())),
                preferred_element_type=F32,
            )

        each(0, nz, add)
        rows = grad_parts.shape[3]
        for h in range(CORES):
            for m in range(nn):
                grad_parts[m, r, h] = grad_acc[pl.ds((h * nn + m) * rows, rows), :]

    relation_grad(0)
    reduce_step(half)
    ret_pair(half - 2)
    for r in range(1, rels):
        relation_grad(r)

    def y_copy(dn):
        return remote(
            grad_parts.at[(n + dn) % nn],
            grad_in.at[nn - dn],
            y_send.at[0],
            y_recv.at[0],
            y_dev(dn),
        )

    for dn in range(1, nn):
        y_copy(dn).start()

    def reduce_pair(d):
        reduce_step(d)
        reduce_step(nz - d)
        ret_pair(d - 2)

    reduce_pair(half - 1)

    if nn > 1:
        landed(grad_in.at[pl.ds(1, nn - 1)], y_recv.at[0])
    rows = grad_parts.shape[3]
    for r in range(rels):
        for h in range(CORES):
            total = grad_parts[n, r, h]
            for dn in range(1, nn):
                total = total + grad_in[dn, r, h]
            grad_sum[r, h] = total.reshape(nx, group, width)

    def row_copy(p):
        to = grad_sum.at[:, (c + p % CORES) % CORES, (x + p // CORES) % nx]
        return remote(to, row_in.at[back(p)], row_send.at[0], row_recv.at[0], row_dev(p))

    for p in range(1, peers):
        row_copy(p).start()
    row_in[0] = grad_sum[:, c, x]

    load_bases_q.wait()

    def coef_sums(b):
        for r in range(rels):
            total = None
            for h in range(CORES):
                term = (grad_sum[r, h].reshape(rows, width) * bases_q[b, h].astype(F32)).sum(
                    axis=0, keepdims=True
                )
                total = term if total is None else total + term
            line = total[:, :128]
            for k in range(1, width // 128):
                line = line + total[:, k * 128 : (k + 1) * 128]
            coef_part[pl.ds(r * nb + b, 1), :] = line

    each(0, nb, coef_sums)

    def cp_copy(dn):
        return remote(
            coef_part, coef_recv.at[nn - dn], cp_send.at[0], cp_recv.at[0], y_dev(dn)
        )

    for dn in range(1, nn):
        cp_copy(dn).start()

    if half > 2:
        reduce_pair(half - 2)

    landed(row_in.at[others], row_recv.at[0])

    def basis_sums(b):
        total = jnp.zeros((group, width), F32)
        for p in range(peers):
            for r in range(rels):
                total = total + coefs[p, r, b] * row_in[p, r]
        basis_part[b % nz, b // nz] = total

    each(0, nb, basis_sums)

    def zb_copy(dz):
        return remote(
            basis_part.at[zs[nz - dz]],
            basis_in.at[nz - dz],
            zb_send.at[0],
            zb_recv.at[0],
            z_dev(dz),
        )

    for dz in range(1, nz):
        zb_copy(dz).start()

    for d in range(half - 3, 0, -1):
        reduce_pair(d)

    landed(basis_in.at[pl.ds(1, nz - 1)], zb_recv.at[0])
    total = basis_part[z]
    for dz in range(1, nz):
        total = total + basis_in[dz]
    basis_sum[...] = total

    def xb_copy(dx):
        return remote(
            basis_sum.at[(x + dx) % nx],
            basis_rows.at[x],
            xb_send.at[0],
            xb_recv.at[0],
            row_dev(dx * CORES),
        )

    for dx in range(1, nx):
        xb_copy(dx).start()
    basis_rows[x] = basis_sum[x]

    rx_arrived(0)
    rs_copy(1, -1).wait_recv()
    rs_copy(nz - 1, 1).wait_recv()

    def finish(o):
        arrived = rb[0, o].astype(F32) + rb[half, o].astype(F32)
        out[o] = (self_term[o] + collect(0, o) + arrived).astype(BF16)

    each(0, owned, finish)

    landed(basis_rows.at[pl.ds(0, nx - 1)], xb_recv.at[0])
    out_basis[...] = basis_rows[...]

    if nn > 1:
        landed(coef_recv.at[pl.ds(1, nn - 1)], cp_recv.at[0])
    total = coef_part[...]
    for dn in range(1, nn):
        total = total + coef_recv[dn]
    column = total.sum(axis=1, keepdims=True)
    wide_shape = (rels * nb, rels * nb)
    diagonal = lax.broadcasted_iota(jnp.int32, wide_shape, 0) == lax.broadcasted_iota(
        jnp.int32, wide_shape, 1
    )
    line = jnp.where(diagonal, jnp.broadcast_to(column, wide_shape), 0.0).sum(axis=0, keepdims=True)
    for r in range(rels):
        out_coef[r : r + 1, :] = line[:, r * nb : (r + 1) * nb]

    z_done(zc)
    sent(stage.at[0, others], x_send.at[0, 0])
    for j in range(nz):
        sent(stage.at[0, others], x_send.at[1, j])
    sent(rx.at[pl.ds(0, nz), others], ret_send.at[0])
    for j in range(1, half + 1):
        rs_copy(j, -1).wait_send()
        rs_copy(nz - j, 1).wait_send()
    sent(ids_v.at[others], id_send.at[0])
    sent(coef_v.at[others], coef_send.at[0])
    sent(row_in.at[others], row_send.at[0])
    if nn > 1:
        sent(grad_in.at[pl.ds(1, nn - 1)], y_send.at[0])
        sent(coef_recv.at[pl.ds(1, nn - 1)], cp_send.at[0])
    sent(basis_in.at[pl.ds(1, nz - 1)], zb_send.at[0])
    sent(basis_sum.at[pl.ds(0, nx - 1)], xb_send.at[0])


def keep_kernel(a, b, c, a_out, b_out, c_out):
    a_out[...] = a[...]
    b_out[...] = b[...]
    c_out[...] = c[...]


def per_device(
    nx, nz, nn, features, cotangent, self_weight, bases, basis_coef, block_values, block_slots, fetch_ids
):
    rels, blocks, block, _ = block_values.shape
    width = features.shape[1]
    slots = fetch_ids.shape[0]
    owned = features.shape[0] // block
    nb = bases.shape[0]
    peers = nx * CORES
    rows = width // (CORES * nn)
    group = rows // nx

    vmem = pl.BlockSpec(memory_space=pltpu.VMEM)
    anywhere = pl.BlockSpec(memory_space=pl.ANY)
    dma = pltpu.SemaphoreType.DMA
    output, basis_grad, coef_grad = pl.pallas_call(
        functools.partial(layer_kernel, nx, nz, nn),
        out_shape=(
            jax.ShapeDtypeStruct((owned, block, width), BF16),
            jax.ShapeDtypeStruct((nx, group, width), F32),
            jax.ShapeDtypeStruct((rels, nb), F32),
        ),
        in_specs=[vmem, vmem, vmem, vmem, vmem, vmem, anywhere, anywhere, anywhere],
        out_specs=(vmem, vmem, vmem),
        scratch_shapes=[
            pltpu.VMEM((3 * rels, 1, 128), jnp.int32),
            pltpu.VMEM((peers, 1, 128), jnp.int32),
            pltpu.VMEM((peers, rels, 128), F32),
            pltpu.SMEM((3 * rels, 1, 128), jnp.int32),
            pltpu.SMEM((peers, 1, 128), jnp.int32),
            pltpu.SMEM((peers, rels, 128), F32),
            pltpu.VMEM((nz, owned, block, width), BF16),
            pltpu.VMEM((nz, owned, block, width), BF16),
            pltpu.VMEM((owned, block, width), BF16),
            pltpu.VMEM((nz + 1, peers, block, width), BF16),
            pltpu.VMEM((slots, block, width), BF16),
            pltpu.VMEM((slots, block, width), BF16),
            pltpu.VMEM((rels, blocks, block, block), BF16),
            pltpu.VMEM((blocks, block, width), F32),
            pltpu.VMEM((rels, slots, block, width), BF16),
            pltpu.VMEM((rels, width, width), BF16),
            pltpu.VMEM((owned, block, width), F32),
            pltpu.VMEM((nz, peers, block, width), BF16),
            pltpu.VMEM((nz, owned, block, width), BF16),
            pltpu.VMEM((width, width), F32),
            pltpu.VMEM((nn, rels, CORES, rows, width), F32),
            pltpu.VMEM((nn, rels, CORES, rows, width), F32),
            pltpu.VMEM((rels, CORES, nx, group, width), F32),
            pltpu.VMEM((nb, CORES, rows, width), BF16),
            pltpu.VMEM((rels * nb, 128), F32),
            pltpu.VMEM((nn, rels * nb, 128), F32),
            pltpu.VMEM((peers, rels, group, width), F32),
            pltpu.VMEM((nz, nx, group, width), F32),
            pltpu.VMEM((nz, nx, group, width), F32),
            pltpu.VMEM((nx, group, width), F32),
            pltpu.VMEM((nx, group, width), F32),
            dma((6,)),
            dma((1,)),
            dma((1,)),
            dma((1,)),
            dma((1,)),
            dma((2, nz)),
            dma((2, nz)),
            dma((2, nz)),
            dma((2,)),
            dma((1,)),
            dma((nz,)),
            dma((nz,)),
            dma((nz,)),
        ]
        + [dma((1,))] * 10,
        compiler_params=pltpu.CompilerParams(
            collective_id=0, has_side_effects=True, vmem_limit_bytes=62 * 1024 * 1024
        ),
    )(
        block_slots.transpose(0, 2, 1),
        fetch_ids.reshape(1, slots),
        basis_coef,
        features.reshape(owned, block, width),
        cotangent.reshape(owned, block, width),
        self_weight,
        bases.reshape(nb * width // block, block, width),
        bases.reshape(nb, CORES, nn, rows, width),
        block_values,
    )
    output, basis_grad, coef_grad = pl.pallas_call(
        keep_kernel,
        out_shape=tuple(jax.ShapeDtypeStruct(a.shape, a.dtype) for a in (output, basis_grad, coef_grad)),
        in_specs=[vmem] * 3,
        out_specs=(vmem,) * 3,
    )(output, basis_grad, coef_grad)
    return (
        output.reshape(owned * block, width),
        basis_grad.reshape(rows, width),
        coef_grad,
    )


def solution(mesh, nx=4):
    nz = mesh.shape["wide"] // (CORES * nx)
    return jax.shard_map(
        functools.partial(per_device, nx, nz, mesh.shape["narrow"]),
        mesh=mesh,
        in_specs=(
            P(("wide", "narrow"), None),
            P(("wide", "narrow"), None),
            P(),
            P(),
            P("wide", None),
            P("wide", "narrow", None, None),
            P("wide", "narrow", None),
            P(("wide", "narrow")),
        ),
        out_specs=(P(("wide", "narrow"), None), P(("wide", "narrow"), None), P("wide", None)),
        check_vma=False,
    )
```

```python
import functools

import jax
import jax.numpy as jnp
from jax import lax
from jax.experimental import pallas as pl
from jax.experimental.pallas import tpu as pltpu
from jax.sharding import PartitionSpec as P

MESH = pl.DeviceIdType.MESH
F32 = jnp.float32
BF16 = jnp.bfloat16
CORES = 2


def layer_kernel(
    nx,
    nz,
    nn,
    block_slots,
    ids_in,
    coef_in,
    feat,
    cot,
    selfw,
    bases_flat,
    bases_split,
    values_hbm,
    out,
    out_basis,
    out_coef,
    meta_v,
    ids_v,
    coef_v,
    meta,
    ids,
    coefs,
    zfeat,
    zcot,
    picked,
    stage,
    ffeat,
    fcot,
    values,
    running,
    slot_g,
    weights,
    self_term,
    rx,
    rb,
    grad_acc,
    grad_parts,
    grad_in,
    grad_sum,
    bases_q,
    coef_part,
    coef_recv,
    row_in,
    basis_part,
    basis_in,
    basis_sum,
    basis_rows,
    local_sem,
    id_send,
    id_recv,
    coef_send,
    coef_recv_sem,
    z_send,
    z_recv,
    x_send,
    x_recv,
    ret_send,
    ret_recv,
    rs_send,
    rs_recv,
    y_send,
    y_recv,
    cp_send,
    cp_recv,
    row_send,
    row_recv,
    zb_send,
    zb_recv,
    xb_send,
    xb_recv,
):
    w = lax.axis_index("wide")
    n = lax.axis_index("narrow")
    x, z, c = w // (CORES * nz), (w // CORES) % nz, w % CORES
    peers = nx * CORES
    owned, block, width = feat.shape
    slots = ffeat.shape[0]
    rels = slot_g.shape[0]
    blocks = values.shape[1]
    nb = basis_part.shape[0] * basis_part.shape[1]
    group = grad_sum.shape[3]
    half = nz // 2
    cut = owned // 2

    zs = [(z + nz - j) % nz for j in range(nz)]
    along = [
        ((x + p // CORES) % nx) * (nz * CORES) + (c + p % CORES) % CORES for p in range(peers)
    ]

    def slot(p, j):
        return along[p] + zs[j] * CORES

    def row_dev(p):
        return (along[p] + z * CORES, n)

    def back(p):
        return ((nx - p // CORES) % nx) * CORES + p % CORES

    def z_dev(dz):
        return (along[0] + zs[(nz - dz) % nz] * CORES, n)

    def y_dev(dn):
        return (w, (n + dn) % nn)

    def remote(src, dst, ssem, rsem, dev):
        return pltpu.make_async_remote_copy(
            src_ref=src, dst_ref=dst, send_sem=ssem, recv_sem=rsem, device_id=dev, device_id_type=MESH
        )

    def sent(block_ref, sem):
        remote(block_ref, block_ref, sem, sem, row_dev(1)).wait_send()

    def landed(block_ref, sem):
        remote(block_ref, block_ref, sem, sem, row_dev(1)).wait_recv()

    def each(lo, hi, body):
        def step(i, carry):
            body(i)
            return carry

        lax.fori_loop(lo, hi, step, 0)

    load_bases = pltpu.make_async_copy(bases_flat, slot_g.at[1], local_sem.at[0])
    load_values = pltpu.make_async_copy(values_hbm, values, local_sem.at[1])
    load_bases_q = pltpu.make_async_copy(bases_split.at[:, :, n], bases_q, local_sem.at[2])
    load_bases.start()
    load_values.start()
    load_bases_q.start()

    barrier = pltpu.get_barrier_semaphore()
    for p in range(1, peers):
        pl.semaphore_signal(barrier, inc=1, device_id=row_dev(p), device_id_type=MESH)
    for dz in range(1, nz):
        pl.semaphore_signal(barrier, inc=1, device_id=z_dev(dz), device_id_type=MESH)
    for dn in range(1, nn):
        pl.semaphore_signal(barrier, inc=1, device_id=y_dev(dn), device_id_type=MESH)
    pl.semaphore_wait(barrier, peers + nz + nn - 3)

    def z_copy(which, own, buf, to, way):
        frm = to - 1 if way > 0 else (to + 1) % nz
        src = own if frm == 0 else buf.at[frm]
        dst = buf.at[to]
        sem = to
        if to == half:
            part = pl.ds(0, cut) if way > 0 else pl.ds(cut, cut)
            src, dst = src.at[part], dst.at[part]
            sem = half if way > 0 else 0
        return remote(src, dst, z_send.at[which, sem], z_recv.at[which, sem], z_dev(way))

    zf = functools.partial(z_copy, 0, feat, zfeat)
    zc = functools.partial(z_copy, 1, cot, zcot)

    def z_first(zcp):
        zcp(1, 1).start()
        zcp(nz - 1, -1).start()

    def z_step(zcp, d):
        if d < half:
            zcp(d, 1).wait_recv()
            zcp(d + 1, 1).start()
            zcp(nz - d, -1).wait_recv()
            zcp(nz - d - 1, -1).start()
        else:
            zcp(half, 1).wait_recv()
            zcp(half, -1).wait_recv()

    def z_done(zcp):
        for d in range(1, half + 1):
            zcp(d, 1).wait_send()
            zcp(nz - d, -1).wait_send()

    others = pl.ds(1, peers - 1)

    reach = sorted(range(1, nx), key=lambda dx: min(dx, nx - dx))
    order = [dx * CORES + k for k in range(CORES) for dx in reach] + list(range(1, CORES))

    def x_step(which, own, buf, dst, j):
        src = own
        if j > 0:
            picked[...] = buf[j]
            src = picked
        at = nz if which == 1 and j == 0 else j
        s = slot(0, j)
        if which == 1 and j > 0:
            sent(stage.at[0, others], x_send.at[0, j])
        for p in order:
            stage[at, p] = src[ids[p, 0, s]]
            remote(
                stage.at[at, p], dst.at[s], x_send.at[which, j], x_recv.at[which], row_dev(p)
            ).start()
        dst[s] = src[ids[0, 0, s]]

    xf = functools.partial(x_step, 0, feat, zfeat, ffeat)
    xc = functools.partial(x_step, 1, cot, zcot, fcot)

    def x_arrived(which, dst):
        landed(dst.at[pl.ds(0, (peers - 1) * nz)], x_recv.at[which])

    z_first(zf)
    ids_v[0] = jnp.zeros_like(ids_v[0])
    ids_v[0, :, :slots] = ids_in[...]
    coef_v[0] = jnp.zeros_like(coef_v[0])
    coef_v[0, :, :nb] = coef_in[...].astype(F32)

    for p in range(1, peers):
        remote(ids_v.at[0], ids_v.at[back(p)], id_send.at[0], id_recv.at[0], row_dev(p)).start()
        remote(coef_v.at[0], coef_v.at[back(p)], coef_send.at[0], coef_recv_sem.at[0], row_dev(p)).start()

    own_coef_down = pltpu.make_async_copy(coef_v.at[0], coefs.at[0], local_sem.at[4])
    own_coef_down.start()

    meta_v[...] = jnp.zeros_like(meta_v)
    down = lax.broadcasted_iota(jnp.int32, (blocks, blocks), 0)
    across = lax.broadcasted_iota(jnp.int32, (blocks, blocks), 1)
    down_slot = lax.broadcasted_iota(jnp.int32, (blocks, slots), 0)
    across_slot = lax.broadcasted_iota(jnp.int32, (blocks, slots), 1)
    for r in range(rels):
        row = block_slots[r, 0:1, :]
        spread = jnp.broadcast_to(row, (blocks, blocks))
        column = jnp.max(jnp.where(down == across, spread, -1), axis=1, keepdims=True)
        same = (column == spread) & (down < across)
        meta_v[r, :, :blocks] = block_slots[r, 1:2, :]
        meta_v[rels + r, :, :blocks] = jnp.max(jnp.where(same, down, -1), axis=0, keepdims=True)
        meta_v[2 * rels + r, :, :slots] = jnp.max(
            jnp.where(column == across_slot, down_slot, -1), axis=0, keepdims=True
        )
    meta_down = pltpu.make_async_copy(meta_v, meta, local_sem.at[5])
    meta_down.start()
    meta_down.wait()
    own_coef_down.wait()

    landed(ids_v.at[others], id_recv.at[0])
    landed(coef_v.at[others], coef_recv_sem.at[0])
    ids_down = pltpu.make_async_copy(ids_v, ids, local_sem.at[3])
    coef_down = pltpu.make_async_copy(
        coef_v.at[pl.ds(1, peers - 1)], coefs.at[pl.ds(1, peers - 1)], local_sem.at[4]
    )
    ids_down.start()
    coef_down.start()
    ids_down.wait()
    coef_down.wait()

    xf(0)
    xc(0)

    load_bases.wait()
    tile = 16
    per = block // tile
    parts = width // block

    def weigh(t):
        hb = t // per
        row = pl.multiple_of((t % per) * tile, tile)
        acc = [jnp.zeros((tile, width), F32) for _ in range(rels)]
        for b in range(nb):
            v = slot_g[1, b * parts + hb, pl.ds(row, tile), :].astype(F32)
            for r in range(rels):
                acc[r] = acc[r] + coefs[0, r, b] * v
        for r in range(rels):
            weights[r, pl.ds(pl.multiple_of(hb * block + row, tile), tile), :] = acc[r].astype(BF16)

    each(0, parts * per, weigh)

    def own_term(o):
        self_term[o] = jnp.dot(feat[o], selfw[...], preferred_element_type=F32)

    each(0, owned, own_term)

    for d in range(1, half):
        z_step(zf, d)
        if d == half - 1:
            z_first(zc)
        xf(d)
        xf(nz - d)
    z_step(zf, half)
    xf(half)

    z_step(zc, 1)
    xc(1)
    xc(nz - 1)
    load_values.wait()
    x_arrived(0, ffeat)

    burst = 4

    def messages(r):
        def some(q):
            found = []
            for u in range(burst):
                j = q * burst + u
                found.append(
                    jnp.dot(values[r, j], ffeat[meta[r, 0, j]], preferred_element_type=F32).astype(BF16)
                )
            for u in range(burst):
                j = q * burst + u
                before = meta[rels + r, 0, j]
                earlier = running[jnp.maximum(before, 0)]
                running[j] = jnp.where(before >= 0, earlier, 0.0) + found[u].astype(F32)

        each(0, blocks // burst, some)

        def pick(s):
            at = meta[2 * rels + r, 0, s]
            slot_g[r, s] = jnp.where(at >= 0, running[jnp.maximum(at, 0)], 0.0).astype(BF16)

        each(0, slots, pick)

    messages(0)
    for d in range(2, half - 1):
        z_step(zc, d)
        xc(d)
        xc(nz - d)
    messages(1)
    if half > 2:
        z_step(zc, half - 1)
        xc(half - 1)
        xc(half + 1)
    z_done(zf)
    slot_sums = zfeat

    def sum_slots(m):
        rows = (owned * block, width)
        at = pl.ds(m * owned, owned)
        total = jnp.dot(slot_g[0, at].reshape(rows), weights[0], preferred_element_type=F32)
        for r in range(1, rels):
            total += jnp.dot(slot_g[r, at].reshape(rows), weights[r], preferred_element_type=F32)
        slot_sums[m] = total.astype(BF16).reshape(owned, block, width)

    each(0, nz, sum_slots)

    def ret_go(j):
        for p in order:
            s = slot(p, j)
            remote(
                slot_sums.at[s // owned, s % owned],
                rx.at[j, back(p)],
                ret_send.at[0],
                ret_recv.at[j],
                row_dev(p),
            ).start()

    z_step(zc, half)
    xc(half)
    def ret_pair(d):
        if d > 0:
            ret_go(d)
            ret_go(nz - d)
        elif d == 0:
            ret_go(0)

    ret_go(half)
    ret_pair(half - 1)

    def rs_copy(j, way):
        to = j - 1 if way < 0 else (j + 1) % nz
        at = half if way > 0 and to == 0 else to
        src, dst = ffeat.at[pl.ds(j * owned, owned)], rb.at[at]
        if j == half:
            first = 0 if way < 0 else cut
            src, dst = ffeat.at[pl.ds(j * owned + first, cut)], rb.at[at, pl.ds(first, cut)]
        return remote(src, dst, rs_send.at[at], rs_recv.at[at], z_dev(way))

    def collect(j, o):
        s = slot(0, j)
        total = None
        for p in range(peers):
            weight = jnp.where(ids[p, 0, s] == o, 1.0, 0.0).astype(F32)
            term = (slot_sums[s // owned, s % owned] if p == 0 else rx[j, p]).astype(F32) * weight
            total = term if total is None else total + term
        return total

    def rx_arrived(j):
        landed(rx.at[j, others], ret_recv.at[j])

    def reduce_step(j):
        rx_arrived(j)
        lo, hi = 0, 0
        if 0 < j < half:
            rs_copy(j + 1, -1).wait_recv()
            lo, hi = 0, (cut if j + 1 == half else owned)
        elif j > half:
            rs_copy(j - 1, 1).wait_recv()
            lo, hi = (cut if j - 1 == half else 0), owned

        def plain(o):
            ffeat[j * owned + o] = collect(j, o).astype(BF16)

        def more(o):
            ffeat[j * owned + o] = (collect(j, o) + rb[j, o].astype(F32)).astype(BF16)

        if lo > 0:
            each(0, lo, plain)
        if hi > lo:
            each(lo, hi, more)
        if hi < owned:
            each(hi, owned, plain)
        if j <= half:
            rs_copy(j, -1).start()
        if j >= half:
            rs_copy(j, 1).start()

    reduce_step(half)
    ret_pair(half - 2)

    x_arrived(1, fcot)

    def relation_grad(r):
        grad_acc[...] = jnp.zeros_like(grad_acc)

        def add(m):
            at = pl.ds(m * owned, owned)
            rows = (owned * block, width)
            grad_acc[...] += lax.dot_general(
                slot_g[r, at].reshape(rows),
                fcot[at].reshape(rows),
                (((0,), (0,)), ((), ())),
                preferred_element_type=F32,
            )

        each(0, nz, add)
        rows = grad_parts.shape[3]
        for h in range(CORES):
            for m in range(nn):
                grad_parts[m, r, h] = grad_acc[pl.ds((h * nn + m) * rows, rows), :]

    def reduce_pair(d):
        reduce_step(d)
        reduce_step(nz - d)
        ret_pair(d - 2)

    relation_grad(0)
    if half > 2:
        reduce_pair(half - 1)
    for r in range(1, rels):
        relation_grad(r)

    def y_copy(dn):
        return remote(
            grad_parts.at[(n + dn) % nn],
            grad_in.at[nn - dn],
            y_send.at[0],
            y_recv.at[0],
            y_dev(dn),
        )

    for dn in range(1, nn):
        y_copy(dn).start()

    if half > 2:
        reduce_pair(half - 2)

    if nn > 1:
        landed(grad_in.at[pl.ds(1, nn - 1)], y_recv.at[0])
    rows = grad_parts.shape[3]
    for r in range(rels):
        for h in range(CORES):
            total = grad_parts[n, r, h]
            for dn in range(1, nn):
                total = total + grad_in[dn, r, h]
            grad_sum[r, h] = total.reshape(nx, group, width)

    def row_copy(p):
        to = grad_sum.at[:, (c + p % CORES) % CORES, (x + p // CORES) % nx]
        return remote(to, row_in.at[back(p)], row_send.at[0], row_recv.at[0], row_dev(p))

    for p in range(1, peers):
        row_copy(p).start()
    row_in[0] = grad_sum[:, c, x]

    load_bases_q.wait()

    def coef_sums(b):
        for r in range(rels):
            total = None
            for h in range(CORES):
                term = (grad_sum[r, h].reshape(rows, width) * bases_q[b, h].astype(F32)).sum(
                    axis=0, keepdims=True
                )
                total = term if total is None else total + term
            line = total[:, :128]
            for k in range(1, width // 128):
                line = line + total[:, k * 128 : (k + 1) * 128]
            coef_part[pl.ds(r * nb + b, 1), :] = line

    each(0, nb, coef_sums)

    def cp_copy(dn):
        return remote(
            coef_part, coef_recv.at[nn - dn], cp_send.at[0], cp_recv.at[0], y_dev(dn)
        )

    for dn in range(1, nn):
        cp_copy(dn).start()

    landed(row_in.at[others], row_recv.at[0])

    def basis_sums(b):
        total = jnp.zeros((group, width), F32)
        for p in range(peers):
            for r in range(rels):
                total = total + coefs[p, r, b] * row_in[p, r]
        basis_part[b % nz, b // nz] = total

    each(0, nb, basis_sums)

    def zb_copy(dz):
        return remote(
            basis_part.at[zs[nz - dz]],
            basis_in.at[nz - dz],
            zb_send.at[0],
            zb_recv.at[0],
            z_dev(dz),
        )

    for dz in range(1, nz):
        zb_copy(dz).start()

    for d in range(half - 3 if half > 2 else 1, 0, -1):
        reduce_pair(d)

    landed(basis_in.at[pl.ds(1, nz - 1)], zb_recv.at[0])
    total = basis_part[z]
    for dz in range(1, nz):
        total = total + basis_in[dz]
    basis_sum[...] = total

    def xb_copy(dx):
        return remote(
            basis_sum.at[(x + dx) % nx],
            basis_rows.at[x],
            xb_send.at[0],
            xb_recv.at[0],
            row_dev(dx * CORES),
        )

    for dx in range(1, nx):
        xb_copy(dx).start()
    basis_rows[x] = basis_sum[x]

    if nn > 1:
        landed(coef_recv.at[pl.ds(1, nn - 1)], cp_recv.at[0])
    total = coef_part[...]
    for dn in range(1, nn):
        total = total + coef_recv[dn]
    column = total.sum(axis=1, keepdims=True)
    wide_shape = (rels * nb, rels * nb)
    diagonal = lax.broadcasted_iota(jnp.int32, wide_shape, 0) == lax.broadcasted_iota(
        jnp.int32, wide_shape, 1
    )
    line = jnp.where(diagonal, jnp.broadcast_to(column, wide_shape), 0.0).sum(axis=0, keepdims=True)
    for r in range(rels):
        out_coef[r : r + 1, :] = line[:, r * nb : (r + 1) * nb]

    rx_arrived(0)
    rs_copy(1, -1).wait_recv()
    rs_copy(nz - 1, 1).wait_recv()

    def finish(o):
        arrived = rb[0, o].astype(F32) + rb[half, o].astype(F32)
        out[o] = (self_term[o] + collect(0, o) + arrived).astype(BF16)

    each(0, owned, finish)

    landed(basis_rows.at[pl.ds(0, nx - 1)], xb_recv.at[0])
    out_basis[...] = basis_rows[...]

    z_done(zc)
    sent(stage.at[0, others], x_send.at[0, 0])
    for j in range(nz):
        sent(stage.at[0, others], x_send.at[1, j])
    sent(rx.at[pl.ds(0, nz), others], ret_send.at[0])
    for j in range(1, half + 1):
        rs_copy(j, -1).wait_send()
        rs_copy(nz - j, 1).wait_send()
    sent(ids_v.at[others], id_send.at[0])
    sent(coef_v.at[others], coef_send.at[0])
    sent(row_in.at[others], row_send.at[0])
    if nn > 1:
        sent(grad_in.at[pl.ds(1, nn - 1)], y_send.at[0])
        sent(coef_recv.at[pl.ds(1, nn - 1)], cp_send.at[0])
    sent(basis_in.at[pl.ds(1, nz - 1)], zb_send.at[0])
    sent(basis_sum.at[pl.ds(0, nx - 1)], xb_send.at[0])


def keep_kernel(a, b, c, a_out, b_out, c_out):
    a_out[...] = a[...]
    b_out[...] = b[...]
    c_out[...] = c[...]


def per_device(
    nx, nz, nn, features, cotangent, self_weight, bases, basis_coef, block_values, block_slots, fetch_ids
):
    rels, blocks, block, _ = block_values.shape
    width = features.shape[1]
    slots = fetch_ids.shape[0]
    owned = features.shape[0] // block
    nb = bases.shape[0]
    peers = nx * CORES
    rows = width // (CORES * nn)
    group = rows // nx

    vmem = pl.BlockSpec(memory_space=pltpu.VMEM)
    anywhere = pl.BlockSpec(memory_space=pl.ANY)
    dma = pltpu.SemaphoreType.DMA
    output, basis_grad, coef_grad = pl.pallas_call(
        functools.partial(layer_kernel, nx, nz, nn),
        out_shape=(
            jax.ShapeDtypeStruct((owned, block, width), BF16),
            jax.ShapeDtypeStruct((nx, group, width), F32),
            jax.ShapeDtypeStruct((rels, nb), F32),
        ),
        in_specs=[vmem, vmem, vmem, vmem, vmem, vmem, anywhere, anywhere, anywhere],
        out_specs=(vmem, vmem, vmem),
        scratch_shapes=[
            pltpu.VMEM((3 * rels, 1, 128), jnp.int32),
            pltpu.VMEM((peers, 1, 128), jnp.int32),
            pltpu.VMEM((peers, rels, 128), F32),
            pltpu.SMEM((3 * rels, 1, 128), jnp.int32),
            pltpu.SMEM((peers, 1, 128), jnp.int32),
            pltpu.SMEM((peers, rels, 128), F32),
            pltpu.VMEM((nz, owned, block, width), BF16),
            pltpu.VMEM((nz, owned, block, width), BF16),
            pltpu.VMEM((owned, block, width), BF16),
            pltpu.VMEM((nz + 1, peers, block, width), BF16),
            pltpu.VMEM((slots, block, width), BF16),
            pltpu.VMEM((slots, block, width), BF16),
            pltpu.VMEM((rels, blocks, block, block), BF16),
            pltpu.VMEM((blocks, block, width), F32),
            pltpu.VMEM((rels, slots, block, width), BF16),
            pltpu.VMEM((rels, width, width), BF16),
            pltpu.VMEM((owned, block, width), F32),
            pltpu.VMEM((nz, peers, block, width), BF16),
            pltpu.VMEM((nz, owned, block, width), BF16),
            pltpu.VMEM((width, width), F32),
            pltpu.VMEM((nn, rels, CORES, rows, width), F32),
            pltpu.VMEM((nn, rels, CORES, rows, width), F32),
            pltpu.VMEM((rels, CORES, nx, group, width), F32),
            pltpu.VMEM((nb, CORES, rows, width), BF16),
            pltpu.VMEM((rels * nb, 128), F32),
            pltpu.VMEM((nn, rels * nb, 128), F32),
            pltpu.VMEM((peers, rels, group, width), F32),
            pltpu.VMEM((nz, nx, group, width), F32),
            pltpu.VMEM((nz, nx, group, width), F32),
            pltpu.VMEM((nx, group, width), F32),
            pltpu.VMEM((nx, group, width), F32),
            dma((6,)),
            dma((1,)),
            dma((1,)),
            dma((1,)),
            dma((1,)),
            dma((2, nz)),
            dma((2, nz)),
            dma((2, nz)),
            dma((2,)),
            dma((1,)),
            dma((nz,)),
            dma((nz,)),
            dma((nz,)),
        ]
        + [dma((1,))] * 10,
        compiler_params=pltpu.CompilerParams(
            collective_id=0, has_side_effects=True, vmem_limit_bytes=62 * 1024 * 1024
        ),
    )(
        block_slots.transpose(0, 2, 1),
        fetch_ids.reshape(1, slots),
        basis_coef,
        features.reshape(owned, block, width),
        cotangent.reshape(owned, block, width),
        self_weight,
        bases.reshape(nb * width // block, block, width),
        bases.reshape(nb, CORES, nn, rows, width),
        block_values,
    )
    output, basis_grad, coef_grad = pl.pallas_call(
        keep_kernel,
        out_shape=tuple(jax.ShapeDtypeStruct(a.shape, a.dtype) for a in (output, basis_grad, coef_grad)),
        in_specs=[vmem] * 3,
        out_specs=(vmem,) * 3,
    )(output, basis_grad, coef_grad)
    return (
        output.reshape(owned * block, width),
        basis_grad.reshape(rows, width),
        coef_grad,
    )


def solution(mesh, nx=4):
    nz = mesh.shape["wide"] // (CORES * nx)
    return jax.shard_map(
        functools.partial(per_device, nx, nz, mesh.shape["narrow"]),
        mesh=mesh,
        in_specs=(
            P(("wide", "narrow"), None),
            P(("wide", "narrow"), None),
            P(),
            P(),
            P("wide", None),
            P("wide", "narrow", None, None),
            P("wide", "narrow", None),
            P(("wide", "narrow")),
        ),
        out_specs=(P(("wide", "narrow"), None), P(("wide", "narrow"), None), P("wide", None)),
        check_vma=False,
    )
```

```python
import functools

import jax
import jax.numpy as jnp
from jax import lax
from jax.experimental import pallas as pl
from jax.experimental.pallas import tpu as pltpu
from jax.sharding import PartitionSpec as P

MESH = pl.DeviceIdType.MESH
F32 = jnp.float32
BF16 = jnp.bfloat16
CORES = 2


def layer_kernel(
    nx,
    nz,
    nn,
    block_slots,
    ids_in,
    coef_in,
    feat,
    cot,
    selfw,
    bases_flat,
    bases_split,
    values_hbm,
    out,
    out_basis,
    out_coef,
    meta_v,
    ids_v,
    coef_v,
    meta,
    ids,
    coefs,
    zfeat,
    zcot,
    picked,
    stage,
    ffeat,
    fcot,
    values,
    running,
    slot_g,
    weights,
    self_term,
    rx,
    rb,
    grad_acc,
    grad_parts,
    grad_in,
    grad_sum,
    bases_q,
    coef_part,
    coef_recv,
    row_in,
    basis_part,
    basis_in,
    basis_sum,
    basis_rows,
    local_sem,
    id_send,
    id_recv,
    coef_send,
    coef_recv_sem,
    z_send,
    z_recv,
    x_send,
    x_recv,
    ret_send,
    ret_recv,
    rs_send,
    rs_recv,
    y_send,
    y_recv,
    cp_send,
    cp_recv,
    row_send,
    row_recv,
    zb_send,
    zb_recv,
    xb_send,
    xb_recv,
):
    w = lax.axis_index("wide")
    n = lax.axis_index("narrow")
    x, z, c = w // (CORES * nz), (w // CORES) % nz, w % CORES
    peers = nx * CORES
    owned, block, width = feat.shape
    slots = ffeat.shape[0]
    rels = slot_g.shape[0]
    blocks = values.shape[1]
    nb = basis_part.shape[0] * basis_part.shape[1]
    group = grad_sum.shape[3]
    half = nz // 2
    cut = owned // 2

    zs = [(z + nz - j) % nz for j in range(nz)]
    along = [
        ((x + p // CORES) % nx) * (nz * CORES) + (c + p % CORES) % CORES for p in range(peers)
    ]

    def slot(p, j):
        return along[p] + zs[j] * CORES

    def row_dev(p):
        return (along[p] + z * CORES, n)

    def back(p):
        return ((nx - p // CORES) % nx) * CORES + p % CORES

    def z_dev(dz):
        return (along[0] + zs[(nz - dz) % nz] * CORES, n)

    def y_dev(dn):
        return (w, (n + dn) % nn)

    def remote(src, dst, ssem, rsem, dev):
        return pltpu.make_async_remote_copy(
            src_ref=src, dst_ref=dst, send_sem=ssem, recv_sem=rsem, device_id=dev, device_id_type=MESH
        )

    def sent(block_ref, sem):
        remote(block_ref, block_ref, sem, sem, row_dev(1)).wait_send()

    def landed(block_ref, sem):
        remote(block_ref, block_ref, sem, sem, row_dev(1)).wait_recv()

    def each(lo, hi, body):
        def step(i, carry):
            body(i)
            return carry

        lax.fori_loop(lo, hi, step, 0)

    load_bases = pltpu.make_async_copy(bases_flat, slot_g.at[1], local_sem.at[0])
    load_values = pltpu.make_async_copy(values_hbm, values, local_sem.at[1])
    load_bases_q = pltpu.make_async_copy(bases_split.at[:, :, n], bases_q, local_sem.at[2])
    load_bases.start()
    load_values.start()
    load_bases_q.start()

    barrier = pltpu.get_barrier_semaphore()
    for p in range(1, peers):
        pl.semaphore_signal(barrier, inc=1, device_id=row_dev(p), device_id_type=MESH)
    for dz in range(1, nz):
        pl.semaphore_signal(barrier, inc=1, device_id=z_dev(dz), device_id_type=MESH)
    for dn in range(1, nn):
        pl.semaphore_signal(barrier, inc=1, device_id=y_dev(dn), device_id_type=MESH)
    pl.semaphore_wait(barrier, peers + nz + nn - 3)

    def z_copy(which, own, buf, to, way):
        frm = to - 1 if way > 0 else (to + 1) % nz
        src = own if frm == 0 else buf.at[frm]
        dst = buf.at[to]
        sem = to
        if to == half:
            part = pl.ds(0, cut) if way > 0 else pl.ds(cut, cut)
            src, dst = src.at[part], dst.at[part]
            sem = half if way > 0 else 0
        return remote(src, dst, z_send.at[which, sem], z_recv.at[which, sem], z_dev(way))

    zf = functools.partial(z_copy, 0, feat, zfeat)
    zc = functools.partial(z_copy, 1, cot, zcot)

    def z_first(zcp):
        zcp(1, 1).start()
        zcp(nz - 1, -1).start()

    def z_step(zcp, d):
        if d < half:
            zcp(d, 1).wait_recv()
            zcp(d + 1, 1).start()
            zcp(nz - d, -1).wait_recv()
            zcp(nz - d - 1, -1).start()
        else:
            zcp(half, 1).wait_recv()
            zcp(half, -1).wait_recv()

    def z_done(zcp):
        for d in range(1, half + 1):
            zcp(d, 1).wait_send()
            zcp(nz - d, -1).wait_send()

    others = pl.ds(1, peers - 1)

    def x_step(which, own, buf, dst, j):
        src = own
        if j > 0:
            picked[...] = buf[j]
            src = picked
        at = nz if which == 1 and j == 0 else j
        s = slot(0, j)
        if which == 1 and j > 0:
            sent(stage.at[0, others], x_send.at[0, j])
        for p in range(1, peers):
            stage[at, p] = src[ids[p, 0, s]]
            remote(
                stage.at[at, p], dst.at[s], x_send.at[which, j], x_recv.at[which], row_dev(p)
            ).start()
        dst[s] = src[ids[0, 0, s]]

    xf = functools.partial(x_step, 0, feat, zfeat, ffeat)
    xc = functools.partial(x_step, 1, cot, zcot, fcot)

    def x_arrived(which, dst):
        landed(dst.at[pl.ds(0, (peers - 1) * nz)], x_recv.at[which])

    z_first(zf)
    ids_v[0] = jnp.zeros_like(ids_v[0])
    ids_v[0, :, :slots] = ids_in[...]
    coef_v[0] = jnp.zeros_like(coef_v[0])
    coef_v[0, :, :nb] = coef_in[...].astype(F32)

    for p in range(1, peers):
        remote(ids_v.at[0], ids_v.at[back(p)], id_send.at[0], id_recv.at[0], row_dev(p)).start()
        remote(coef_v.at[0], coef_v.at[back(p)], coef_send.at[0], coef_recv_sem.at[0], row_dev(p)).start()

    own_coef_down = pltpu.make_async_copy(coef_v.at[0], coefs.at[0], local_sem.at[4])
    own_coef_down.start()

    meta_v[...] = jnp.zeros_like(meta_v)
    down = lax.broadcasted_iota(jnp.int32, (blocks, blocks), 0)
    across = lax.broadcasted_iota(jnp.int32, (blocks, blocks), 1)
    down_slot = lax.broadcasted_iota(jnp.int32, (blocks, slots), 0)
    across_slot = lax.broadcasted_iota(jnp.int32, (blocks, slots), 1)
    for r in range(rels):
        row = block_slots[r, 0:1, :]
        spread = jnp.broadcast_to(row, (blocks, blocks))
        column = jnp.max(jnp.where(down == across, spread, -1), axis=1, keepdims=True)
        same = (column == spread) & (down < across)
        meta_v[r, :, :blocks] = block_slots[r, 1:2, :]
        meta_v[rels + r, :, :blocks] = jnp.max(jnp.where(same, down, -1), axis=0, keepdims=True)
        meta_v[2 * rels + r, :, :slots] = jnp.max(
            jnp.where(column == across_slot, down_slot, -1), axis=0, keepdims=True
        )
    meta_down = pltpu.make_async_copy(meta_v, meta, local_sem.at[5])
    meta_down.start()
    meta_down.wait()
    own_coef_down.wait()

    landed(ids_v.at[others], id_recv.at[0])
    landed(coef_v.at[others], coef_recv_sem.at[0])
    ids_down = pltpu.make_async_copy(ids_v, ids, local_sem.at[3])
    coef_down = pltpu.make_async_copy(
        coef_v.at[pl.ds(1, peers - 1)], coefs.at[pl.ds(1, peers - 1)], local_sem.at[4]
    )
    ids_down.start()
    coef_down.start()
    ids_down.wait()
    coef_down.wait()

    xf(0)
    xc(0)

    load_bases.wait()
    tile = 16
    per = block // tile
    parts = width // block

    def weigh(t):
        hb = t // per
        row = pl.multiple_of((t % per) * tile, tile)
        acc = [jnp.zeros((tile, width), F32) for _ in range(rels)]
        for b in range(nb):
            v = slot_g[1, b * parts + hb, pl.ds(row, tile), :].astype(F32)
            for r in range(rels):
                acc[r] = acc[r] + coefs[0, r, b] * v
        for r in range(rels):
            weights[r, pl.ds(pl.multiple_of(hb * block + row, tile), tile), :] = acc[r].astype(BF16)

    each(0, parts * per, weigh)

    def own_term(o):
        self_term[o] = jnp.dot(feat[o], selfw[...], preferred_element_type=F32)

    each(0, owned, own_term)

    for d in range(1, half):
        z_step(zf, d)
        if d == half - 1:
            z_first(zc)
        xf(d)
        xf(nz - d)
    z_step(zf, half)
    xf(half)

    z_step(zc, 1)
    xc(1)
    xc(nz - 1)
    load_values.wait()
    x_arrived(0, ffeat)

    burst = 4

    def messages(r):
        def some(q):
            found = []
            for u in range(burst):
                j = q * burst + u
                found.append(
                    jnp.dot(values[r, j], ffeat[meta[r, 0, j]], preferred_element_type=F32).astype(BF16)
                )
            for u in range(burst):
                j = q * burst + u
                before = meta[rels + r, 0, j]
                earlier = running[jnp.maximum(before, 0)]
                running[j] = jnp.where(before >= 0, earlier, 0.0) + found[u].astype(F32)

        each(0, blocks // burst, some)

        def pick(s):
            at = meta[2 * rels + r, 0, s]
            slot_g[r, s] = jnp.where(at >= 0, running[jnp.maximum(at, 0)], 0.0).astype(BF16)

        each(0, slots, pick)

    messages(0)
    for d in range(2, half - 1):
        z_step(zc, d)
        xc(d)
        xc(nz - d)
    messages(1)
    if half > 2:
        z_step(zc, half - 1)
        xc(half - 1)
        xc(half + 1)
    z_done(zf)
    slot_sums = zfeat

    def sum_slots(m):
        rows = (owned * block, width)
        at = pl.ds(m * owned, owned)
        total = jnp.dot(slot_g[0, at].reshape(rows), weights[0], preferred_element_type=F32)
        for r in range(1, rels):
            total += jnp.dot(slot_g[r, at].reshape(rows), weights[r], preferred_element_type=F32)
        slot_sums[m] = total.astype(BF16).reshape(owned, block, width)

    each(0, nz, sum_slots)

    def ret_go(j):
        for p in range(1, peers):
            s = slot(p, j)
            remote(
                slot_sums.at[s // owned, s % owned],
                rx.at[j, back(p)],
                ret_send.at[0],
                ret_recv.at[j],
                row_dev(p),
            ).start()

    z_step(zc, half)
    xc(half)
    def ret_pair(d):
        if d > 0:
            ret_go(d)
            ret_go(nz - d)
        elif d == 0:
            ret_go(0)

    ret_go(half)
    ret_pair(half - 1)

    def rs_copy(j, way):
        to = j - 1 if way < 0 else (j + 1) % nz
        at = half if way > 0 and to == 0 else to
        src, dst = ffeat.at[pl.ds(j * owned, owned)], rb.at[at]
        if j == half:
            first = 0 if way < 0 else cut
            src, dst = ffeat.at[pl.ds(j * owned + first, cut)], rb.at[at, pl.ds(first, cut)]
        return remote(src, dst, rs_send.at[at], rs_recv.at[at], z_dev(way))

    def collect(j, o):
        s = slot(0, j)
        total = None
        for p in range(peers):
            weight = jnp.where(ids[p, 0, s] == o, 1.0, 0.0).astype(F32)
            term = (slot_sums[s // owned, s % owned] if p == 0 else rx[j, p]).astype(F32) * weight
            total = term if total is None else total + term
        return total

    def rx_arrived(j):
        landed(rx.at[j, others], ret_recv.at[j])

    def reduce_step(j):
        rx_arrived(j)
        lo, hi = 0, 0
        if 0 < j < half:
            rs_copy(j + 1, -1).wait_recv()
            lo, hi = 0, (cut if j + 1 == half else owned)
        elif j > half:
            rs_copy(j - 1, 1).wait_recv()
            lo, hi = (cut if j - 1 == half else 0), owned

        def plain(o):
            ffeat[j * owned + o] = collect(j, o).astype(BF16)

        def more(o):
            ffeat[j * owned + o] = (collect(j, o) + rb[j, o].astype(F32)).astype(BF16)

        if lo > 0:
            each(0, lo, plain)
        if hi > lo:
            each(lo, hi, more)
        if hi < owned:
            each(hi, owned, plain)
        if j <= half:
            rs_copy(j, -1).start()
        if j >= half:
            rs_copy(j, 1).start()

    reduce_step(half)
    ret_pair(half - 2)

    x_arrived(1, fcot)

    def relation_grad(r):
        grad_acc[...] = jnp.zeros_like(grad_acc)

        def add(m):
            at = pl.ds(m * owned, owned)
            rows = (owned * block, width)
            grad_acc[...] += lax.dot_general(
                slot_g[r, at].reshape(rows),
                fcot[at].reshape(rows),
                (((0,), (0,)), ((), ())),
                preferred_element_type=F32,
            )

        each(0, nz, add)
        rows = grad_parts.shape[3]
        for h in range(CORES):
            for m in range(nn):
                grad_parts[m, r, h] = grad_acc[pl.ds((h * nn + m) * rows, rows), :]

    def reduce_pair(d):
        reduce_step(d)
        reduce_step(nz - d)
        ret_pair(d - 2)

    relation_grad(0)
    if half > 2:
        reduce_pair(half - 1)
    for r in range(1, rels):
        relation_grad(r)

    def y_copy(dn):
        return remote(
            grad_parts.at[(n + dn) % nn],
            grad_in.at[nn - dn],
            y_send.at[0],
            y_recv.at[0],
            y_dev(dn),
        )

    for dn in range(1, nn):
        y_copy(dn).start()

    if half > 2:
        reduce_pair(half - 2)

    if nn > 1:
        landed(grad_in.at[pl.ds(1, nn - 1)], y_recv.at[0])
    rows = grad_parts.shape[3]
    for r in range(rels):
        for h in range(CORES):
            total = grad_parts[n, r, h]
            for dn in range(1, nn):
                total = total + grad_in[dn, r, h]
            grad_sum[r, h] = total.reshape(nx, group, width)

    def row_copy(p):
        to = grad_sum.at[:, (c + p % CORES) % CORES, (x + p // CORES) % nx]
        return remote(to, row_in.at[back(p)], row_send.at[0], row_recv.at[0], row_dev(p))

    for p in range(1, peers):
        row_copy(p).start()
    row_in[0] = grad_sum[:, c, x]

    load_bases_q.wait()

    def coef_sums(b):
        for r in range(rels):
            total = None
            for h in range(CORES):
                term = (grad_sum[r, h].reshape(rows, width) * bases_q[b, h].astype(F32)).sum(
                    axis=0, keepdims=True
                )
                total = term if total is None else total + term
            line = total[:, :128]
            for k in range(1, width // 128):
                line = line + total[:, k * 128 : (k + 1) * 128]
            coef_part[pl.ds(r * nb + b, 1), :] = line

    each(0, nb, coef_sums)

    def cp_copy(dn):
        return remote(
            coef_part, coef_recv.at[nn - dn], cp_send.at[0], cp_recv.at[0], y_dev(dn)
        )

    for dn in range(1, nn):
        cp_copy(dn).start()

    landed(row_in.at[others], row_recv.at[0])

    def basis_sums(b):
        total = jnp.zeros((group, width), F32)
        for p in range(peers):
            for r in range(rels):
                total = total + coefs[p, r, b] * row_in[p, r]
        basis_part[b % nz, b // nz] = total

    each(0, nb, basis_sums)

    def zb_copy(dz):
        return remote(
            basis_part.at[zs[nz - dz]],
            basis_in.at[nz - dz],
            zb_send.at[0],
            zb_recv.at[0],
            z_dev(dz),
        )

    for dz in range(1, nz):
        zb_copy(dz).start()

    for d in range(half - 3 if half > 2 else 1, 0, -1):
        reduce_pair(d)

    landed(basis_in.at[pl.ds(1, nz - 1)], zb_recv.at[0])
    total = basis_part[z]
    for dz in range(1, nz):
        total = total + basis_in[dz]
    basis_sum[...] = total

    def xb_copy(dx):
        return remote(
            basis_sum.at[(x + dx) % nx],
            basis_rows.at[x],
            xb_send.at[0],
            xb_recv.at[0],
            row_dev(dx * CORES),
        )

    for dx in range(1, nx):
        xb_copy(dx).start()
    basis_rows[x] = basis_sum[x]

    if nn > 1:
        landed(coef_recv.at[pl.ds(1, nn - 1)], cp_recv.at[0])
    total = coef_part[...]
    for dn in range(1, nn):
        total = total + coef_recv[dn]
    column = total.sum(axis=1, keepdims=True)
    wide_shape = (rels * nb, rels * nb)
    diagonal = lax.broadcasted_iota(jnp.int32, wide_shape, 0) == lax.broadcasted_iota(
        jnp.int32, wide_shape, 1
    )
    line = jnp.where(diagonal, jnp.broadcast_to(column, wide_shape), 0.0).sum(axis=0, keepdims=True)
    for r in range(rels):
        out_coef[r : r + 1, :] = line[:, r * nb : (r + 1) * nb]

    rx_arrived(0)
    rs_copy(1, -1).wait_recv()
    rs_copy(nz - 1, 1).wait_recv()

    def finish(o):
        arrived = rb[0, o].astype(F32) + rb[half, o].astype(F32)
        out[o] = (self_term[o] + collect(0, o) + arrived).astype(BF16)

    each(0, owned, finish)

    landed(basis_rows.at[pl.ds(0, nx - 1)], xb_recv.at[0])
    out_basis[...] = basis_rows[...]

    z_done(zc)
    sent(stage.at[0, others], x_send.at[0, 0])
    for j in range(nz):
        sent(stage.at[0, others], x_send.at[1, j])
    sent(rx.at[pl.ds(0, nz), others], ret_send.at[0])
    for j in range(1, half + 1):
        rs_copy(j, -1).wait_send()
        rs_copy(nz - j, 1).wait_send()
    sent(ids_v.at[others], id_send.at[0])
    sent(coef_v.at[others], coef_send.at[0])
    sent(row_in.at[others], row_send.at[0])
    if nn > 1:
        sent(grad_in.at[pl.ds(1, nn - 1)], y_send.at[0])
        sent(coef_recv.at[pl.ds(1, nn - 1)], cp_send.at[0])
    sent(basis_in.at[pl.ds(1, nz - 1)], zb_send.at[0])
    sent(basis_sum.at[pl.ds(0, nx - 1)], xb_send.at[0])


def keep_kernel(a, b, c, a_out, b_out, c_out):
    a_out[...] = a[...]
    b_out[...] = b[...]
    c_out[...] = c[...]


def per_device(
    nx, nz, nn, features, cotangent, self_weight, bases, basis_coef, block_values, block_slots, fetch_ids
):
    rels, blocks, block, _ = block_values.shape
    width = features.shape[1]
    slots = fetch_ids.shape[0]
    owned = features.shape[0] // block
    nb = bases.shape[0]
    peers = nx * CORES
    rows = width // (CORES * nn)
    group = rows // nx

    vmem = pl.BlockSpec(memory_space=pltpu.VMEM)
    anywhere = pl.BlockSpec(memory_space=pl.ANY)
    dma = pltpu.SemaphoreType.DMA
    output, basis_grad, coef_grad = pl.pallas_call(
        functools.partial(layer_kernel, nx, nz, nn),
        out_shape=(
            jax.ShapeDtypeStruct((owned, block, width), BF16),
            jax.ShapeDtypeStruct((nx, group, width), F32),
            jax.ShapeDtypeStruct((rels, nb), F32),
        ),
        in_specs=[vmem, vmem, vmem, vmem, vmem, vmem, anywhere, anywhere, anywhere],
        out_specs=(vmem, vmem, vmem),
        scratch_shapes=[
            pltpu.VMEM((3 * rels, 1, 128), jnp.int32),
            pltpu.VMEM((peers, 1, 128), jnp.int32),
            pltpu.VMEM((peers, rels, 128), F32),
            pltpu.SMEM((3 * rels, 1, 128), jnp.int32),
            pltpu.SMEM((peers, 1, 128), jnp.int32),
            pltpu.SMEM((peers, rels, 128), F32),
            pltpu.VMEM((nz, owned, block, width), BF16),
            pltpu.VMEM((nz, owned, block, width), BF16),
            pltpu.VMEM((owned, block, width), BF16),
            pltpu.VMEM((nz + 1, peers, block, width), BF16),
            pltpu.VMEM((slots, block, width), BF16),
            pltpu.VMEM((slots, block, width), BF16),
            pltpu.VMEM((rels, blocks, block, block), BF16),
            pltpu.VMEM((blocks, block, width), F32),
            pltpu.VMEM((rels, slots, block, width), BF16),
            pltpu.VMEM((rels, width, width), BF16),
            pltpu.VMEM((owned, block, width), F32),
            pltpu.VMEM((nz, peers, block, width), BF16),
            pltpu.VMEM((nz, owned, block, width), BF16),
            pltpu.VMEM((width, width), F32),
            pltpu.VMEM((nn, rels, CORES, rows, width), F32),
            pltpu.VMEM((nn, rels, CORES, rows, width), F32),
            pltpu.VMEM((rels, CORES, nx, group, width), F32),
            pltpu.VMEM((nb, CORES, rows, width), BF16),
            pltpu.VMEM((rels * nb, 128), F32),
            pltpu.VMEM((nn, rels * nb, 128), F32),
            pltpu.VMEM((peers, rels, group, width), F32),
            pltpu.VMEM((nz, nx, group, width), F32),
            pltpu.VMEM((nz, nx, group, width), F32),
            pltpu.VMEM((nx, group, width), F32),
            pltpu.VMEM((nx, group, width), F32),
            dma((6,)),
            dma((1,)),
            dma((1,)),
            dma((1,)),
            dma((1,)),
            dma((2, nz)),
            dma((2, nz)),
            dma((2, nz)),
            dma((2,)),
            dma((1,)),
            dma((nz,)),
            dma((nz,)),
            dma((nz,)),
        ]
        + [dma((1,))] * 10,
        compiler_params=pltpu.CompilerParams(
            collective_id=0, has_side_effects=True, vmem_limit_bytes=62 * 1024 * 1024
        ),
    )(
        block_slots.transpose(0, 2, 1),
        fetch_ids.reshape(1, slots),
        basis_coef,
        features.reshape(owned, block, width),
        cotangent.reshape(owned, block, width),
        self_weight,
        bases.reshape(nb * width // block, block, width),
        bases.reshape(nb, CORES, nn, rows, width),
        block_values,
    )
    output, basis_grad, coef_grad = pl.pallas_call(
        keep_kernel,
        out_shape=tuple(jax.ShapeDtypeStruct(a.shape, a.dtype) for a in (output, basis_grad, coef_grad)),
        in_specs=[vmem] * 3,
        out_specs=(vmem,) * 3,
    )(output, basis_grad, coef_grad)
    return (
        output.reshape(owned * block, width),
        basis_grad.reshape(rows, width),
        coef_grad,
    )


def solution(mesh, nx=4):
    nz = mesh.shape["wide"] // (CORES * nx)
    return jax.shard_map(
        functools.partial(per_device, nx, nz, mesh.shape["narrow"]),
        mesh=mesh,
        in_specs=(
            P(("wide", "narrow"), None),
            P(("wide", "narrow"), None),
            P(),
            P(),
            P("wide", None),
            P("wide", "narrow", None, None),
            P("wide", "narrow", None),
            P(("wide", "narrow")),
        ),
        out_specs=(P(("wide", "narrow"), None), P(("wide", "narrow"), None), P("wide", None)),
        check_vma=False,
    )
```

```python
import functools

import jax
import jax.numpy as jnp
from jax import lax
from jax.experimental import pallas as pl
from jax.experimental.pallas import tpu as pltpu
from jax.sharding import PartitionSpec as P

MESH = pl.DeviceIdType.MESH
F32 = jnp.float32
BF16 = jnp.bfloat16
CORES = 2


def layer_kernel(
    nx,
    nz,
    nn,
    block_slots,
    ids_in,
    coef_in,
    feat,
    cot,
    selfw,
    bases_flat,
    bases_split,
    values_hbm,
    out,
    out_basis,
    out_coef,
    meta_v,
    ids_v,
    coef_v,
    meta,
    ids,
    coefs,
    zfeat,
    zcot,
    picked,
    stage,
    ffeat,
    fcot,
    values,
    running,
    slot_g,
    weights,
    self_term,
    rx,
    rb,
    grad_acc,
    grad_parts,
    grad_in,
    grad_sum,
    bases_q,
    coef_part,
    coef_recv,
    row_in,
    basis_part,
    basis_in,
    basis_sum,
    basis_rows,
    local_sem,
    id_send,
    id_recv,
    coef_send,
    coef_recv_sem,
    z_send,
    z_recv,
    x_send,
    x_recv,
    ret_send,
    ret_recv,
    rs_send,
    rs_recv,
    y_send,
    y_recv,
    cp_send,
    cp_recv,
    row_send,
    row_recv,
    zb_send,
    zb_recv,
    xb_send,
    xb_recv,
):
    w = lax.axis_index("wide")
    n = lax.axis_index("narrow")
    x, z, c = w // (CORES * nz), (w // CORES) % nz, w % CORES
    peers = nx * CORES
    owned, block, width = feat.shape
    slots = ffeat.shape[0]
    rels = slot_g.shape[0]
    blocks = values.shape[1]
    nb = basis_part.shape[0] * basis_part.shape[1]
    group = grad_sum.shape[3]
    half = nz // 2
    cut = owned // 2

    zs = [(z + nz - j) % nz for j in range(nz)]
    along = [
        ((x + p // CORES) % nx) * (nz * CORES) + (c + p % CORES) % CORES for p in range(peers)
    ]

    def slot(p, j):
        return along[p] + zs[j] * CORES

    def row_dev(p):
        return (along[p] + z * CORES, n)

    def back(p):
        return ((nx - p // CORES) % nx) * CORES + p % CORES

    def z_dev(dz):
        return (along[0] + zs[(nz - dz) % nz] * CORES, n)

    def y_dev(dn):
        return (w, (n + dn) % nn)

    def remote(src, dst, ssem, rsem, dev):
        return pltpu.make_async_remote_copy(
            src_ref=src, dst_ref=dst, send_sem=ssem, recv_sem=rsem, device_id=dev, device_id_type=MESH
        )

    def sent(block_ref, sem):
        remote(block_ref, block_ref, sem, sem, row_dev(1)).wait_send()

    def landed(block_ref, sem):
        remote(block_ref, block_ref, sem, sem, row_dev(1)).wait_recv()

    def each(lo, hi, body):
        def step(i, carry):
            body(i)
            return carry

        lax.fori_loop(lo, hi, step, 0)

    load_bases = pltpu.make_async_copy(bases_flat, slot_g.at[1], local_sem.at[0])
    load_values = pltpu.make_async_copy(values_hbm, values, local_sem.at[1])
    load_bases_q = pltpu.make_async_copy(bases_split.at[:, :, n], bases_q, local_sem.at[2])
    load_bases.start()
    load_values.start()
    load_bases_q.start()

    barrier = pltpu.get_barrier_semaphore()
    for p in range(1, peers):
        pl.semaphore_signal(barrier, inc=1, device_id=row_dev(p), device_id_type=MESH)
    for dz in range(1, nz):
        pl.semaphore_signal(barrier, inc=1, device_id=z_dev(dz), device_id_type=MESH)
    for dn in range(1, nn):
        pl.semaphore_signal(barrier, inc=1, device_id=y_dev(dn), device_id_type=MESH)
    pl.semaphore_wait(barrier, peers + nz + nn - 3)

    def z_copy(which, own, buf, to, way):
        frm = to - 1 if way > 0 else (to + 1) % nz
        src = own if frm == 0 else buf.at[frm]
        dst = buf.at[to]
        sem = to
        if to == half:
            part = pl.ds(0, cut) if way > 0 else pl.ds(cut, cut)
            src, dst = src.at[part], dst.at[part]
            sem = half if way > 0 else 0
        return remote(src, dst, z_send.at[which, sem], z_recv.at[which, sem], z_dev(way))

    zf = functools.partial(z_copy, 0, feat, zfeat)
    zc = functools.partial(z_copy, 1, cot, zcot)

    def z_first(zcp):
        zcp(1, 1).start()
        zcp(nz - 1, -1).start()

    def z_step(zcp, d):
        if d < half:
            zcp(d, 1).wait_recv()
            zcp(d + 1, 1).start()
            zcp(nz - d, -1).wait_recv()
            zcp(nz - d - 1, -1).start()
        else:
            zcp(half, 1).wait_recv()
            zcp(half, -1).wait_recv()

    def z_done(zcp):
        for d in range(1, half + 1):
            zcp(d, 1).wait_send()
            zcp(nz - d, -1).wait_send()

    others = pl.ds(1, peers - 1)

    def x_step(which, own, buf, dst, j):
        src = own
        if j > 0:
            picked[...] = buf[j]
            src = picked
        at = nz if which == 1 and j == 0 else j
        s = slot(0, j)
        if which == 1 and j > 0:
            sent(stage.at[0, others], x_send.at[0, j])
        for p in range(1, peers):
            stage[at, p] = src[ids[p, 0, s]]
            remote(
                stage.at[at, p], dst.at[s], x_send.at[which, j], x_recv.at[which], row_dev(p)
            ).start()
        dst[s] = src[ids[0, 0, s]]

    xf = functools.partial(x_step, 0, feat, zfeat, ffeat)
    xc = functools.partial(x_step, 1, cot, zcot, fcot)

    def x_arrived(which, dst):
        landed(dst.at[pl.ds(0, (peers - 1) * nz)], x_recv.at[which])

    z_first(zf)
    ids_v[0] = jnp.zeros_like(ids_v[0])
    ids_v[0, :, :slots] = ids_in[...]
    coef_v[0] = jnp.zeros_like(coef_v[0])
    coef_v[0, :, :nb] = coef_in[...].astype(F32)

    for p in range(1, peers):
        remote(ids_v.at[0], ids_v.at[back(p)], id_send.at[0], id_recv.at[0], row_dev(p)).start()
        remote(coef_v.at[0], coef_v.at[back(p)], coef_send.at[0], coef_recv_sem.at[0], row_dev(p)).start()

    own_coef_down = pltpu.make_async_copy(coef_v.at[0], coefs.at[0], local_sem.at[4])
    own_coef_down.start()

    meta_v[...] = jnp.zeros_like(meta_v)
    down = lax.broadcasted_iota(jnp.int32, (blocks, blocks), 0)
    across = lax.broadcasted_iota(jnp.int32, (blocks, blocks), 1)
    down_slot = lax.broadcasted_iota(jnp.int32, (blocks, slots), 0)
    across_slot = lax.broadcasted_iota(jnp.int32, (blocks, slots), 1)
    for r in range(rels):
        row = block_slots[r, 0:1, :]
        spread = jnp.broadcast_to(row, (blocks, blocks))
        column = jnp.max(jnp.where(down == across, spread, -1), axis=1, keepdims=True)
        same = (column == spread) & (down < across)
        meta_v[r, :, :blocks] = block_slots[r, 1:2, :]
        meta_v[rels + r, :, :blocks] = jnp.max(jnp.where(same, down, -1), axis=0, keepdims=True)
        meta_v[2 * rels + r, :, :slots] = jnp.max(
            jnp.where(column == across_slot, down_slot, -1), axis=0, keepdims=True
        )
    meta_down = pltpu.make_async_copy(meta_v, meta, local_sem.at[5])
    meta_down.start()
    meta_down.wait()
    own_coef_down.wait()

    landed(ids_v.at[others], id_recv.at[0])
    landed(coef_v.at[others], coef_recv_sem.at[0])
    ids_down = pltpu.make_async_copy(ids_v, ids, local_sem.at[3])
    coef_down = pltpu.make_async_copy(
        coef_v.at[pl.ds(1, peers - 1)], coefs.at[pl.ds(1, peers - 1)], local_sem.at[4]
    )
    ids_down.start()
    coef_down.start()
    ids_down.wait()
    coef_down.wait()

    xf(0)
    xc(0)

    load_bases.wait()
    tile = 16
    per = block // tile
    parts = width // block

    def weigh(t):
        hb = t // per
        row = pl.multiple_of((t % per) * tile, tile)
        acc = [jnp.zeros((tile, width), F32) for _ in range(rels)]
        for b in range(nb):
            v = slot_g[1, b * parts + hb, pl.ds(row, tile), :].astype(F32)
            for r in range(rels):
                acc[r] = acc[r] + coefs[0, r, b] * v
        for r in range(rels):
            weights[r, pl.ds(pl.multiple_of(hb * block + row, tile), tile), :] = acc[r].astype(BF16)

    each(0, parts * per, weigh)

    def own_term(o):
        self_term[o] = jnp.dot(feat[o], selfw[...], preferred_element_type=F32)

    each(0, owned, own_term)

    for d in range(1, half):
        z_step(zf, d)
        if d == half - 1:
            z_first(zc)
        xf(d)
        xf(nz - d)
    z_step(zf, half)
    xf(half)

    z_step(zc, 1)
    xc(1)
    xc(nz - 1)
    load_values.wait()
    x_arrived(0, ffeat)

    burst = 4

    def messages(r):
        def some(q):
            found = []
            for u in range(burst):
                j = q * burst + u
                found.append(
                    jnp.dot(values[r, j], ffeat[meta[r, 0, j]], preferred_element_type=F32).astype(BF16)
                )
            for u in range(burst):
                j = q * burst + u
                before = meta[rels + r, 0, j]
                earlier = running[jnp.maximum(before, 0)]
                running[j] = jnp.where(before >= 0, earlier, 0.0) + found[u].astype(F32)

        each(0, blocks // burst, some)

        def pick(s):
            at = meta[2 * rels + r, 0, s]
            slot_g[r, s] = jnp.where(at >= 0, running[jnp.maximum(at, 0)], 0.0).astype(BF16)

        each(0, slots, pick)

    messages(0)
    for d in range(2, half - 1):
        z_step(zc, d)
        xc(d)
        xc(nz - d)
    messages(1)
    if half > 2:
        z_step(zc, half - 1)
        xc(half - 1)
        xc(half + 1)
    z_done(zf)
    slot_sums = zfeat

    def sum_slots(m):
        rows = (owned * block, width)
        at = pl.ds(m * owned, owned)
        total = jnp.dot(slot_g[0, at].reshape(rows), weights[0], preferred_element_type=F32)
        for r in range(1, rels):
            total += jnp.dot(slot_g[r, at].reshape(rows), weights[r], preferred_element_type=F32)
        slot_sums[m] = total.astype(BF16).reshape(owned, block, width)

    each(0, nz, sum_slots)

    def ret_go(j):
        for p in range(1, peers):
            s = slot(p, j)
            remote(
                slot_sums.at[s // owned, s % owned],
                rx.at[j, back(p)],
                ret_send.at[0],
                ret_recv.at[j],
                row_dev(p),
            ).start()

    z_step(zc, half)
    xc(half)
    def ret_pair(d):
        if d > 0:
            ret_go(d)
            ret_go(nz - d)
        elif d == 0:
            ret_go(0)

    ret_go(half)
    ret_pair(half - 1)

    def rs_copy(j, way):
        to = j - 1 if way < 0 else (j + 1) % nz
        at = half if way > 0 and to == 0 else to
        src, dst = ffeat.at[pl.ds(j * owned, owned)], rb.at[at]
        if j == half:
            first = 0 if way < 0 else cut
            src, dst = ffeat.at[pl.ds(j * owned + first, cut)], rb.at[at, pl.ds(first, cut)]
        return remote(src, dst, rs_send.at[at], rs_recv.at[at], z_dev(way))

    def collect(j, o):
        s = slot(0, j)
        total = None
        for p in range(peers):
            weight = jnp.where(ids[p, 0, s] == o, 1.0, 0.0).astype(F32)
            term = (slot_sums[s // owned, s % owned] if p == 0 else rx[j, p]).astype(F32) * weight
            total = term if total is None else total + term
        return total

    def rx_arrived(j):
        landed(rx.at[j, others], ret_recv.at[j])

    def gather_sums(j, at):
        rx_arrived(j)

        def one(o):
            running[at * owned + o] = collect(j, o)

        each(0, owned, one)

    def pass_on(j, at):
        lo, hi = 0, 0
        if 0 < j < half:
            rs_copy(j + 1, -1).wait_recv()
            lo, hi = 0, (cut if j + 1 == half else owned)
        elif j > half:
            rs_copy(j - 1, 1).wait_recv()
            lo, hi = (cut if j - 1 == half else 0), owned

        def plain(o):
            ffeat[j * owned + o] = running[at * owned + o].astype(BF16)

        def more(o):
            ffeat[j * owned + o] = (running[at * owned + o] + rb[j, o].astype(F32)).astype(BF16)

        if lo > 0:
            each(0, lo, plain)
        if hi > lo:
            each(lo, hi, more)
        if hi < owned:
            each(hi, owned, plain)
        if j <= half:
            rs_copy(j, -1).start()
        if j >= half:
            rs_copy(j, 1).start()

    x_arrived(1, fcot)

    def relation_grad(r):
        grad_acc[...] = jnp.zeros_like(grad_acc)

        def add(m):
            at = pl.ds(m * owned, owned)
            rows = (owned * block, width)
            grad_acc[...] += lax.dot_general(
                slot_g[r, at].reshape(rows),
                fcot[at].reshape(rows),
                (((0,), (0,)), ((), ())),
                preferred_element_type=F32,
            )

        each(0, nz, add)
        rows = grad_parts.shape[3]
        for h in range(CORES):
            for m in range(nn):
                grad_parts[m, r, h] = grad_acc[pl.ds((h * nn + m) * rows, rows), :]

    relation_grad(0)
    gather_sums(half, 0)
    pass_on(half, 0)
    ret_pair(half - 2)
    for r in range(1, rels):
        relation_grad(r)

    def y_copy(dn):
        return remote(
            grad_parts.at[(n + dn) % nn],
            grad_in.at[nn - dn],
            y_send.at[0],
            y_recv.at[0],
            y_dev(dn),
        )

    for dn in range(1, nn):
        y_copy(dn).start()

    def reduce_pair(d):
        gather_sums(d, 0)
        gather_sums(nz - d, 1)
        ret_pair(d - 2)
        pass_on(d, 0)
        pass_on(nz - d, 1)

    reduce_pair(half - 1)

    if nn > 1:
        landed(grad_in.at[pl.ds(1, nn - 1)], y_recv.at[0])
    rows = grad_parts.shape[3]
    for r in range(rels):
        for h in range(CORES):
            total = grad_parts[n, r, h]
            for dn in range(1, nn):
                total = total + grad_in[dn, r, h]
            grad_sum[r, h] = total.reshape(nx, group, width)

    def row_copy(p):
        to = grad_sum.at[:, (c + p % CORES) % CORES, (x + p // CORES) % nx]
        return remote(to, row_in.at[back(p)], row_send.at[0], row_recv.at[0], row_dev(p))

    for p in range(1, peers):
        row_copy(p).start()
    row_in[0] = grad_sum[:, c, x]

    load_bases_q.wait()

    def coef_sums(b):
        for r in range(rels):
            total = None
            for h in range(CORES):
                term = (grad_sum[r, h].reshape(rows, width) * bases_q[b, h].astype(F32)).sum(
                    axis=0, keepdims=True
                )
                total = term if total is None else total + term
            line = total[:, :128]
            for k in range(1, width // 128):
                line = line + total[:, k * 128 : (k + 1) * 128]
            coef_part[pl.ds(r * nb + b, 1), :] = line

    each(0, nb, coef_sums)

    def cp_copy(dn):
        return remote(
            coef_part, coef_recv.at[nn - dn], cp_send.at[0], cp_recv.at[0], y_dev(dn)
        )

    for dn in range(1, nn):
        cp_copy(dn).start()

    if half > 2:
        reduce_pair(half - 2)

    landed(row_in.at[others], row_recv.at[0])

    def basis_sums(b):
        total = jnp.zeros((group, width), F32)
        for p in range(peers):
            for r in range(rels):
                total = total + coefs[p, r, b] * row_in[p, r]
        basis_part[b % nz, b // nz] = total

    each(0, nb, basis_sums)

    def zb_copy(dz):
        return remote(
            basis_part.at[zs[nz - dz]],
            basis_in.at[nz - dz],
            zb_send.at[0],
            zb_recv.at[0],
            z_dev(dz),
        )

    for dz in range(1, nz):
        zb_copy(dz).start()

    for d in range(half - 3, 0, -1):
        reduce_pair(d)

    landed(basis_in.at[pl.ds(1, nz - 1)], zb_recv.at[0])
    total = basis_part[z]
    for dz in range(1, nz):
        total = total + basis_in[dz]
    basis_sum[...] = total

    def xb_copy(dx):
        return remote(
            basis_sum.at[(x + dx) % nx],
            basis_rows.at[x],
            xb_send.at[0],
            xb_recv.at[0],
            row_dev(dx * CORES),
        )

    for dx in range(1, nx):
        xb_copy(dx).start()
    basis_rows[x] = basis_sum[x]

    if nn > 1:
        landed(coef_recv.at[pl.ds(1, nn - 1)], cp_recv.at[0])
    total = coef_part[...]
    for dn in range(1, nn):
        total = total + coef_recv[dn]
    column = total.sum(axis=1, keepdims=True)
    wide_shape = (rels * nb, rels * nb)
    diagonal = lax.broadcasted_iota(jnp.int32, wide_shape, 0) == lax.broadcasted_iota(
        jnp.int32, wide_shape, 1
    )
    line = jnp.where(diagonal, jnp.broadcast_to(column, wide_shape), 0.0).sum(axis=0, keepdims=True)
    for r in range(rels):
        out_coef[r : r + 1, :] = line[:, r * nb : (r + 1) * nb]

    gather_sums(0, 0)
    rs_copy(1, -1).wait_recv()
    rs_copy(nz - 1, 1).wait_recv()

    def finish(o):
        arrived = rb[0, o].astype(F32) + rb[half, o].astype(F32)
        out[o] = (self_term[o] + running[o] + arrived).astype(BF16)

    each(0, owned, finish)

    landed(basis_rows.at[pl.ds(0, nx - 1)], xb_recv.at[0])
    out_basis[...] = basis_rows[...]

    z_done(zc)
    sent(stage.at[0, others], x_send.at[0, 0])
    for j in range(nz):
        sent(stage.at[0, others], x_send.at[1, j])
    sent(rx.at[pl.ds(0, nz), others], ret_send.at[0])
    for j in range(1, half + 1):
        rs_copy(j, -1).wait_send()
        rs_copy(nz - j, 1).wait_send()
    sent(ids_v.at[others], id_send.at[0])
    sent(coef_v.at[others], coef_send.at[0])
    sent(row_in.at[others], row_send.at[0])
    if nn > 1:
        sent(grad_in.at[pl.ds(1, nn - 1)], y_send.at[0])
        sent(coef_recv.at[pl.ds(1, nn - 1)], cp_send.at[0])
    sent(basis_in.at[pl.ds(1, nz - 1)], zb_send.at[0])
    sent(basis_sum.at[pl.ds(0, nx - 1)], xb_send.at[0])


def keep_kernel(a, b, c, a_out, b_out, c_out):
    a_out[...] = a[...]
    b_out[...] = b[...]
    c_out[...] = c[...]


def per_device(
    nx, nz, nn, features, cotangent, self_weight, bases, basis_coef, block_values, block_slots, fetch_ids
):
    rels, blocks, block, _ = block_values.shape
    width = features.shape[1]
    slots = fetch_ids.shape[0]
    owned = features.shape[0] // block
    nb = bases.shape[0]
    peers = nx * CORES
    rows = width // (CORES * nn)
    group = rows // nx

    vmem = pl.BlockSpec(memory_space=pltpu.VMEM)
    anywhere = pl.BlockSpec(memory_space=pl.ANY)
    dma = pltpu.SemaphoreType.DMA
    output, basis_grad, coef_grad = pl.pallas_call(
        functools.partial(layer_kernel, nx, nz, nn),
        out_shape=(
            jax.ShapeDtypeStruct((owned, block, width), BF16),
            jax.ShapeDtypeStruct((nx, group, width), F32),
            jax.ShapeDtypeStruct((rels, nb), F32),
        ),
        in_specs=[vmem, vmem, vmem, vmem, vmem, vmem, anywhere, anywhere, anywhere],
        out_specs=(vmem, vmem, vmem),
        scratch_shapes=[
            pltpu.VMEM((3 * rels, 1, 128), jnp.int32),
            pltpu.VMEM((peers, 1, 128), jnp.int32),
            pltpu.VMEM((peers, rels, 128), F32),
            pltpu.SMEM((3 * rels, 1, 128), jnp.int32),
            pltpu.SMEM((peers, 1, 128), jnp.int32),
            pltpu.SMEM((peers, rels, 128), F32),
            pltpu.VMEM((nz, owned, block, width), BF16),
            pltpu.VMEM((nz, owned, block, width), BF16),
            pltpu.VMEM((owned, block, width), BF16),
            pltpu.VMEM((nz + 1, peers, block, width), BF16),
            pltpu.VMEM((slots, block, width), BF16),
            pltpu.VMEM((slots, block, width), BF16),
            pltpu.VMEM((rels, blocks, block, block), BF16),
            pltpu.VMEM((blocks, block, width), F32),
            pltpu.VMEM((rels, slots, block, width), BF16),
            pltpu.VMEM((rels, width, width), BF16),
            pltpu.VMEM((owned, block, width), F32),
            pltpu.VMEM((nz, peers, block, width), BF16),
            pltpu.VMEM((nz, owned, block, width), BF16),
            pltpu.VMEM((width, width), F32),
            pltpu.VMEM((nn, rels, CORES, rows, width), F32),
            pltpu.VMEM((nn, rels, CORES, rows, width), F32),
            pltpu.VMEM((rels, CORES, nx, group, width), F32),
            pltpu.VMEM((nb, CORES, rows, width), BF16),
            pltpu.VMEM((rels * nb, 128), F32),
            pltpu.VMEM((nn, rels * nb, 128), F32),
            pltpu.VMEM((peers, rels, group, width), F32),
            pltpu.VMEM((nz, nx, group, width), F32),
            pltpu.VMEM((nz, nx, group, width), F32),
            pltpu.VMEM((nx, group, width), F32),
            pltpu.VMEM((nx, group, width), F32),
            dma((6,)),
            dma((1,)),
            dma((1,)),
            dma((1,)),
            dma((1,)),
            dma((2, nz)),
            dma((2, nz)),
            dma((2, nz)),
            dma((2,)),
            dma((1,)),
            dma((nz,)),
            dma((nz,)),
            dma((nz,)),
        ]
        + [dma((1,))] * 10,
        compiler_params=pltpu.CompilerParams(
            collective_id=0, has_side_effects=True, vmem_limit_bytes=62 * 1024 * 1024
        ),
    )(
        block_slots.transpose(0, 2, 1),
        fetch_ids.reshape(1, slots),
        basis_coef,
        features.reshape(owned, block, width),
        cotangent.reshape(owned, block, width),
        self_weight,
        bases.reshape(nb * width // block, block, width),
        bases.reshape(nb, CORES, nn, rows, width),
        block_values,
    )
    output, basis_grad, coef_grad = pl.pallas_call(
        keep_kernel,
        out_shape=tuple(jax.ShapeDtypeStruct(a.shape, a.dtype) for a in (output, basis_grad, coef_grad)),
        in_specs=[vmem] * 3,
        out_specs=(vmem,) * 3,
    )(output, basis_grad, coef_grad)
    return (
        output.reshape(owned * block, width),
        basis_grad.reshape(rows, width),
        coef_grad,
    )


def solution(mesh, nx=4):
    nz = mesh.shape["wide"] // (CORES * nx)
    return jax.shard_map(
        functools.partial(per_device, nx, nz, mesh.shape["narrow"]),
        mesh=mesh,
        in_specs=(
            P(("wide", "narrow"), None),
            P(("wide", "narrow"), None),
            P(),
            P(),
            P("wide", None),
            P("wide", "narrow", None, None),
            P("wide", "narrow", None),
            P(("wide", "narrow")),
        ),
        out_specs=(P(("wide", "narrow"), None), P(("wide", "narrow"), None), P("wide", None)),
        check_vma=False,
    )
```
